512 devices in a mesh: ctx: 128 (over y, z, core), ch: 4 (over x).
Axes of the slice: x: 4, y: 4, z: 16, core: 2. Of those that a mesh axis runs over, the one named last changes fastest.
Arguments:
- projections: bfloat16 [3, 32768, 1024], P(None, 'ctx', 'ch'), may hold values from -6 to 6
- filtered: bfloat16 [32768, 1024], P('ctx', 'ch'), may hold values from -6 to 6
- cotangent: bfloat16 [32768, 1024], P('ctx', 'ch'), may hold values from -9 to 9
- short_taps: float32 [3, 3, 1024], P(None, None, 'ch'), may hold values from -3.5 to 3.5
- residues: float32 [1024, 16], P('ch'), may hold values from -1.5 to 1.5
- pole_rates: float32 [1024, 16], P('ch'), may hold values from 0.5 to 1092.2667
- skip_gain: float32 [1024], P('ch'), may hold values from -4 to 4
Outputs:
- grad_projections: bfloat16 [3, 32768, 1024], P(None, 'ctx', 'ch')
- grad_short: float32 [3, 3, 1024], P(None, None, 'ch')
- grad_residues: float32 [1024, 16], P('ch')
- grad_rates: float32 [1024, 16], P('ch')
- grad_skip: float32 [1024], P('ch')
The draws below stay inside these ranges and needn't reach their ends.
All inputs are finite; a program needn't handle non-finite values.
Results may differ from the reference program's by a relative error of at most 0.013.
Values may be sent and summed in bfloat16 or wider, within the bound.
A program may use at most 64 MiB of HBM per device.

```python
import math
import jax
import jax.numpy as jnp
from jax import lax

C = 1024
MODES = 16
TAPS = 3
TOKENS = 32768


def draw_cotangent(key, part):
    key = jax.random.fold_in(key, 11)
    noise_key = jax.random.fold_in(key, 0)
    placed = jnp.arange(TOKENS, dtype=jnp.float32)[:, None] / TOKENS
    values = jnp.clip(jax.random.normal(noise_key, (TOKENS, C), jnp.float32), -4.0, 4.0)
    return (values * (0.5 + placed)).astype(jnp.bfloat16)


def steps_of(rng, extent, cuts, smallest, high):
    loudness = 1.0
    for dim, shards_of in cuts:
        draws = jax.random.uniform(jax.random.fold_in(jax.random.fold_in(rng, 6), dim), (shards_of,), jnp.float32, smallest / len(cuts), high / len(cuts))
        loudness = loudness * jnp.repeat(jnp.exp(draws), extent[dim] // shards_of).reshape((-1,) + (1,) * (len(extent) - 1 - dim))
    return loudness


def scatter_about(stream_key, shape, deviation, limit, pieces=(), kind=jnp.bfloat16):
    drawn = deviation * jax.random.normal(stream_key, shape, jnp.float32)
    if pieces:
        drawn = drawn * steps_of(stream_key, shape, pieces, -0.22, 0.18)
    return jnp.clip(drawn, -limit, limit).astype(kind)


def setup_inputs(seed: int = 0) -> dict:
    keys = jax.random.split(jax.random.key(seed), 8)
    projections = scatter_about(keys[0], (3, TOKENS, C), 1.0, 6.0, ((1, 128), (2, 4)))
    filtered = scatter_about(keys[1], (TOKENS, C), 1.0, 6.0, ((0, 128), (1, 4)))
    cotangent = draw_cotangent(jax.random.fold_in(keys[7], 71), 0)
    short_taps = scatter_about(keys[3], (3, TAPS, C), TAPS ** -0.5, 3.5, ((2, 4),), jnp.float32)
    residues = scatter_about(keys[4], (C, MODES), MODES ** -0.5, 1.5, ((0, 4),), jnp.float32)
    pole_rates = jnp.clip(jnp.exp(math.log(1092.2667) - 7.6891576 * jax.random.uniform(keys[5], (C, MODES), jnp.float32) ** steps_of(keys[5], (C, MODES), ((0, 4),), -0.2, 0.2)), 0.5, 1092.2667)
    skip_gain = scatter_about(keys[6], (C,), 1.0, 4.0, ((0, 4),), jnp.float32)
    return {"projections": projections, "filtered": filtered, "cotangent": cotangent, "short_taps": short_taps, "residues": residues, "pole_rates": pole_rates, "skip_gain": skip_gain}


def long_block(block_items):
    grad_filtered, gated_value, residue, rate_value = block_items
    spectrum_size = 2 * TOKENS
    position = jnp.arange(TOKENS, dtype=jnp.float32)[:, None, None]
    per_token = rate_value / TOKENS
    root_decay = jnp.sqrt(per_token)
    falloff = jnp.exp(-position * per_token)
    impulse = lax.optimization_barrier(jnp.sum(residue * root_decay * falloff, axis=2))
    filter_spec = jnp.fft.rfft(impulse, n=spectrum_size, axis=0)
    grad_spec = jnp.fft.rfft(grad_filtered, n=spectrum_size, axis=0)
    gated_spec = jnp.fft.rfft(gated_value, n=spectrum_size, axis=0)
    long_part = jnp.fft.irfft(jnp.conj(filter_spec) * grad_spec, n=spectrum_size, axis=0)[:TOKENS]
    lag_grad = jnp.fft.irfft(grad_spec * jnp.conj(gated_spec), n=spectrum_size, axis=0)[:TOKENS]
    residue_grad = root_decay * jnp.einsum('tc,tcm->cm', lag_grad, falloff, precision=lax.Precision.HIGHEST)
    weighted = falloff * (0.5 / rate_value - position / TOKENS)
    rate_grad = residue * root_decay * jnp.einsum('tc,tcm->cm', lag_grad, weighted, precision=lax.Precision.HIGHEST)
    return (long_part, residue_grad, rate_grad)

def reference(projections, filtered, cotangent, short_taps, residues, pole_rates, skip_gain):
    inputs = projections.astype(jnp.float32)
    padded = jnp.pad(inputs, ((0, 0), (TAPS - 1, 0), (0, 0)))
    features = jnp.zeros_like(inputs)
    for tap_index in range(TAPS):
        lead_rows = TAPS - 1 - tap_index
        features = features + short_taps[:, tap_index, None, :] * padded[:, lead_rows:lead_rows + TOKENS, :]
    query_feat = features[0]
    key_feat = features[1]
    value_feat = features[2]
    upstream = cotangent.astype(jnp.float32)
    grad_filtered = upstream * query_feat
    grad_query = upstream * filtered.astype(jnp.float32)
    gated_value = key_feat * value_feat
    block_width = 16
    block_count = C // block_width

    def by_blocks(values):
        return values.reshape(TOKENS, block_count, block_width).transpose(1, 0, 2)
    long_parts, residue_grad, rate_grad = lax.map(long_block, (by_blocks(grad_filtered), by_blocks(gated_value), residues.reshape(block_count, block_width, MODES), pole_rates.reshape(block_count, block_width, MODES)))
    long_part = long_parts.transpose(1, 0, 2).reshape(TOKENS, C)
    grad_gated = long_part + skip_gain * grad_filtered
    grad_stack = jnp.stack([grad_query, grad_gated * value_feat, grad_gated * key_feat])
    grads_padded = jnp.pad(grad_stack, ((0, 0), (0, TAPS - 1), (0, 0)))
    grad_proj = jnp.zeros_like(grad_stack)
    tap_terms = []
    for tap_index in range(TAPS):
        grad_proj = grad_proj + short_taps[:, tap_index, None, :] * grads_padded[:, tap_index:tap_index + TOKENS, :]
        lead_rows = TAPS - 1 - tap_index
        tap_terms.append(lax.optimization_barrier(jnp.sum(grad_stack * padded[:, lead_rows:lead_rows + TOKENS, :], axis=1)))
    token_scale = TOKENS ** (-0.5)
    return (grad_proj.astype(jnp.bfloat16), jnp.stack(tap_terms, axis=1) * token_scale, residue_grad.reshape(C, MODES) * token_scale, rate_grad.reshape(C, MODES) * token_scale, lax.optimization_barrier(jnp.sum(grad_filtered * gated_value, axis=0)) * token_scale)
```

```python
import functools
import math

import jax
import jax.numpy as jnp
from jax import lax
from jax.experimental import pallas as pl
from jax.experimental.pallas import tpu as pltpu
from jax.sharding import PartitionSpec as P

MESH = pl.DeviceIdType.MESH
F32 = jnp.float32
BF16 = jnp.bfloat16

RUNS = 8
MODES = 16
ROWS = 16
ROW_L, ROW_LP, ROW_V, ROW_VP, ROW_W, ROW_R, ROW_D, ROW_X = 0, 1, 2, 3, 4, 10, 11, 12
REST = 3


def up(x, by, size):
    return pltpu.roll(x, size - by, axis=0)


def suffix(state, slope, lam, length, count):
    row = lax.broadcasted_iota(jnp.int32, state.shape, 0)
    by = 1
    while by < count:
        decay = jnp.where(row < count - by, jnp.exp(lam * float(-length * by)), 0.0)
        later, later_slope = up(state, by, count), up(slope, by, count)
        slope = slope + decay * (later_slope + float(length * by) * later)
        state = state + decay * later
        by *= 2
    inside = row < count - 1
    return (
        state,
        slope,
        jnp.where(inside, up(state, 1, count), 0.0),
        jnp.where(inside, up(slope, 1, count), 0.0),
    )


def total(x):
    return jnp.sum(x, axis=0, keepdims=True)


def rest(x):
    return x - x.astype(BF16).astype(F32)


def kernel(
    geometry,
    proj_ref,
    filt_ref,
    cot_ref,
    taps_ref,
    res_ref,
    rate_ref,
    skip_ref,
    gp_ref,
    gshort_ref,
    gres_ref,
    grate_ref,
    gskip_ref,
    ext,
    feat,
    gf,
    gv,
    gq,
    ys,
    longs,
    lams,
    coefs,
    owner_lam,
    owner_coef,
    sloc,
    crosses,
    sums,
    sbuf,
    rbuf,
    flat,
    bbuf,
    bb,
    flat2,
    si_ref,
    cbuf,
    cr,
    gs,
    halo_out_prev,
    halo_out_next,
    halo_prev,
    halo_next,
    halo_send,
    halo_recv,
    a_send,
    a_recv,
    b_send,
    b_recv,
    c_send,
    c_recv,
):
    n_ctx, n_blocks = geometry
    rows = proj_ref.shape[1]
    width = proj_ref.shape[2]
    half = width // 2
    run = rows // RUNS
    tokens = rows * n_ctx
    per_block = 8
    group = 32
    me = lax.axis_index("ctx")
    y = me // (per_block * n_blocks)
    zh = (me // per_block) % n_blocks
    lo = me % per_block
    pos = y * per_block + lo

    def member(p):
        return (p // per_block) * (per_block * n_blocks) + zh * per_block + p % per_block

    def cousin(b):
        return y * (per_block * n_blocks) + b * per_block + lo

    before, after = (me + n_ctx - 1) % n_ctx, (me + 1) % n_ctx
    barrier = pltpu.get_barrier_semaphore()
    for j in range(1, group):
        pl.semaphore_signal(barrier, inc=1, device_id={"ctx": member((pos + j) % group)}, device_id_type=MESH)
    for j in range(1, n_blocks):
        pl.semaphore_signal(barrier, inc=1, device_id={"ctx": cousin((zh + j) % n_blocks)}, device_id_type=MESH)
    for d in (before, after):
        pl.semaphore_signal(barrier, inc=1, device_id={"ctx": d}, device_id_type=MESH)

    for i in range(3):
        halo_out_next[2 * i : 2 * i + 2, :] = proj_ref[i, rows - 16 :, :].astype(F32)[14:16]
        halo_out_prev[2 * i : 2 * i + 2, :] = proj_ref[i, :16, :].astype(F32)[0:2]
    halo_out_next[6:8, :] = jnp.zeros((2, width), F32)
    halo_out_prev[6:8, :] = cot_ref[:16, :].astype(F32)[0:2]
    halo_out_prev[8:10, :] = filt_ref[:16, :].astype(F32)[0:2]
    halo_out_prev[10:16, :] = jnp.zeros((6, width), F32)

    lam_t = jnp.transpose(rate_ref[...]) * (1.0 / tokens)
    coef_t = jnp.transpose(res_ref[...]) * jnp.sqrt(lam_t)
    for m in range(MODES):
        lam_m = jnp.broadcast_to(lam_t[m : m + 1, :], (RUNS, width))
        coef_m = jnp.broadcast_to(coef_t[m : m + 1, :], (RUNS, width))
        lams[m] = lam_m
        coefs[m] = coef_m
        for h in range(2):
            owner_lam[2 * m + h] = lam_m[:, h * half : (h + 1) * half]
            owner_coef[2 * m + h] = coef_m[:, h * half : (h + 1) * half]

    row = lax.broadcasted_iota(jnp.int32, (rows, rows), 0)
    col = lax.broadcasted_iota(jnp.int32, (rows, rows), 1)
    spread = jnp.where(col == run * (row % RUNS) + row // RUNS, 1.0, 0.0).astype(BF16)

    def placed(x):
        return jnp.dot(spread, x, preferred_element_type=F32)

    for i in range(3):
        ext[i, 16:, :] = placed(proj_ref[i])
    cot = placed(cot_ref[...])
    gq[...] = cot * placed(filt_ref[...])

    pl.semaphore_wait(barrier, group - 1 + n_blocks - 1 + 2)
    to_next = pltpu.make_async_remote_copy(
        halo_out_next, halo_prev, halo_send.at[0], halo_recv.at[0], device_id={"ctx": after}, device_id_type=MESH
    )
    to_prev = pltpu.make_async_remote_copy(
        halo_out_prev, halo_next, halo_send.at[1], halo_recv.at[1], device_id={"ctx": before}, device_id_type=MESH
    )
    to_next.start()
    to_prev.start()
    to_next.wait_recv()

    first = lax.broadcasted_iota(jnp.int32, (RUNS, width), 0) == 0
    has_before = jnp.where(me > 0, 1.0, 0.0)
    for i in range(3):
        for back in (2, 1):
            tail = pltpu.roll(ext[i, 16 + RUNS * (run - back) : 16 + RUNS * (run - back + 1), :], 1, axis=0)
            rim = halo_prev[2 * i + 2 - back : 2 * i + 3 - back, :] * has_before
            ext[i, 16 - 8 * back : 24 - 8 * back, :] = jnp.where(first, rim, tail)

    def tap(i, j):
        return taps_ref[i, j : j + 1, :]

    def shifted(i, j):
        return ext[i, 16 - 8 * j : 16 - 8 * j + rows, :]

    for i in range(3):
        made = tap(i, 0) * shifted(i, 0) + tap(i, 1) * shifted(i, 1) + tap(i, 2) * shifted(i, 2)
        if i == 0:
            gf[...] = cot * made
        else:
            feat[i - 1] = made
    gv[...] = feat[0] * feat[1]
    for j in range(3):
        ys[j] = feat[1] * shifted(1, j)
        ys[3 + j] = feat[0] * shifted(2, j)
    longs[...] = jnp.zeros_like(longs)
    crosses[...] = jnp.zeros_like(crosses)

    rank = lax.broadcasted_iota(jnp.int32, (RUNS, width), 0).astype(F32)

    def one_mode(m, _):
        lam = lams[m]
        coef = coefs[m]
        a = jnp.exp(-lam)
        zero = jnp.zeros((RUNS, width), F32)
        state, slope, r_sum, d_sum, v, vp = zero, zero, zero, zero, zero, zero
        w = [zero] * 6
        for step in range(run):
            low = slice(RUNS * (run - 1 - step), RUNS * (run - step))
            high = slice(RUNS * step, RUNS * (step + 1))
            slope = a * (slope + state)
            state = a * state + gf[low, :]
            longs[low, :] += coef * state
            gv_low = gv[low, :]
            r_sum = r_sum + gv_low * state
            d_sum = d_sum + gv_low * slope
            v = a * (v + gv[high, :])
            vp = a * vp + v
            for k in range(6):
                w[k] = a * (w[k] + ys[k, high, :])
        inner, inner_slope, s_loc, sp_loc = suffix(state, slope, lam, run, RUNS)
        sloc[m] = s_loc
        weight = jnp.exp(lam * (float(run) * (rank - float(RUNS - 1))))
        sums[m, ROW_L : ROW_L + 1, :] = inner[0:1, :]
        sums[m, ROW_LP : ROW_LP + 1, :] = inner_slope[0:1, :]
        sums[m, ROW_V : ROW_V + 1, :] = total(weight * v)
        sums[m, ROW_VP : ROW_VP + 1, :] = total(weight * (vp + float(run) * (float(RUNS - 1) - rank) * v))
        state_in = coef * s_loc
        for k in range(6):
            sums[m, ROW_W + k : ROW_W + k + 1, :] = total(weight * w[k])
            crosses[k] += state_in * w[k]
        pair = (total(r_sum + v * s_loc), total(d_sum + vp * s_loc + v * sp_loc))
        for at, value in zip((ROW_R, ROW_D, ROW_X), pair + (jnp.zeros((1, width), F32),)):
            sums[m, at : at + 1, :] = value
            sums[m, at + REST : at + REST + 1, :] = rest(value)
        return 0

    lax.fori_loop(0, MODES, one_mode, 0)

    skip = skip_ref[...]
    inner_gated = longs[...] + skip * gf[...]
    plain = [total(gq[...] * shifted(0, j)) for j in range(3)]
    plain += [total(inner_gated * ys[k]) + total(crosses[k]) for k in range(6)]
    plain.append(total(gf[...] * gv[...]))
    for m, value in enumerate(plain):
        sums[m, ROW_X : ROW_X + 1, :] = value
        sums[m, ROW_X + REST : ROW_X + REST + 1, :] = rest(value)
    for m in range(MODES):
        for h in range(2):
            sbuf[2 * m + h] = sums[m, :, h * half : (h + 1) * half].astype(BF16)

    own_a = pltpu.make_async_copy(sbuf.at[pos], rbuf.at[pos], a_recv)
    own_a.start()
    for j in range(1, group):
        p = (pos + j) % group
        pltpu.make_async_remote_copy(
            sbuf.at[p], rbuf.at[pos], a_send, a_recv, device_id={"ctx": member(p)}, device_id_type=MESH
        ).start()
    pltpu.make_async_copy(rbuf, rbuf, a_recv).wait()

    lam_o = owner_lam[pos]
    coef_o = owner_coef[pos]
    flat[...] = rbuf[...].astype(F32).reshape(group * ROWS, half)
    rank8 = lax.broadcasted_iota(jnp.int32, (per_block, half), 0).astype(F32)
    weight = jnp.exp(lam_o * (float(rows) * (rank8 - float(per_block - 1))))
    inside = []
    acc_r = acc_d = acc_x = jnp.zeros((per_block, half), F32)
    acc_w = [acc_r] * 6
    for b in range(4):
        base = b * per_block * ROWS

        def item(k):
            return flat[pl.ds(base + k, per_block, stride=ROWS), :]

        state, slope, v, vp = item(ROW_L), item(ROW_LP), item(ROW_V), item(ROW_VP)
        inner, inner_slope, s_int, sp_int = suffix(state, slope, lam_o, rows, per_block)
        inside.append(s_int)
        parts = [
            inner[0:1, :],
            inner_slope[0:1, :],
            total(weight * v),
            total(weight * (vp + float(rows) * (float(per_block - 1) - rank8) * v)),
        ]
        acc_r = acc_r + (item(ROW_R) + item(ROW_R + REST)) + v * s_int
        acc_d = acc_d + (item(ROW_D) + item(ROW_D + REST)) + vp * s_int + v * sp_int
        acc_x = acc_x + (item(ROW_X) + item(ROW_X + REST))
        for k in range(6):
            w_k = item(ROW_W + k)
            parts.append(total(weight * w_k))
            acc_w[k] = acc_w[k] + w_k * s_int
        for k, part in enumerate(parts):
            flat2[b * ROWS + k : b * ROWS + k + 1, :] = part
        flat2[b * ROWS + 10 : b * ROWS + ROWS, :] = jnp.zeros((ROWS - 10, half), F32)
    for k in range(6):
        value = total(acc_w[k])
        flat2[10 + k : 11 + k, :] = value
        flat2[2 * ROWS + 10 + k : 2 * ROWS + 11 + k, :] = rest(value)
    for k, acc in enumerate((acc_r, acc_d, acc_x)):
        value = total(acc)
        flat2[ROWS + 10 + k : ROWS + 11 + k, :] = value
        flat2[ROWS + 10 + REST + k : ROWS + 11 + REST + k, :] = rest(value)
    bbuf[...] = flat2[: 4 * ROWS, :].astype(BF16).reshape(4, ROWS, half)

    own_b = pltpu.make_async_copy(bbuf, bb.at[:, zh], b_recv)
    own_b.start()
    for j in range(1, n_blocks):
        pltpu.make_async_remote_copy(
            bbuf, bb.at[:, zh], b_send, b_recv, device_id={"ctx": cousin((zh + j) % n_blocks)}, device_id_type=MESH
        ).start()
    pltpu.make_async_copy(bb, bb, b_recv).wait()

    n_int = 4 * n_blocks
    flat2[...] = bb[...].astype(F32).reshape(n_int * ROWS, half)

    def item2(k):
        return flat2[pl.ds(k, n_int, stride=ROWS), :]

    lam2 = jnp.concatenate([lam_o, lam_o], axis=0)
    v, vp = item2(ROW_V), item2(ROW_VP)
    _, _, s_all, sp_all = suffix(item2(ROW_L), item2(ROW_LP), lam2, rows * per_block, n_int)
    si_ref[...] = s_all
    parts = [total(v * s_all), total(vp * s_all + v * sp_all)]
    interval = lax.broadcasted_iota(jnp.int32, (n_int, half), 0) // n_blocks
    in_1, in_0_2 = interval == 1, (interval == 0) | (interval == 2)

    def sum_1(k):
        return total(jnp.where(in_1, item2(10 + k) + item2(10 + REST + k), 0.0))

    for k in range(2):
        parts[k] = parts[k] + sum_1(k)
    for k in range(6):
        parts.append(coef_o[0:1, :] * total(item2(ROW_W + k) * s_all + jnp.where(in_0_2, item2(10 + k), 0.0)))
    parts.append(sum_1(2))
    parts += [rest(parts[0]), rest(parts[1]), rest(parts[8])]
    row16 = lax.broadcasted_iota(jnp.int32, (ROWS, half), 0)
    common = jnp.zeros((ROWS, half), F32)
    for k, part in enumerate(parts):
        common = jnp.where(row16 == 1 + k, part, common)
    for b in range(4):
        s_dev = inside[b] + weight * si_ref[pl.ds(b * n_blocks + zh, 1), :]
        s_rest = rest(s_dev)
        for i in range(per_block):
            own = jnp.where(row16 == 0, s_dev[i : i + 1, :], common)
            cbuf[b * per_block + i] = jnp.where(row16 == 13, s_rest[i : i + 1, :], own).astype(BF16)

    own_c = pltpu.make_async_copy(cbuf.at[pos], cr.at[pos], c_recv)
    own_c.start()
    for j in range(1, group):
        p = (pos + j) % group
        pltpu.make_async_remote_copy(
            cbuf.at[p], cr.at[pos], c_send, c_recv, device_id={"ctx": member(p)}, device_id_type=MESH
        ).start()

    to_prev.wait_recv()
    has_after = jnp.where(me < n_ctx - 1, 1.0, 0.0)
    ahead = halo_next[...] * has_after

    def ahead_feat(i, k):
        mine = [ext[i, 16 + RUNS * (run - 1 - b) + RUNS - 1 : 16 + RUNS * (run - b), :] for b in range(2)]
        if k == 0:
            return tap(i, 0) * ahead[2 * i : 2 * i + 1] + tap(i, 1) * mine[0] + tap(i, 2) * mine[1]
        return tap(i, 0) * ahead[2 * i + 1 : 2 * i + 2] + tap(i, 1) * ahead[2 * i : 2 * i + 1] + tap(i, 2) * mine[0]

    ahead_f = [[ahead_feat(i, k) for k in range(2)] for i in range(3)]
    ahead_gf = [ahead[6 + k : 7 + k] * ahead_f[0][k] for k in range(2)]
    ahead_gq = [ahead[6 + k : 7 + k] * ahead[8 + k : 9 + k] for k in range(2)]

    pltpu.make_async_copy(cr, cr, c_recv).wait()
    flat[...] = cr[...].astype(F32).reshape(group * ROWS, half)

    def item3(k):
        return jnp.concatenate(
            [flat[pl.ds(h * ROWS + k, MODES, stride=2 * ROWS), :] for h in range(2)], axis=1
        )

    scale = 1.0 / math.sqrt(tokens)
    s_dev = item3(0) + item3(13)
    r_tot, d_tot, x_tot = item3(1) + item3(10), item3(2) + item3(11), item3(9) + item3(12)
    root = jnp.sqrt(lam_t)
    res_t = jnp.transpose(res_ref[...])
    rate_t = jnp.transpose(rate_ref[...])
    gres_ref[...] = jnp.transpose(scale * root * r_tot)
    grate_ref[...] = jnp.transpose(scale * res_t * root * (0.5 / rate_t * r_tot - d_tot * (1.0 / tokens)))
    for j in range(3):
        gshort_ref[0, j : j + 1, :] = scale * x_tot[j : j + 1, :]
        for i in (1, 2):
            k = 3 * (i - 1) + j
            gshort_ref[i, j : j + 1, :] = scale * (x_tot[3 + k : 4 + k, :] + total(item3(3 + k)))
    gskip_ref[...] = scale * x_tot[9:10, :]

    rank_h = lax.broadcasted_iota(jnp.int32, (RUNS, half), 0).astype(F32)
    for h in range(2):
        lanes = slice(h * half, (h + 1) * half)
        a, p = [], []
        for m in range(MODES):
            lam = lams[m, :, lanes]
            back = jnp.exp(lam * (float(run) * (rank_h - float(RUNS - 1))))
            a.append(jnp.exp(-lam))
            p.append(coefs[m, :, lanes] * (sloc[m, :, lanes] + back * s_dev[m : m + 1, lanes]))
        for r in range(run - 1, -1, -1):
            at = slice(RUNS * r, RUNS * (r + 1))
            p = [x * d for x, d in zip(p, a)]
            terms = p
            while len(terms) > 1:
                terms = [u + w for u, w in zip(terms[::2], terms[1::2])]
            longs[at, lanes] += terms[0]

    gated = longs[...] + skip * gf[...]
    gs[0, :rows, :] = gq[...]
    gs[1, :rows, :] = gated * feat[1]
    gs[2, :rows, :] = gated * feat[0]
    ahead_long = [
        total(coef_t * s_dev),
        total(coef_t * (s_dev - ahead_gf[0]) * jnp.exp(lam_t)),
    ]
    last = lax.broadcasted_iota(jnp.int32, (RUNS, width), 0) == RUNS - 1
    for k in range(2):
        ahead_gated = (ahead_long[k] + skip * ahead_gf[k]) * has_after
        beyond = (ahead_gq[k], ahead_gated * ahead_f[2][k], ahead_gated * ahead_f[1][k])
        for i in range(3):
            head = pltpu.roll(gs[i, RUNS * k : RUNS * (k + 1), :], RUNS - 1, axis=0)
            gs[i, rows + RUNS * k : rows + RUNS * (k + 1), :] = jnp.where(last, beyond[i], head)
    gather = jnp.where(col == RUNS * (row % run) + row // run, 1.0, 0.0).astype(BF16)
    for i in range(3):
        made = (
            tap(i, 0) * gs[i, :rows, :]
            + tap(i, 1) * gs[i, RUNS : rows + RUNS, :]
            + tap(i, 2) * gs[i, 2 * RUNS : rows + 2 * RUNS, :]
        )
        gp_ref[i] = jnp.dot(gather, made.astype(BF16), preferred_element_type=F32).astype(BF16)

    to_next.wait_send()
    to_prev.wait_send()
    others = pl.ds(0, group - 1)
    pltpu.make_async_copy(sbuf.at[others], sbuf.at[others], a_send).wait()
    pltpu.make_async_copy(bb.at[pl.ds(0, n_blocks - 1)], bb.at[pl.ds(0, n_blocks - 1)], b_send).wait()
    pltpu.make_async_copy(cbuf.at[others], cbuf.at[others], c_send).wait()


def solution(mesh):
    n_ctx = mesh.shape["ctx"]
    n_blocks = n_ctx // 32

    def body(projections, filtered, cotangent, short_taps, residues, pole_rates, skip_gain):
        rows, width = filtered.shape
        half = width // 2
        vmem = pl.BlockSpec(memory_space=pltpu.VMEM)
        full = (rows, width)
        out = pl.pallas_call(
            functools.partial(kernel, (n_ctx, n_blocks)),
            out_shape=(
                jax.ShapeDtypeStruct((3,) + full, BF16),
                jax.ShapeDtypeStruct((3, 3, width), F32),
                jax.ShapeDtypeStruct((width, MODES), F32),
                jax.ShapeDtypeStruct((width, MODES), F32),
                jax.ShapeDtypeStruct((1, width), F32),
            ),
            in_specs=[vmem] * 7,
            out_specs=[vmem] * 5,
            scratch_shapes=[
                pltpu.VMEM((3, rows + 16, width), F32),
                pltpu.VMEM((2,) + full, F32),
                pltpu.VMEM(full, F32),
                pltpu.VMEM(full, F32),
                pltpu.VMEM(full, F32),
                pltpu.VMEM((6,) + full, F32),
                pltpu.VMEM(full, F32),
                pltpu.VMEM((MODES, RUNS, width), F32),
                pltpu.VMEM((MODES, RUNS, width), F32),
                pltpu.VMEM((2 * MODES, RUNS, half), F32),
                pltpu.VMEM((2 * MODES, RUNS, half), F32),
                pltpu.VMEM((MODES, RUNS, width), F32),
                pltpu.VMEM((6, RUNS, width), F32),
                pltpu.VMEM((MODES, ROWS, width), F32),
                pltpu.VMEM((32, ROWS, half), BF16),
                pltpu.VMEM((32, ROWS, half), BF16),
                pltpu.VMEM((32 * ROWS, half), F32),
                pltpu.VMEM((4, ROWS, half), BF16),
                pltpu.VMEM((4, n_blocks, ROWS, half), BF16),
                pltpu.VMEM((4 * n_blocks * ROWS, half), F32),
                pltpu.VMEM((4 * n_blocks, half), F32),
                pltpu.VMEM((32, ROWS, half), BF16),
                pltpu.VMEM((32, ROWS, half), BF16),
                pltpu.VMEM((3, rows + 16, width), F32),
                pltpu.VMEM((16, width), F32),
                pltpu.VMEM((8, width), F32),
                pltpu.VMEM((8, width), F32),
                pltpu.VMEM((16, width), F32),
                pltpu.SemaphoreType.DMA((2,)),
                pltpu.SemaphoreType.DMA((2,)),
                pltpu.SemaphoreType.DMA,
                pltpu.SemaphoreType.DMA,
                pltpu.SemaphoreType.DMA,
                pltpu.SemaphoreType.DMA,
                pltpu.SemaphoreType.DMA,
                pltpu.SemaphoreType.DMA,
            ],
            compiler_params=pltpu.CompilerParams(
                collective_id=0, has_side_effects=True, vmem_limit_bytes=40 * 1024 * 1024
            ),
        )(projections, filtered, cotangent, short_taps, residues, pole_rates, skip_gain.reshape(1, width))
        return out[0], out[1], out[2], out[3], out[4].reshape(width)

    return jax.shard_map(
        body,
        mesh=mesh,
        in_specs=(
            P(None, "ctx", "ch"),
            P("ctx", "ch"),
            P("ctx", "ch"),
            P(None, None, "ch"),
            P("ch", None),
            P("ch", None),
            P("ch"),
        ),
        out_specs=(
            P(None, "ctx", "ch"),
            P(None, None, "ch"),
            P("ch", None),
            P("ch", None),
            P("ch"),
        ),
        check_vma=False,
    )
```

```python
import functools
import math

import jax
import jax.numpy as jnp
from jax import lax
from jax.experimental import pallas as pl
from jax.experimental.pallas import tpu as pltpu
from jax.sharding import PartitionSpec as P

MESH = pl.DeviceIdType.MESH
F32 = jnp.float32
BF16 = jnp.bfloat16

RUNS = 8
MODES = 16
ROWS = 16
ROW_L, ROW_LP, ROW_V, ROW_VP, ROW_W, ROW_R, ROW_D, ROW_X = 0, 1, 2, 3, 4, 10, 11, 12
REST = 3


def up(x, by, size):
    return pltpu.roll(x, size - by, axis=0)


def suffix(state, slope, lam, length, count):
    row = lax.broadcasted_iota(jnp.int32, state.shape, 0)
    by = 1
    while by < count:
        decay = jnp.where(row < count - by, jnp.exp(lam * float(-length * by)), 0.0)
        later, later_slope = up(state, by, count), up(slope, by, count)
        slope = slope + decay * (later_slope + float(length * by) * later)
        state = state + decay * later
        by *= 2
    inside = row < count - 1
    return (
        state,
        slope,
        jnp.where(inside, up(state, 1, count), 0.0),
        jnp.where(inside, up(slope, 1, count), 0.0),
    )


def total(x):
    return jnp.sum(x, axis=0, keepdims=True)


def rest(x):
    return x - x.astype(BF16).astype(F32)


def kernel(
    geometry,
    proj_hbm,
    filt_hbm,
    cot_hbm,
    taps_hbm,
    res_hbm,
    rate_hbm,
    skip_hbm,
    gp_ref,
    gshort_ref,
    gres_ref,
    grate_ref,
    gskip_ref,
    proj_ref,
    filt_ref,
    cot_ref,
    taps_ref,
    res_ref,
    rate_ref,
    skip_ref,
    ext,
    feat,
    gf,
    gv,
    gq,
    ys,
    longs,
    lams,
    coefs,
    owner_lam,
    owner_coef,
    sloc,
    crosses,
    sums,
    sbuf,
    rbuf,
    flat,
    bbuf,
    bb,
    flat2,
    si_ref,
    cbuf,
    cr,
    gs,
    halo_prev,
    halo_next,
    in_sem,
    halo_send,
    halo_recv,
    a_send,
    a_recv,
    b_send,
    b_recv,
    c_send,
    c_recv,
):
    n_ctx, n_blocks = geometry
    rows = proj_ref.shape[1]
    width = proj_ref.shape[2]
    half = width // 2
    run = rows // RUNS
    tokens = rows * n_ctx
    per_block = 8
    group = 32
    me = lax.axis_index("ctx")
    y = me // (per_block * n_blocks)
    zh = (me // per_block) % n_blocks
    lo = me % per_block
    pos = y * per_block + lo

    def member(p):
        return (p // per_block) * (per_block * n_blocks) + zh * per_block + p % per_block

    def cousin(b):
        return y * (per_block * n_blocks) + b * per_block + lo

    before, after = (me + n_ctx - 1) % n_ctx, (me + 1) % n_ctx
    barrier = pltpu.get_barrier_semaphore()
    for j in range(1, group):
        pl.semaphore_signal(barrier, inc=1, device_id={"ctx": member((pos + j) % group)}, device_id_type=MESH)
    for j in range(1, n_blocks):
        pl.semaphore_signal(barrier, inc=1, device_id={"ctx": cousin((zh + j) % n_blocks)}, device_id_type=MESH)
    for d in (before, after):
        pl.semaphore_signal(barrier, inc=1, device_id={"ctx": d}, device_id_type=MESH)

    held = (
        (taps_hbm, taps_ref),
        (res_hbm, res_ref),
        (rate_hbm, rate_ref),
        (skip_hbm, skip_ref),
        (proj_hbm, proj_ref),
        (cot_hbm, cot_ref),
        (filt_hbm, filt_ref),
    )
    loads = [pltpu.make_async_copy(src, dst, in_sem.at[i]) for i, (src, dst) in enumerate(held)]
    for load in loads:
        load.start()

    row = lax.broadcasted_iota(jnp.int32, (rows, rows), 0)
    col = lax.broadcasted_iota(jnp.int32, (rows, rows), 1)
    spread = jnp.where(col == run * (row % RUNS) + row // RUNS, 1.0, 0.0).astype(BF16)
    for load in loads[:4]:
        load.wait()

    lam_t = rate_ref[...] * (1.0 / tokens)
    coef_t = res_ref[...] * jnp.sqrt(lam_t)
    for m in range(MODES):
        lam_m = jnp.broadcast_to(lam_t[m : m + 1, :], (RUNS, width))
        coef_m = jnp.broadcast_to(coef_t[m : m + 1, :], (RUNS, width))
        lams[m] = lam_m
        coefs[m] = coef_m
        for h in range(2):
            owner_lam[2 * m + h] = lam_m[:, h * half : (h + 1) * half]
            owner_coef[2 * m + h] = coef_m[:, h * half : (h + 1) * half]

    def placed(x):
        return jnp.dot(spread, x, preferred_element_type=F32)

    first = lax.broadcasted_iota(jnp.int32, (RUNS, width), 0) == 0
    first_two = lax.broadcasted_iota(jnp.int32, (2 * RUNS, width), 0) % RUNS == 0
    for load in loads[4:]:
        load.wait()
    for i in range(3):
        ext[i, 16:, :] = placed(proj_ref[i])
        for back in (2, 1):
            tail = pltpu.roll(ext[i, 16 + RUNS * (run - back) : 16 + RUNS * (run - back + 1), :], 1, axis=0)
            ext[i, 16 - 8 * back : 24 - 8 * back, :] = jnp.where(first, 0.0, tail)

    def tap(i, j):
        return taps_ref[i, j : j + 1, :]

    def shifted(i, j):
        return ext[i, 16 - 8 * j : 16 - 8 * j + rows, :]

    def masked(x):
        return jnp.concatenate([jnp.where(first_two, 0.0, x[: 2 * RUNS]), x[2 * RUNS :]], axis=0)

    cot = placed(cot_ref[...])
    gq[...] = cot * placed(filt_ref[...])
    for i in range(3):
        made = tap(i, 0) * shifted(i, 0) + tap(i, 1) * shifted(i, 1) + tap(i, 2) * shifted(i, 2)
        if i == 0:
            gf[...] = masked(cot * made)
        else:
            feat[i - 1] = made
    gv[...] = masked(feat[0] * feat[1])
    for j in range(3):
        ys[j] = masked(feat[1] * shifted(1, j))
        ys[3 + j] = masked(feat[0] * shifted(2, j))

    pl.semaphore_wait(barrier, group - 1 + n_blocks - 1 + 2)
    last_rows, first_rows = pl.ds(rows - 16, 16), pl.ds(0, 16)
    rims = (
        (proj_ref.at[:, last_rows], halo_prev, after),
        (proj_ref.at[:, first_rows], halo_next.at[pl.ds(0, 3)], before),
        (cot_ref.at[first_rows], halo_next.at[3], before),
        (filt_ref.at[first_rows], halo_next.at[4], before),
    )
    rims = [
        pltpu.make_async_remote_copy(
            src, dst, halo_send.at[i], halo_recv.at[i], device_id={"ctx": to}, device_id_type=MESH
        )
        for i, (src, dst, to) in enumerate(rims)
    ]
    for rim in rims:
        rim.start()
    longs[...] = jnp.zeros_like(longs)
    crosses[...] = jnp.zeros_like(crosses)

    rank = lax.broadcasted_iota(jnp.int32, (RUNS, width), 0).astype(F32)

    def one_mode(m, _):
        lam = lams[m]
        coef = coefs[m]
        a = jnp.exp(-lam)
        zero = jnp.zeros((RUNS, width), F32)
        state, slope, r_sum, d_sum, v, vp = zero, zero, zero, zero, zero, zero
        w = [zero] * 6
        for step in range(run):
            low = slice(RUNS * (run - 1 - step), RUNS * (run - step))
            high = slice(RUNS * step, RUNS * (step + 1))
            slope = a * (slope + state)
            state = a * state + gf[low, :]
            longs[low, :] += coef * state
            gv_low = gv[low, :]
            r_sum = r_sum + gv_low * state
            d_sum = d_sum + gv_low * slope
            v = a * (v + gv[high, :])
            vp = a * vp + v
            for k in range(6):
                w[k] = a * (w[k] + ys[k, high, :])
        inner, inner_slope, s_loc, sp_loc = suffix(state, slope, lam, run, RUNS)
        sloc[m] = s_loc
        weight = jnp.exp(lam * (float(run) * (rank - float(RUNS - 1))))
        at = m * ROWS

        def put(k, value):
            for h in range(2):
                sums[pl.ds(h * MODES * ROWS + at + k, 1), :] = value[:, h * half : (h + 1) * half]

        put(ROW_L, inner[0:1, :])
        put(ROW_LP, inner_slope[0:1, :])
        put(ROW_V, total(weight * v))
        put(ROW_VP, total(weight * (vp + float(run) * (float(RUNS - 1) - rank) * v)))
        state_in = coef * s_loc
        for k in range(6):
            put(ROW_W + k, total(weight * w[k]))
            crosses[k] += state_in * w[k]
        put(ROW_R, total(r_sum + v * s_loc))
        put(ROW_D, total(d_sum + vp * s_loc + v * sp_loc))
        return 0

    lax.fori_loop(0, MODES, one_mode, 0)

    skip = skip_ref[...]
    inner_gated = longs[...] + skip * gf[...]
    own_query = masked(gq[...])
    plain = [total(own_query * shifted(0, j)) for j in range(3)]
    plain += [total(inner_gated * ys[k]) + total(crosses[k]) for k in range(6)]
    plain.append(total(gf[...] * gv[...]))

    rims[0].wait_recv()
    has_before = jnp.where(me > 0, 1.0, 0.0)
    before_rows = [halo_prev[i].astype(F32)[14:16] * has_before for i in range(3)]
    x = [
        {-2: before_rows[i][0:1], -1: before_rows[i][1:2], 0: ext[i, 16:17, :], 1: ext[i, 24:25, :]}
        for i in range(3)
    ]
    f = [[tap(i, 0) * x[i][t] + tap(i, 1) * x[i][t - 1] + tap(i, 2) * x[i][t - 2] for t in range(2)] for i in range(3)]
    cot_two = [cot[0:1], cot[RUNS : RUNS + 1]]
    gf_two = [cot_two[t] * f[0][t] for t in range(2)]
    gv_two = [f[1][t] * f[2][t] for t in range(2)]
    ys_two = [[f[2][t] * x[1][t - j] for j in range(3)] + [f[1][t] * x[2][t - j] for j in range(3)] for t in range(2)]

    def each_mode(k):
        return jnp.concatenate(
            [sums[pl.ds(h * MODES * ROWS + k, MODES, stride=ROWS), :] for h in range(2)], axis=1
        )

    def keep(k, value):
        for h in range(2):
            sums[pl.ds(h * MODES * ROWS + k, MODES, stride=ROWS), :] = value[:, h * half : (h + 1) * half]

    a_t = jnp.exp(-lam_t)
    back_two = jnp.exp(2.0 * lam_t)
    two, two_slope = each_mode(ROW_L), each_mode(ROW_LP)
    two, two_slope = back_two * two, back_two * (two_slope - 2.0 * two)
    slope_1 = a_t * (two_slope + two)
    state_1 = gf_two[1] + a_t * two
    slope_0 = a_t * (slope_1 + state_1)
    state_0 = gf_two[0] + a_t * state_1
    decays = [jnp.exp(lam_t * -float(rows)), jnp.exp(lam_t * -float(rows - 1))]
    parts = [decays[t] * gv_two[t] for t in range(2)]
    keep(ROW_L, state_0)
    keep(ROW_LP, slope_0)
    keep(ROW_V, each_mode(ROW_V) + parts[0] + parts[1])
    keep(ROW_VP, each_mode(ROW_VP) + float(rows) * parts[0] + float(rows - 1) * parts[1])
    for k in range(6):
        keep(ROW_W + k, each_mode(ROW_W + k) + decays[0] * ys_two[0][k] + decays[1] * ys_two[1][k])
    r_all = each_mode(ROW_R) + gv_two[1] * state_1 + gv_two[0] * state_0
    d_all = each_mode(ROW_D) + gv_two[1] * slope_1 + gv_two[0] * slope_0
    keep(ROW_R, r_all)
    keep(ROW_R + REST, rest(r_all))
    keep(ROW_D, d_all)
    keep(ROW_D + REST, rest(d_all))
    gated_two = [total(coef_t * state_0) + skip * gf_two[0], total(coef_t * state_1) + skip * gf_two[1]]
    for t in range(2):
        for j in range(3):
            plain[j] = plain[j] + gq[RUNS * t : RUNS * t + 1, :] * x[0][t - j]
        for k in range(6):
            plain[3 + k] = plain[3 + k] + gated_two[t] * ys_two[t][k]
        plain[9] = plain[9] + gf_two[t] * gv_two[t]
    plain = jnp.concatenate(plain + [jnp.zeros((MODES - len(plain), width), F32)], axis=0)
    keep(ROW_X, plain)
    keep(ROW_X + REST, rest(plain))
    for m in range(MODES):
        for h in range(2):
            at = (h * MODES + m) * ROWS
            sbuf[2 * m + h] = sums[at : at + ROWS, :].astype(BF16)

    own_a = pltpu.make_async_copy(sbuf.at[pos], rbuf.at[pos], a_recv)
    own_a.start()
    for j in range(1, group):
        p = (pos + j) % group
        pltpu.make_async_remote_copy(
            sbuf.at[p], rbuf.at[pos], a_send, a_recv, device_id={"ctx": member(p)}, device_id_type=MESH
        ).start()

    direct = [total(coef_t) * gf_two[0] + total(coef_t * a_t) * gf_two[1], total(coef_t) * gf_two[1]]
    for t in range(2):
        at = slice(RUNS * t, RUNS * t + 1)
        gf[at, :] = gf_two[t]
        longs[at, :] += direct[t]
        for i in (1, 2):
            feat[i - 1, at, :] = f[i][t]

    pltpu.make_async_copy(rbuf, rbuf, a_recv).wait()

    lam_o = owner_lam[pos]
    coef_o = owner_coef[pos]
    flat[...] = rbuf[...].astype(F32).reshape(group * ROWS, half)
    rank8 = lax.broadcasted_iota(jnp.int32, (per_block, half), 0).astype(F32)
    weight = jnp.exp(lam_o * (float(rows) * (rank8 - float(per_block - 1))))
    inside = []
    acc_r = acc_d = acc_x = jnp.zeros((per_block, half), F32)
    acc_w = [acc_r] * 6
    for b in range(4):
        base = b * per_block * ROWS

        def item(k):
            return flat[pl.ds(base + k, per_block, stride=ROWS), :]

        state, slope, v, vp = item(ROW_L), item(ROW_LP), item(ROW_V), item(ROW_VP)
        inner, inner_slope, s_int, sp_int = suffix(state, slope, lam_o, rows, per_block)
        inside.append(s_int)
        parts = [
            inner[0:1, :],
            inner_slope[0:1, :],
            total(weight * v),
            total(weight * (vp + float(rows) * (float(per_block - 1) - rank8) * v)),
        ]
        acc_r = acc_r + (item(ROW_R) + item(ROW_R + REST)) + v * s_int
        acc_d = acc_d + (item(ROW_D) + item(ROW_D + REST)) + vp * s_int + v * sp_int
        acc_x = acc_x + (item(ROW_X) + item(ROW_X + REST))
        for k in range(6):
            w_k = item(ROW_W + k)
            parts.append(total(weight * w_k))
            acc_w[k] = acc_w[k] + w_k * s_int
        for k, part in enumerate(parts):
            flat2[b * ROWS + k : b * ROWS + k + 1, :] = part
        flat2[b * ROWS + 10 : b * ROWS + ROWS, :] = jnp.zeros((ROWS - 10, half), F32)
    for k in range(6):
        value = total(acc_w[k])
        flat2[10 + k : 11 + k, :] = value
        flat2[2 * ROWS + 10 + k : 2 * ROWS + 11 + k, :] = rest(value)
    for k, acc in enumerate((acc_r, acc_d, acc_x)):
        value = total(acc)
        flat2[ROWS + 10 + k : ROWS + 11 + k, :] = value
        flat2[ROWS + 10 + REST + k : ROWS + 11 + REST + k, :] = rest(value)
    bbuf[...] = flat2[: 4 * ROWS, :].astype(BF16).reshape(4, ROWS, half)

    own_b = pltpu.make_async_copy(bbuf, bb.at[:, zh], b_recv)
    own_b.start()
    for j in range(1, n_blocks):
        pltpu.make_async_remote_copy(
            bbuf, bb.at[:, zh], b_send, b_recv, device_id={"ctx": cousin((zh + j) % n_blocks)}, device_id_type=MESH
        ).start()
    pltpu.make_async_copy(bb, bb, b_recv).wait()

    n_int = 4 * n_blocks
    flat2[...] = bb[...].astype(F32).reshape(n_int * ROWS, half)

    def item2(k):
        return flat2[pl.ds(k, n_int, stride=ROWS), :]

    lam2 = jnp.concatenate([lam_o, lam_o], axis=0)
    v, vp = item2(ROW_V), item2(ROW_VP)
    _, _, s_all, sp_all = suffix(item2(ROW_L), item2(ROW_LP), lam2, rows * per_block, n_int)
    si_ref[...] = s_all
    parts = [total(v * s_all), total(vp * s_all + v * sp_all)]
    interval = lax.broadcasted_iota(jnp.int32, (n_int, half), 0) // n_blocks
    in_1, in_0_2 = interval == 1, (interval == 0) | (interval == 2)

    def sum_1(k):
        return total(jnp.where(in_1, item2(10 + k) + item2(10 + REST + k), 0.0))

    for k in range(2):
        parts[k] = parts[k] + sum_1(k)
    for k in range(6):
        parts.append(coef_o[0:1, :] * total(item2(ROW_W + k) * s_all + jnp.where(in_0_2, item2(10 + k), 0.0)))
    parts.append(sum_1(2))
    parts += [rest(parts[0]), rest(parts[1]), rest(parts[8])]
    row16 = lax.broadcasted_iota(jnp.int32, (ROWS, half), 0)
    common = jnp.zeros((ROWS, half), F32)
    for k, part in enumerate(parts):
        common = jnp.where(row16 == 1 + k, part, common)
    for b in range(4):
        s_dev = inside[b] + weight * si_ref[pl.ds(b * n_blocks + zh, 1), :]
        s_rest = rest(s_dev)
        for i in range(per_block):
            own = jnp.where(row16 == 0, s_dev[i : i + 1, :], common)
            cbuf[b * per_block + i] = jnp.where(row16 == 13, s_rest[i : i + 1, :], own).astype(BF16)

    own_c = pltpu.make_async_copy(cbuf.at[pos], cr.at[pos], c_recv)
    own_c.start()
    for j in range(1, group):
        p = (pos + j) % group
        pltpu.make_async_remote_copy(
            cbuf.at[p], cr.at[pos], c_send, c_recv, device_id={"ctx": member(p)}, device_id_type=MESH
        ).start()

    for rim in rims[1:]:
        rim.wait_recv()
    has_after = jnp.where(me < n_ctx - 1, 1.0, 0.0)
    ahead = [halo_next[i].astype(F32) * has_after for i in range(5)]

    def ahead_feat(i, k):
        mine = [ext[i, 16 + RUNS * (run - 1 - b) + RUNS - 1 : 16 + RUNS * (run - b), :] for b in range(2)]
        if k == 0:
            return tap(i, 0) * ahead[i][0:1] + tap(i, 1) * mine[0] + tap(i, 2) * mine[1]
        return tap(i, 0) * ahead[i][1:2] + tap(i, 1) * ahead[i][0:1] + tap(i, 2) * mine[0]

    ahead_f = [[ahead_feat(i, k) for k in range(2)] for i in range(3)]
    ahead_gf = [ahead[3][k : k + 1] * ahead_f[0][k] for k in range(2)]
    ahead_gq = [ahead[3][k : k + 1] * ahead[4][k : k + 1] for k in range(2)]

    pltpu.make_async_copy(cr, cr, c_recv).wait()
    flat[...] = cr[...].astype(F32).reshape(group * ROWS, half)

    def item3(k):
        return jnp.concatenate(
            [flat[pl.ds(h * ROWS + k, MODES, stride=2 * ROWS), :] for h in range(2)], axis=1
        )

    scale = 1.0 / math.sqrt(tokens)
    s_dev = item3(0) + item3(13)
    r_tot, d_tot, x_tot = item3(1) + item3(10), item3(2) + item3(11), item3(9) + item3(12)
    root = jnp.sqrt(lam_t)
    gres_ref[...] = scale * root * r_tot
    grate_ref[...] = scale * res_ref[...] * root * (0.5 / rate_ref[...] * r_tot - d_tot * (1.0 / tokens))
    for j in range(3):
        gshort_ref[0, j : j + 1, :] = scale * x_tot[j : j + 1, :]
        for i in (1, 2):
            k = 3 * (i - 1) + j
            gshort_ref[i, j : j + 1, :] = scale * (x_tot[3 + k : 4 + k, :] + total(item3(3 + k)))
    gskip_ref[...] = scale * x_tot[9:10, :]

    rank_h = lax.broadcasted_iota(jnp.int32, (RUNS, half), 0).astype(F32)
    for h in range(2):
        lanes = slice(h * half, (h + 1) * half)
        a, p = [], []
        for m in range(MODES):
            lam = lams[m, :, lanes]
            back = jnp.exp(lam * (float(run) * (rank_h - float(RUNS - 1))))
            a.append(jnp.exp(-lam))
            p.append(coefs[m, :, lanes] * (sloc[m, :, lanes] + back * s_dev[m : m + 1, lanes]))
        for r in range(run - 1, -1, -1):
            at = slice(RUNS * r, RUNS * (r + 1))
            p = [x * d for x, d in zip(p, a)]
            terms = p
            while len(terms) > 1:
                terms = [u + w for u, w in zip(terms[::2], terms[1::2])]
            longs[at, lanes] += terms[0]

    gated = longs[...] + skip * gf[...]
    gs[0, :rows, :] = gq[...]
    gs[1, :rows, :] = gated * feat[1]
    gs[2, :rows, :] = gated * feat[0]
    ahead_long = [
        total(coef_t * s_dev),
        total(coef_t * (s_dev - ahead_gf[0]) * jnp.exp(lam_t)),
    ]
    last = lax.broadcasted_iota(jnp.int32, (RUNS, width), 0) == RUNS - 1
    for k in range(2):
        ahead_gated = (ahead_long[k] + skip * ahead_gf[k]) * has_after
        beyond = (ahead_gq[k], ahead_gated * ahead_f[2][k], ahead_gated * ahead_f[1][k])
        for i in range(3):
            head = pltpu.roll(gs[i, RUNS * k : RUNS * (k + 1), :], RUNS - 1, axis=0)
            gs[i, rows + RUNS * k : rows + RUNS * (k + 1), :] = jnp.where(last, beyond[i], head)
    gather = jnp.where(col == RUNS * (row % run) + row // run, 1.0, 0.0).astype(BF16)
    for i in range(3):
        made = (
            tap(i, 0) * gs[i, :rows, :]
            + tap(i, 1) * gs[i, RUNS : rows + RUNS, :]
            + tap(i, 2) * gs[i, 2 * RUNS : rows + 2 * RUNS, :]
        )
        gp_ref[i] = jnp.dot(gather, made.astype(BF16), preferred_element_type=F32).astype(BF16)

    for rim in rims:
        rim.wait_send()
    others = pl.ds(0, group - 1)
    pltpu.make_async_copy(sbuf.at[others], sbuf.at[others], a_send).wait()
    pltpu.make_async_copy(bb.at[pl.ds(0, n_blocks - 1)], bb.at[pl.ds(0, n_blocks - 1)], b_send).wait()
    pltpu.make_async_copy(cbuf.at[others], cbuf.at[others], c_send).wait()


def hand_over(*refs):
    count = (len(refs) - 1) // 2
    sems = refs[-1]
    copies = [
        pltpu.make_async_copy(src, dst, sems.at[i])
        for i, (src, dst) in enumerate(zip(refs[:count], refs[count : 2 * count]))
    ]
    for copy in copies:
        copy.start()
    for copy in copies:
        copy.wait()


def solution(mesh):
    n_ctx = mesh.shape["ctx"]
    n_blocks = n_ctx // 32

    def body(projections, filtered, cotangent, short_taps, residues, pole_rates, skip_gain):
        rows, width = filtered.shape
        half = width // 2
        vmem = pl.BlockSpec(memory_space=pltpu.VMEM)
        full = (rows, width)
        made = (
            jax.ShapeDtypeStruct((3,) + full, BF16),
            jax.ShapeDtypeStruct((3, 3, width), F32),
            jax.ShapeDtypeStruct((MODES, width), F32),
            jax.ShapeDtypeStruct((MODES, width), F32),
            jax.ShapeDtypeStruct((1, width), F32),
        )
        args = (projections, filtered, cotangent, short_taps, residues.T, pole_rates.T, skip_gain.reshape(1, width))
        out = pl.pallas_call(
            functools.partial(kernel, (n_ctx, n_blocks)),
            out_shape=[pltpu.VMEM(x.shape, x.dtype) for x in made],
            in_specs=[pl.BlockSpec(memory_space=pltpu.HBM)] * 7,
            out_specs=[vmem] * 5,
            scratch_shapes=[pltpu.VMEM(x.shape, x.dtype) for x in args]
            + [
                pltpu.VMEM((3, rows + 16, width), F32),
                pltpu.VMEM((2,) + full, F32),
                pltpu.VMEM(full, F32),
                pltpu.VMEM(full, F32),
                pltpu.VMEM(full, F32),
                pltpu.VMEM((6,) + full, F32),
                pltpu.VMEM(full, F32),
                pltpu.VMEM((MODES, RUNS, width), F32),
                pltpu.VMEM((MODES, RUNS, width), F32),
                pltpu.VMEM((2 * MODES, RUNS, half), F32),
                pltpu.VMEM((2 * MODES, RUNS, half), F32),
                pltpu.VMEM((MODES, RUNS, width), F32),
                pltpu.VMEM((6, RUNS, width), F32),
                pltpu.VMEM((2 * MODES * ROWS, half), F32),
                pltpu.VMEM((32, ROWS, half), BF16),
                pltpu.VMEM((32, ROWS, half), BF16),
                pltpu.VMEM((32 * ROWS, half), F32),
                pltpu.VMEM((4, ROWS, half), BF16),
                pltpu.VMEM((4, n_blocks, ROWS, half), BF16),
                pltpu.VMEM((4 * n_blocks * ROWS, half), F32),
                pltpu.VMEM((4 * n_blocks, half), F32),
                pltpu.VMEM((32, ROWS, half), BF16),
                pltpu.VMEM((32, ROWS, half), BF16),
                pltpu.VMEM((3, rows + 16, width), F32),
                pltpu.VMEM((3, 16, width), BF16),
                pltpu.VMEM((5, 16, width), BF16),
                pltpu.SemaphoreType.DMA((7,)),
                pltpu.SemaphoreType.DMA((4,)),
                pltpu.SemaphoreType.DMA((4,)),
                pltpu.SemaphoreType.DMA,
                pltpu.SemaphoreType.DMA,
                pltpu.SemaphoreType.DMA,
                pltpu.SemaphoreType.DMA,
                pltpu.SemaphoreType.DMA,
                pltpu.SemaphoreType.DMA,
            ],
            compiler_params=pltpu.CompilerParams(
                collective_id=0, has_side_effects=True, vmem_limit_bytes=40 * 1024 * 1024
            ),
        )(*(pltpu.with_memory_space_constraint(x, pltpu.HBM) for x in args))
        out = pl.pallas_call(
            hand_over,
            out_shape=[pltpu.HBM(x.shape, x.dtype) for x in made],
            in_specs=[vmem] * 5,
            out_specs=[pl.BlockSpec(memory_space=pltpu.HBM)] * 5,
            scratch_shapes=[pltpu.SemaphoreType.DMA((5,))],
        )(*(pltpu.with_memory_space_constraint(x, pltpu.VMEM) for x in out))
        return out[0], out[1], out[2].T, out[3].T, out[4].reshape(width)

    return jax.shard_map(
        body,
        mesh=mesh,
        in_specs=(
            P(None, "ctx", "ch"),
            P("ctx", "ch"),
            P("ctx", "ch"),
            P(None, None, "ch"),
            P("ch", None),
            P("ch", None),
            P("ch"),
        ),
        out_specs=(
            P(None, "ctx", "ch"),
            P(None, None, "ch"),
            P("ch", None),
            P("ch", None),
            P("ch"),
        ),
        check_vma=False,
    )
```

```python
import functools
import math

import jax
import jax.numpy as jnp
from jax import lax
from jax.experimental import pallas as pl
from jax.experimental.pallas import tpu as pltpu
from jax.sharding import PartitionSpec as P

MESH = pl.DeviceIdType.MESH
F32 = jnp.float32
BF16 = jnp.bfloat16

RUNS = 8
MODES = 16
ROWS = 16
ROW_L, ROW_LP, ROW_V, ROW_VP, ROW_W, ROW_R, ROW_D, ROW_X = 0, 1, 2, 3, 4, 10, 11, 12
REST = 3


def up(x, by, size):
    return pltpu.roll(x, size - by, axis=0)


def suffix(state, slope, lam, length, count):
    row = lax.broadcasted_iota(jnp.int32, state.shape, 0)
    by = 1
    while by < count:
        decay = jnp.where(row < count - by, jnp.exp(lam * float(-length * by)), 0.0)
        later, later_slope = up(state, by, count), up(slope, by, count)
        slope = slope + decay * (later_slope + float(length * by) * later)
        state = state + decay * later
        by *= 2
    inside = row < count - 1
    return (
        state,
        slope,
        jnp.where(inside, up(state, 1, count), 0.0),
        jnp.where(inside, up(slope, 1, count), 0.0),
    )


def total(x):
    return jnp.sum(x, axis=0, keepdims=True)


def rest(x):
    return x - x.astype(BF16).astype(F32)


def kernel(
    geometry,
    proj_hbm,
    filt_hbm,
    cot_hbm,
    taps_hbm,
    res_hbm,
    rate_hbm,
    skip_hbm,
    gp_ref,
    gshort_ref,
    gres_ref,
    grate_ref,
    gskip_ref,
    proj_ref,
    filt_ref,
    cot_ref,
    taps_ref,
    res_ref,
    rate_ref,
    skip_ref,
    ext,
    feat,
    gf,
    gv,
    gz,
    gq,
    ys,
    longs,
    lams,
    coefs,
    owner_lam,
    owner_coef,
    sloc,
    crosses,
    sums,
    sbuf,
    rbuf,
    flat,
    bbuf,
    bb,
    flat2,
    si_ref,
    cbuf,
    cr,
    gs,
    halo_prev,
    halo_next,
    in_sem,
    halo_send,
    halo_recv,
    a_send,
    a_recv,
    b_send,
    b_recv,
    c_send,
    c_recv,
):
    n_ctx, n_blocks = geometry
    rows = proj_ref.shape[1]
    width = proj_ref.shape[2]
    half = width // 2
    run = rows // RUNS
    tokens = rows * n_ctx
    per_block = 8
    group = 32
    me = lax.axis_index("ctx")
    y = lax.div(me, per_block * n_blocks)
    zh = lax.rem(lax.div(me, per_block), n_blocks)
    lo = lax.rem(me, per_block)
    pos = y * per_block + lo
    held = (
        (taps_hbm, taps_ref),
        (res_hbm, res_ref),
        (rate_hbm, rate_ref),
        (skip_hbm, skip_ref),
        (proj_hbm, proj_ref),
        (cot_hbm, cot_ref),
        (filt_hbm, filt_ref),
    )
    loads = [pltpu.make_async_copy(src, dst, in_sem.at[i]) for i, (src, dst) in enumerate(held)]
    for load in loads:
        load.start()

    ys_of = [lax.rem(y + d, 4) for d in range(4)]
    los_of = [lo] + [lax.rem(lo + d, per_block) for d in range(1, per_block)]
    bases = [v * (per_block * n_blocks) + zh * per_block for v in ys_of]
    peers = [
        (ys_of[d] * per_block + los_of[k], bases[d] + los_of[k])
        for d in (2, 1, 3, 0)
        for k in (2, 6, 3, 5, 4, 7, 1, 0)
        if (d, k) != (0, 0)
    ]
    cousins = [y * (per_block * n_blocks) + lax.rem(zh + j, n_blocks) * per_block + lo for j in (2, 1, 3)]
    before, after = lax.rem(me + n_ctx - 1, n_ctx), lax.rem(me + 1, n_ctx)
    barrier = pltpu.get_barrier_semaphore()
    for d in cousins + [index for _, index in peers] + [before, after]:
        pl.semaphore_signal(barrier, inc=1, device_id={"ctx": d}, device_id_type=MESH)

    row = lax.broadcasted_iota(jnp.int32, (rows, rows), 0)
    col = lax.broadcasted_iota(jnp.int32, (rows, rows), 1)
    spread = jnp.where(col == run * (row % RUNS) + row // RUNS, 1.0, 0.0).astype(BF16)
    for load in loads[:4]:
        load.wait()

    lam_t = rate_ref[...] * (1.0 / tokens)
    coef_t = res_ref[...] * jnp.sqrt(lam_t)
    for m in range(MODES):
        lam_m = jnp.broadcast_to(lam_t[m : m + 1, :], (RUNS, width))
        coef_m = jnp.broadcast_to(coef_t[m : m + 1, :], (RUNS, width))
        lams[m] = lam_m
        coefs[m] = coef_m
        for h in range(2):
            owner_lam[2 * m + h] = lam_m[:, h * half : (h + 1) * half]
            owner_coef[2 * m + h] = coef_m[:, h * half : (h + 1) * half]

    def placed(x):
        return jnp.dot(spread, x, preferred_element_type=F32)

    first = lax.broadcasted_iota(jnp.int32, (RUNS, width), 0) == 0
    first_two = lax.broadcasted_iota(jnp.int32, (2 * RUNS, width), 0) % RUNS == 0
    for load in loads[4:]:
        load.wait()
    for i in range(3):
        ext[i, 16:, :] = placed(proj_ref[i])
        for back in (2, 1):
            tail = pltpu.roll(ext[i, 16 + RUNS * (run - back) : 16 + RUNS * (run - back + 1), :], 1, axis=0)
            ext[i, 16 - 8 * back : 24 - 8 * back, :] = jnp.where(first, 0.0, tail)

    def tap(i, j):
        return taps_ref[i, j : j + 1, :]

    def shifted(i, j):
        return ext[i, 16 - 8 * j : 16 - 8 * j + rows, :]

    def masked(x):
        return jnp.concatenate([jnp.where(first_two, 0.0, x[: 2 * RUNS]), x[2 * RUNS :]], axis=0)

    cot = placed(cot_ref[...])
    gq[...] = cot * placed(filt_ref[...])
    for i in range(3):
        made = tap(i, 0) * shifted(i, 0) + tap(i, 1) * shifted(i, 1) + tap(i, 2) * shifted(i, 2)
        if i == 0:
            gf[...] = masked(cot * made)
        else:
            feat[i - 1] = made
    gv[...] = masked(feat[0] * feat[1])
    step_of = lax.broadcasted_iota(jnp.int32, (rows, width), 0) // RUNS
    to_end = (run - step_of).astype(F32)
    gz[...] = to_end * gv[...]
    for j in range(3):
        ys[j] = masked(feat[1] * shifted(1, j))
        ys[3 + j] = masked(feat[0] * shifted(2, j))

    pl.semaphore_wait(barrier, group - 1 + n_blocks - 1 + 2)
    last_rows, first_rows = pl.ds(rows - 16, 16), pl.ds(0, 16)
    rims = (
        (proj_ref.at[:, last_rows], halo_prev, after),
        (proj_ref.at[:, first_rows], halo_next.at[pl.ds(0, 3)], before),
        (cot_ref.at[first_rows], halo_next.at[3], before),
        (filt_ref.at[first_rows], halo_next.at[4], before),
    )
    rims = [
        pltpu.make_async_remote_copy(
            src, dst, halo_send.at[i], halo_recv.at[i], device_id={"ctx": to}, device_id_type=MESH
        )
        for i, (src, dst, to) in enumerate(rims)
    ]
    for rim in rims:
        rim.start()
    longs[...] = jnp.zeros_like(longs)
    crosses[...] = jnp.zeros_like(crosses)

    rank = lax.broadcasted_iota(jnp.int32, (RUNS, width), 0).astype(F32)

    def one_mode(m, _):
        lam = lams[m]
        coef = coefs[m]
        a = jnp.exp(-lam)
        zero = jnp.zeros((RUNS, width), F32)
        state, slope, r_sum, d_sum, vp = zero, zero, zero, zero, zero
        w = [zero] * 6
        for step in range(run):
            low = slice(RUNS * (run - 1 - step), RUNS * (run - step))
            high = slice(RUNS * step, RUNS * (step + 1))
            slope = a * (slope + state)
            state = a * state + gf[low, :]
            longs[low, :] += coef * state
            gv_low = gv[low, :]
            r_sum = r_sum + gv_low * state
            d_sum = d_sum + gv_low * slope
            vp = a * (vp + gz[high, :])
            for k in range(6):
                w[k] = a * (w[k] + ys[k, high, :])
        v = tap(1, 0) * w[0] + tap(1, 1) * w[1] + tap(1, 2) * w[2]
        inner, inner_slope, s_loc, sp_loc = suffix(state, slope, lam, run, RUNS)
        sloc[m] = s_loc
        weight = jnp.exp(lam * (float(run) * (rank - float(RUNS - 1))))
        def put(k, value):
            for h in range(2):
                sums[pl.ds((h * ROWS + k) * MODES + m, 1), :] = value[:, h * half : (h + 1) * half]

        put(ROW_L, inner[0:1, :])
        put(ROW_LP, inner_slope[0:1, :])
        put(ROW_V, total(weight * v))
        put(ROW_VP, total(weight * (vp + float(run) * (float(RUNS - 1) - rank) * v)))
        state_in = coef * s_loc
        for k in range(6):
            put(ROW_W + k, total(weight * w[k]))
            crosses[k] += state_in * w[k]
        put(ROW_R, total(r_sum + v * s_loc))
        put(ROW_D, total(d_sum + vp * s_loc + v * sp_loc))
        return 0

    lax.fori_loop(0, MODES, one_mode, 0)

    skip = skip_ref[...]
    inner_gated = longs[...] + skip * gf[...]
    own_query = masked(gq[...])
    plain = [total(own_query * shifted(0, j)) for j in range(3)]
    plain += [total(inner_gated * ys[k]) + total(crosses[k]) for k in range(6)]
    plain.append(total(gf[...] * gv[...]))

    rims[0].wait_recv()
    has_before = jnp.where(me > 0, 1.0, 0.0)
    before_rows = [halo_prev[i].astype(F32)[14:16] * has_before for i in range(3)]
    x = [
        {-2: before_rows[i][0:1], -1: before_rows[i][1:2], 0: ext[i, 16:17, :], 1: ext[i, 24:25, :]}
        for i in range(3)
    ]
    f = [[tap(i, 0) * x[i][t] + tap(i, 1) * x[i][t - 1] + tap(i, 2) * x[i][t - 2] for t in range(2)] for i in range(3)]
    cot_two = [cot[0:1], cot[RUNS : RUNS + 1]]
    gf_two = [cot_two[t] * f[0][t] for t in range(2)]
    gv_two = [f[1][t] * f[2][t] for t in range(2)]
    ys_two = [[f[2][t] * x[1][t - j] for j in range(3)] + [f[1][t] * x[2][t - j] for j in range(3)] for t in range(2)]

    def each_mode(k):
        return jnp.concatenate(
            [sums[(h * ROWS + k) * MODES : (h * ROWS + k + 1) * MODES, :] for h in range(2)], axis=1
        )

    def keep(k, value):
        for h in range(2):
            sums[(h * ROWS + k) * MODES : (h * ROWS + k + 1) * MODES, :] = value[:, h * half : (h + 1) * half]

    a_t = jnp.exp(-lam_t)
    back_two = jnp.exp(2.0 * lam_t)
    two, two_slope = each_mode(ROW_L), each_mode(ROW_LP)
    two, two_slope = back_two * two, back_two * (two_slope - 2.0 * two)
    slope_1 = a_t * (two_slope + two)
    state_1 = gf_two[1] + a_t * two
    slope_0 = a_t * (slope_1 + state_1)
    state_0 = gf_two[0] + a_t * state_1
    decays = [jnp.exp(lam_t * -float(rows)), jnp.exp(lam_t * -float(rows - 1))]
    parts = [decays[t] * gv_two[t] for t in range(2)]
    keep(ROW_L, state_0)
    keep(ROW_LP, slope_0)
    keep(ROW_V, each_mode(ROW_V) + parts[0] + parts[1])
    keep(ROW_VP, each_mode(ROW_VP) + float(rows) * parts[0] + float(rows - 1) * parts[1])
    for k in range(6):
        keep(ROW_W + k, each_mode(ROW_W + k) + decays[0] * ys_two[0][k] + decays[1] * ys_two[1][k])
    r_all = each_mode(ROW_R) + gv_two[1] * state_1 + gv_two[0] * state_0
    d_all = each_mode(ROW_D) + gv_two[1] * slope_1 + gv_two[0] * slope_0
    keep(ROW_R, r_all)
    keep(ROW_R + REST, rest(r_all))
    keep(ROW_D, d_all)
    keep(ROW_D + REST, rest(d_all))
    gated_two = [total(coef_t * state_0) + skip * gf_two[0], total(coef_t * state_1) + skip * gf_two[1]]
    for t in range(2):
        for j in range(3):
            plain[j] = plain[j] + gq[RUNS * t : RUNS * t + 1, :] * x[0][t - j]
        for k in range(6):
            plain[3 + k] = plain[3 + k] + gated_two[t] * ys_two[t][k]
        plain[9] = plain[9] + gf_two[t] * gv_two[t]
    plain = jnp.concatenate(plain + [jnp.zeros((MODES - len(plain), width), F32)], axis=0)
    keep(ROW_X, plain)
    keep(ROW_X + REST, rest(plain))
    for m in range(MODES):
        for h in range(2):
            sbuf[2 * m + h] = sums[pl.ds(h * ROWS * MODES + m, ROWS, stride=MODES), :].astype(BF16)

    own_a = pltpu.make_async_copy(sbuf.at[pos], rbuf.at[pos], a_recv)
    own_a.start()
    for p, index in peers:
        pltpu.make_async_remote_copy(
            sbuf.at[p], rbuf.at[pos], a_send, a_recv, device_id={"ctx": index}, device_id_type=MESH
        ).start()

    direct = [total(coef_t) * gf_two[0] + total(coef_t * a_t) * gf_two[1], total(coef_t) * gf_two[1]]
    for t in range(2):
        at = slice(RUNS * t, RUNS * t + 1)
        gf[at, :] = gf_two[t]
        longs[at, :] += direct[t]
        for i in (1, 2):
            feat[i - 1, at, :] = f[i][t]

    pltpu.make_async_copy(rbuf, rbuf, a_recv).wait()

    lam_o = owner_lam[pos]
    coef_o = owner_coef[pos]
    flat[...] = rbuf[...].astype(F32).reshape(group * ROWS, half)
    rank8 = lax.broadcasted_iota(jnp.int32, (per_block, half), 0).astype(F32)
    weight = jnp.exp(lam_o * (float(rows) * (rank8 - float(per_block - 1))))
    inside = []
    acc_r = acc_d = acc_x = jnp.zeros((per_block, half), F32)
    acc_w = [acc_r] * 6
    for b in range(4):
        base = b * per_block * ROWS

        def item(k):
            return flat[pl.ds(base + k, per_block, stride=ROWS), :]

        state, slope, v, vp = item(ROW_L), item(ROW_LP), item(ROW_V), item(ROW_VP)
        inner, inner_slope, s_int, sp_int = suffix(state, slope, lam_o, rows, per_block)
        inside.append(s_int)
        parts = [
            inner[0:1, :],
            inner_slope[0:1, :],
            total(weight * v),
            total(weight * (vp + float(rows) * (float(per_block - 1) - rank8) * v)),
        ]
        acc_r = acc_r + (item(ROW_R) + item(ROW_R + REST)) + v * s_int
        acc_d = acc_d + (item(ROW_D) + item(ROW_D + REST)) + vp * s_int + v * sp_int
        acc_x = acc_x + (item(ROW_X) + item(ROW_X + REST))
        for k in range(6):
            w_k = item(ROW_W + k)
            parts.append(total(weight * w_k))
            acc_w[k] = acc_w[k] + w_k * s_int
        for k, part in enumerate(parts):
            flat2[b * ROWS + k : b * ROWS + k + 1, :] = part
        flat2[b * ROWS + 10 : b * ROWS + ROWS, :] = jnp.zeros((ROWS - 10, half), F32)
    for k in range(6):
        value = total(acc_w[k])
        flat2[10 + k : 11 + k, :] = value
        flat2[2 * ROWS + 10 + k : 2 * ROWS + 11 + k, :] = rest(value)
    for k, acc in enumerate((acc_r, acc_d, acc_x)):
        value = total(acc)
        flat2[ROWS + 10 + k : ROWS + 11 + k, :] = value
        flat2[ROWS + 10 + REST + k : ROWS + 11 + REST + k, :] = rest(value)
    bbuf[...] = flat2[: 4 * ROWS, :].astype(BF16).reshape(4, ROWS, half)

    own_b = pltpu.make_async_copy(bbuf, bb.at[:, zh], b_recv)
    own_b.start()
    for index in cousins:
        pltpu.make_async_remote_copy(
            bbuf, bb.at[:, zh], b_send, b_recv, device_id={"ctx": index}, device_id_type=MESH
        ).start()
    pltpu.make_async_copy(bb, bb, b_recv).wait()

    n_int = 4 * n_blocks
    flat2[...] = bb[...].astype(F32).reshape(n_int * ROWS, half)

    def item2(k):
        return flat2[pl.ds(k, n_int, stride=ROWS), :]

    lam2 = jnp.concatenate([lam_o, lam_o], axis=0)
    v, vp = item2(ROW_V), item2(ROW_VP)
    _, _, s_all, sp_all = suffix(item2(ROW_L), item2(ROW_LP), lam2, rows * per_block, n_int)
    si_ref[...] = s_all
    parts = [total(v * s_all), total(vp * s_all + v * sp_all)]
    interval = lax.broadcasted_iota(jnp.int32, (n_int, half), 0) // n_blocks
    in_1, in_0_2 = interval == 1, (interval == 0) | (interval == 2)

    def sum_1(k):
        return total(jnp.where(in_1, item2(10 + k) + item2(10 + REST + k), 0.0))

    for k in range(2):
        parts[k] = parts[k] + sum_1(k)
    for k in range(6):
        parts.append(coef_o[0:1, :] * total(item2(ROW_W + k) * s_all + jnp.where(in_0_2, item2(10 + k), 0.0)))
    parts.append(sum_1(2))
    parts += [rest(parts[0]), rest(parts[1]), rest(parts[8])]
    row16 = lax.broadcasted_iota(jnp.int32, (ROWS, half), 0)
    common = jnp.zeros((ROWS, half), F32)
    for k, part in enumerate(parts):
        common = jnp.where(row16 == 1 + k, part, common)
    for b in range(4):
        s_dev = inside[b] + weight * si_ref[pl.ds(b * n_blocks + zh, 1), :]
        s_rest = rest(s_dev)
        for i in range(per_block):
            own = jnp.where(row16 == 0, s_dev[i : i + 1, :], common)
            cbuf[b * per_block + i] = jnp.where(row16 == 13, s_rest[i : i + 1, :], own).astype(BF16)

    own_c = pltpu.make_async_copy(cbuf.at[pos], cr.at[pos], c_recv)
    own_c.start()
    for p, index in peers:
        pltpu.make_async_remote_copy(
            cbuf.at[p], cr.at[pos], c_send, c_recv, device_id={"ctx": index}, device_id_type=MESH
        ).start()

    for rim in rims[1:]:
        rim.wait_recv()
    has_after = jnp.where(me < n_ctx - 1, 1.0, 0.0)
    ahead = [halo_next[i].astype(F32) * has_after for i in range(5)]

    def ahead_feat(i, k):
        mine = [ext[i, 16 + RUNS * (run - 1 - b) + RUNS - 1 : 16 + RUNS * (run - b), :] for b in range(2)]
        if k == 0:
            return tap(i, 0) * ahead[i][0:1] + tap(i, 1) * mine[0] + tap(i, 2) * mine[1]
        return tap(i, 0) * ahead[i][1:2] + tap(i, 1) * ahead[i][0:1] + tap(i, 2) * mine[0]

    ahead_f = [[ahead_feat(i, k) for k in range(2)] for i in range(3)]
    ahead_gf = [ahead[3][k : k + 1] * ahead_f[0][k] for k in range(2)]
    ahead_gq = [ahead[3][k : k + 1] * ahead[4][k : k + 1] for k in range(2)]

    gather = jnp.where(col == RUNS * lax.rem(row, run) + lax.div(row, run), 1.0, 0.0).astype(BF16)
    last = lax.broadcasted_iota(jnp.int32, (RUNS, width), 0) == RUNS - 1

    def finish(i, beyond):
        for k in range(2):
            head = pltpu.roll(gs[i, RUNS * k : RUNS * (k + 1), :], RUNS - 1, axis=0)
            gs[i, rows + RUNS * k : rows + RUNS * (k + 1), :] = jnp.where(last, beyond[k], head)
        made = (
            tap(i, 0) * gs[i, :rows, :]
            + tap(i, 1) * gs[i, RUNS : rows + RUNS, :]
            + tap(i, 2) * gs[i, 2 * RUNS : rows + 2 * RUNS, :]
        )
        gp_ref[i] = jnp.dot(gather, made.astype(BF16), preferred_element_type=F32).astype(BF16)

    gs[0, :rows, :] = gq[...]
    finish(0, ahead_gq)
    for m in range(MODES):
        sloc[m] = coefs[m] * sloc[m]
        coefs[m] = coefs[m] * jnp.exp(lams[m] * (float(run) * (rank - float(RUNS - 1))))
        lams[m] = jnp.exp(-lams[m])

    pltpu.make_async_copy(cr, cr, c_recv).wait()
    flat[...] = cr[...].astype(F32).reshape(group * ROWS, half)

    def item3(k):
        return jnp.concatenate(
            [flat[pl.ds(h * ROWS + k, MODES, stride=2 * ROWS), :] for h in range(2)], axis=1
        )

    scale = 1.0 / math.sqrt(tokens)
    s_dev = item3(0) + item3(13)
    r_tot, d_tot, x_tot = item3(1) + item3(10), item3(2) + item3(11), item3(9) + item3(12)
    root = jnp.sqrt(lam_t)
    gres_ref[...] = scale * root * r_tot
    grate_ref[...] = scale * res_ref[...] * root * (0.5 / rate_ref[...] * r_tot - d_tot * (1.0 / tokens))
    for j in range(3):
        gshort_ref[0, j : j + 1, :] = scale * x_tot[j : j + 1, :]
        for i in (1, 2):
            k = 3 * (i - 1) + j
            gshort_ref[i, j : j + 1, :] = scale * (x_tot[3 + k : 4 + k, :] + total(item3(3 + k)))
    gskip_ref[...] = scale * x_tot[9:10, :]

    for h in range(2):
        lanes = slice(h * half, (h + 1) * half)
        a = [lams[m, :, lanes] for m in range(MODES)]
        p = [sloc[m, :, lanes] + coefs[m, :, lanes] * s_dev[m : m + 1, lanes] for m in range(MODES)]
        for r in range(run - 1, -1, -1):
            at = slice(RUNS * r, RUNS * (r + 1))
            p = [x * d for x, d in zip(p, a)]
            terms = p
            while len(terms) > 1:
                terms = [u + w for u, w in zip(terms[::2], terms[1::2])]
            longs[at, lanes] += terms[0]

    gated = longs[...] + skip * gf[...]
    gs[1, :rows, :] = gated * feat[1]
    gs[2, :rows, :] = gated * feat[0]
    ahead_long = [
        total(coef_t * s_dev),
        total(coef_t * (s_dev - ahead_gf[0]) * jnp.exp(lam_t)),
    ]
    ahead_gated = [(ahead_long[k] + skip * ahead_gf[k]) * has_after for k in range(2)]
    finish(1, [ahead_gated[k] * ahead_f[2][k] for k in range(2)])
    finish(2, [ahead_gated[k] * ahead_f[1][k] for k in range(2)])

    for rim in rims:
        rim.wait_send()
    others = pl.ds(0, group - 1)
    pltpu.make_async_copy(sbuf.at[others], sbuf.at[others], a_send).wait()
    pltpu.make_async_copy(bb.at[pl.ds(0, n_blocks - 1)], bb.at[pl.ds(0, n_blocks - 1)], b_send).wait()
    pltpu.make_async_copy(cbuf.at[others], cbuf.at[others], c_send).wait()


def hand_over(*refs):
    count = (len(refs) - 1) // 2
    sems = refs[-1]
    copies = [
        pltpu.make_async_copy(src, dst, sems.at[i])
        for i, (src, dst) in enumerate(zip(refs[:count], refs[count : 2 * count]))
    ]
    for copy in copies:
        copy.start()
    for copy in copies:
        copy.wait()


def solution(mesh):
    n_ctx = mesh.shape["ctx"]
    n_blocks = n_ctx // 32

    def body(projections, filtered, cotangent, short_taps, residues, pole_rates, skip_gain):
        rows, width = filtered.shape
        half = width // 2
        vmem = pl.BlockSpec(memory_space=pltpu.VMEM)
        full = (rows, width)
        made = (
            jax.ShapeDtypeStruct((3,) + full, BF16),
            jax.ShapeDtypeStruct((3, 3, width), F32),
            jax.ShapeDtypeStruct((MODES, width), F32),
            jax.ShapeDtypeStruct((MODES, width), F32),
            jax.ShapeDtypeStruct((1, width), F32),
        )
        args = (projections, filtered, cotangent, short_taps, residues.T, pole_rates.T, skip_gain.reshape(1, width))
        out = pl.pallas_call(
            functools.partial(kernel, (n_ctx, n_blocks)),
            out_shape=[pltpu.VMEM(x.shape, x.dtype) for x in made],
            in_specs=[pl.BlockSpec(memory_space=pltpu.HBM)] * 7,
            out_specs=[vmem] * 5,
            scratch_shapes=[pltpu.VMEM(x.shape, x.dtype) for x in args]
            + [
                pltpu.VMEM((3, rows + 16, width), F32),
                pltpu.VMEM((2,) + full, F32),
                pltpu.VMEM(full, F32),
                pltpu.VMEM(full, F32),
                pltpu.VMEM(full, F32),
                pltpu.VMEM(full, F32),
                pltpu.VMEM((6,) + full, F32),
                pltpu.VMEM(full, F32),
                pltpu.VMEM((MODES, RUNS, width), F32),
                pltpu.VMEM((MODES, RUNS, width), F32),
                pltpu.VMEM((2 * MODES, RUNS, half), F32),
                pltpu.VMEM((2 * MODES, RUNS, half), F32),
                pltpu.VMEM((MODES, RUNS, width), F32),
                pltpu.VMEM((6, RUNS, width), F32),
                pltpu.VMEM((2 * MODES * ROWS, half), F32),
                pltpu.VMEM((32, ROWS, half), BF16),
                pltpu.VMEM((32, ROWS, half), BF16),
                pltpu.VMEM((32 * ROWS, half), F32),
                pltpu.VMEM((4, ROWS, half), BF16),
                pltpu.VMEM((4, n_blocks, ROWS, half), BF16),
                pltpu.VMEM((4 * n_blocks * ROWS, half), F32),
                pltpu.VMEM((4 * n_blocks, half), F32),
                pltpu.VMEM((32, ROWS, half), BF16),
                pltpu.VMEM((32, ROWS, half), BF16),
                pltpu.VMEM((3, rows + 16, width), F32),
                pltpu.VMEM((3, 16, width), BF16),
                pltpu.VMEM((5, 16, width), BF16),
                pltpu.SemaphoreType.DMA((7,)),
                pltpu.SemaphoreType.DMA((4,)),
                pltpu.SemaphoreType.DMA((4,)),
                pltpu.SemaphoreType.DMA,
                pltpu.SemaphoreType.DMA,
                pltpu.SemaphoreType.DMA,
                pltpu.SemaphoreType.DMA,
                pltpu.SemaphoreType.DMA,
                pltpu.SemaphoreType.DMA,
            ],
            compiler_params=pltpu.CompilerParams(
                collective_id=0, has_side_effects=True, vmem_limit_bytes=40 * 1024 * 1024
            ),
        )(*(pltpu.with_memory_space_constraint(x, pltpu.HBM) for x in args))
        out = pl.pallas_call(
            hand_over,
            out_shape=[pltpu.HBM(x.shape, x.dtype) for x in made],
            in_specs=[vmem] * 5,
            out_specs=[pl.BlockSpec(memory_space=pltpu.HBM)] * 5,
            scratch_shapes=[pltpu.SemaphoreType.DMA((5,))],
        )(*(pltpu.with_memory_space_constraint(x, pltpu.VMEM) for x in out))
        return out[0], out[1], out[2].T, out[3].T, out[4].reshape(width)

    return jax.shard_map(
        body,
        mesh=mesh,
        in_specs=(
            P(None, "ctx", "ch"),
            P("ctx", "ch"),
            P("ctx", "ch"),
            P(None, None, "ch"),
            P("ch", None),
            P("ch", None),
            P("ch"),
        ),
        out_specs=(
            P(None, "ctx", "ch"),
            P(None, None, "ch"),
            P("ch", None),
            P("ch", None),
            P("ch"),
        ),
        check_vma=False,
    )
```

```python
import functools
import math

import jax
import jax.numpy as jnp
from jax import lax
from jax.experimental import pallas as pl
from jax.experimental.pallas import tpu as pltpu
from jax.sharding import PartitionSpec as P

MESH = pl.DeviceIdType.MESH
F32 = jnp.float32
BF16 = jnp.bfloat16

RUNS = 8
MODES = 16
ROWS = 16
EARLY = 12
ROW_L, ROW_LP, ROW_V, ROW_VP, ROW_W, ROW_R, ROW_D, ROW_X = 0, 1, 2, 3, 4, 10, 11, 12
REST = 3


def up(x, by, size):
    return pltpu.roll(x, size - by, axis=0)


def suffix(state, slope, lam, length, count):
    row = lax.broadcasted_iota(jnp.int32, state.shape, 0)
    by = 1
    while by < count:
        decay = jnp.where(row < count - by, jnp.exp(lam * float(-length * by)), 0.0)
        later, later_slope = up(state, by, count), up(slope, by, count)
        slope = slope + decay * (later_slope + float(length * by) * later)
        state = state + decay * later
        by *= 2
    inside = row < count - 1
    return (
        state,
        slope,
        jnp.where(inside, up(state, 1, count), 0.0),
        jnp.where(inside, up(slope, 1, count), 0.0),
    )


def total(x):
    return jnp.sum(x, axis=0, keepdims=True)


def rest(x):
    return x - x.astype(BF16).astype(F32)


def kernel(
    geometry,
    proj_hbm,
    filt_hbm,
    cot_hbm,
    taps_hbm,
    res_hbm,
    rate_hbm,
    skip_hbm,
    gp_ref,
    gshort_ref,
    gres_ref,
    grate_ref,
    gskip_ref,
    proj_ref,
    filt_ref,
    cot_ref,
    taps_ref,
    res_ref,
    rate_ref,
    skip_ref,
    ext,
    feat,
    gf,
    gv,
    gz,
    gq,
    ys,
    longs,
    lams,
    coefs,
    owner_lam,
    owner_coef,
    sloc,
    crosses,
    sums,
    sbuf,
    rbuf,
    flat,
    bbuf,
    bb,
    flat2,
    si_ref,
    cbuf,
    cr,
    gs,
    rim_rows,
    halo_prev,
    halo_next,
    in_sem,
    halo_send,
    halo_recv,
    a_send,
    a_recv,
    b_send,
    b_recv,
    c_send,
    c_recv,
):
    n_ctx, n_blocks = geometry
    rows = proj_ref.shape[1]
    width = proj_ref.shape[2]
    half = width // 2
    run = rows // RUNS
    tokens = rows * n_ctx
    per_block = 8
    group = 32
    me = lax.axis_index("ctx")
    y = lax.div(me, per_block * n_blocks)
    zh = lax.rem(lax.div(me, per_block), n_blocks)
    lo = lax.rem(me, per_block)
    pos = y * per_block + lo
    held = (
        (taps_hbm, taps_ref),
        (res_hbm, res_ref),
        (rate_hbm, rate_ref),
        (skip_hbm, skip_ref),
        (proj_hbm, proj_ref),
        (cot_hbm, cot_ref),
        (filt_hbm, filt_ref),
    )
    loads = [pltpu.make_async_copy(src, dst, in_sem.at[i]) for i, (src, dst) in enumerate(held)]
    for load in loads:
        load.start()

    ys_of = [lax.rem(y + d, 4) for d in range(4)]
    los_of = [lo] + [lax.rem(lo + d, per_block) for d in range(1, per_block)]
    bases = [v * (per_block * n_blocks) + zh * per_block for v in ys_of]
    peers = [
        (ys_of[d] * per_block + los_of[k], bases[d] + los_of[k])
        for d in (2, 1, 3, 0)
        for k in (2, 6, 3, 5, 4, 7, 1, 0)
        if (d, k) != (0, 0)
    ]
    cousins = [y * (per_block * n_blocks) + lax.rem(zh + j, n_blocks) * per_block + lo for j in (2, 1, 3)]
    before, after = lax.rem(me + n_ctx - 1, n_ctx), lax.rem(me + 1, n_ctx)
    barrier = pltpu.get_barrier_semaphore()
    for d in cousins + [index for _, index in peers] + [before, after]:
        pl.semaphore_signal(barrier, inc=1, device_id={"ctx": d}, device_id_type=MESH)

    row = lax.broadcasted_iota(jnp.int32, (rows, rows), 0)
    col = lax.broadcasted_iota(jnp.int32, (rows, rows), 1)
    spread = jnp.where(col == run * (row % RUNS) + row // RUNS, 1.0, 0.0).astype(BF16)
    for load in loads[:4]:
        load.wait()

    lam_t = rate_ref[...] * (1.0 / tokens)
    coef_t = res_ref[...] * jnp.sqrt(lam_t)
    for m in range(MODES):
        lam_m = jnp.broadcast_to(lam_t[m : m + 1, :], (RUNS, width))
        coef_m = jnp.broadcast_to(coef_t[m : m + 1, :], (RUNS, width))
        lams[m] = lam_m
        coefs[m] = coef_m
        for h in range(2):
            owner_lam[2 * m + h] = lam_m[:, h * half : (h + 1) * half]
            owner_coef[2 * m + h] = coef_m[:, h * half : (h + 1) * half]

    def placed(x):
        return jnp.dot(spread, x, preferred_element_type=F32)

    first = lax.broadcasted_iota(jnp.int32, (RUNS, width), 0) == 0
    first_two = lax.broadcasted_iota(jnp.int32, (2 * RUNS, width), 0) % RUNS == 0
    for load in loads[4:]:
        load.wait()
    for i in range(3):
        ext[i, 16:, :] = placed(proj_ref[i])
        for back in (2, 1):
            tail = pltpu.roll(ext[i, 16 + RUNS * (run - back) : 16 + RUNS * (run - back + 1), :], 1, axis=0)
            ext[i, 16 - 8 * back : 24 - 8 * back, :] = jnp.where(first, 0.0, tail)

    def tap(i, j):
        return taps_ref[i, j : j + 1, :]

    def shifted(i, j):
        return ext[i, 16 - 8 * j : 16 - 8 * j + rows, :]

    def masked(x):
        return jnp.concatenate([jnp.where(first_two, 0.0, x[: 2 * RUNS]), x[2 * RUNS :]], axis=0)

    cot = placed(cot_ref[...])
    gq[...] = cot * placed(filt_ref[...])
    for i in range(3):
        made = tap(i, 0) * shifted(i, 0) + tap(i, 1) * shifted(i, 1) + tap(i, 2) * shifted(i, 2)
        if i == 0:
            gf[...] = masked(cot * made)
        else:
            feat[i - 1] = made
    gv[...] = masked(feat[0] * feat[1])
    step_of = lax.broadcasted_iota(jnp.int32, (rows, width), 0) // RUNS
    to_end = (run - step_of).astype(F32)
    gz[...] = to_end * gv[...]
    for j in range(3):
        ys[j] = masked(feat[1] * shifted(1, j))
        ys[3 + j] = masked(feat[0] * shifted(2, j))

    longs[...] = jnp.zeros_like(longs)
    crosses[...] = jnp.zeros_like(crosses)

    rank = lax.broadcasted_iota(jnp.int32, (RUNS, width), 0).astype(F32)

    def one_mode(m, _):
        lam = lams[m]
        coef = coefs[m]
        a = jnp.exp(-lam)
        zero = jnp.zeros((RUNS, width), F32)
        state, slope, r_sum, d_sum, vp = zero, zero, zero, zero, zero
        w = [zero] * 6
        for step in range(run):
            low = slice(RUNS * (run - 1 - step), RUNS * (run - step))
            high = slice(RUNS * step, RUNS * (step + 1))
            slope = a * (slope + state)
            state = a * state + gf[low, :]
            longs[low, :] += coef * state
            gv_low = gv[low, :]
            r_sum = r_sum + gv_low * state
            d_sum = d_sum + gv_low * slope
            vp = a * (vp + gz[high, :])
            for k in range(6):
                w[k] = a * (w[k] + ys[k, high, :])
        v = tap(1, 0) * w[0] + tap(1, 1) * w[1] + tap(1, 2) * w[2]
        inner, inner_slope, s_loc, sp_loc = suffix(state, slope, lam, run, RUNS)
        sloc[m] = s_loc
        weight = jnp.exp(lam * (float(run) * (rank - float(RUNS - 1))))
        def put(k, value):
            for h in range(2):
                sums[pl.ds((h * ROWS + k) * MODES + m, 1), :] = value[:, h * half : (h + 1) * half]

        put(ROW_L, inner[0:1, :])
        put(ROW_LP, inner_slope[0:1, :])
        put(ROW_V, total(weight * v))
        put(ROW_VP, total(weight * (vp + float(run) * (float(RUNS - 1) - rank) * v)))
        state_in = coef * s_loc
        for k in range(6):
            put(ROW_W + k, total(weight * w[k]))
            crosses[k] += state_in * w[k]
        put(ROW_R, total(r_sum + v * s_loc))
        put(ROW_D, total(d_sum + vp * s_loc + v * sp_loc))
        return 0

    for i in range(3):
        for b in range(2):
            at = 16 + RUNS * (run - 1 - b) + RUNS - 1
            rim_rows[2 * i + 1 - b : 2 * i + 2 - b, :] = ext[i, at : at + 1, :]
    rim_rows[6:8, :] = jnp.zeros((2, width), F32)

    lax.fori_loop(0, EARLY, one_mode, 0)

    pl.semaphore_wait(barrier, group - 1 + n_blocks - 1 + 2)
    first_rows = pl.ds(0, 16)
    rims = (
        (rim_rows, halo_prev, after),
        (proj_ref.at[:, first_rows], halo_next.at[pl.ds(0, 3)], before),
        (cot_ref.at[first_rows], halo_next.at[3], before),
        (filt_ref.at[first_rows], halo_next.at[4], before),
    )
    rims = [
        pltpu.make_async_remote_copy(
            src, dst, halo_send.at[i], halo_recv.at[i], device_id={"ctx": to}, device_id_type=MESH
        )
        for i, (src, dst, to) in enumerate(rims)
    ]
    for rim in rims:
        rim.start()
    lax.fori_loop(EARLY, MODES, one_mode, 0)

    skip = skip_ref[...]
    inner_gated = longs[...] + skip * gf[...]
    own_query = masked(gq[...])
    plain = [total(own_query * shifted(0, j)) for j in range(3)]
    plain += [total(inner_gated * ys[k]) + total(crosses[k]) for k in range(6)]
    plain.append(total(gf[...] * gv[...]))

    def each_mode(k):
        return jnp.concatenate(
            [sums[(h * ROWS + k) * MODES : (h * ROWS + k + 1) * MODES, :] for h in range(2)], axis=1
        )

    def keep(k, value):
        for h in range(2):
            sums[(h * ROWS + k) * MODES : (h * ROWS + k + 1) * MODES, :] = value[:, h * half : (h + 1) * half]

    a_t = jnp.exp(-lam_t)
    back_two = jnp.exp(2.0 * lam_t)
    two, two_slope = each_mode(ROW_L), each_mode(ROW_LP)
    two, two_slope = back_two * two, back_two * (two_slope - 2.0 * two)
    slope_1 = a_t * (two_slope + two)
    moved = a_t * two
    decays = [jnp.exp(lam_t * -float(rows)), jnp.exp(lam_t * -float(rows - 1))]
    direct_sum, moved_sum = total(coef_t), total(coef_t * a_t)
    cot_two = [cot[0:1], cot[RUNS : RUNS + 1]]

    rims[0].wait_recv()
    has_before = jnp.where(me > 0, 1.0, 0.0)
    before_rows = [halo_prev[2 * i : 2 * i + 2, :] * has_before for i in range(3)]
    x = [
        {-2: before_rows[i][0:1], -1: before_rows[i][1:2], 0: ext[i, 16:17, :], 1: ext[i, 24:25, :]}
        for i in range(3)
    ]
    f = [[tap(i, 0) * x[i][t] + tap(i, 1) * x[i][t - 1] + tap(i, 2) * x[i][t - 2] for t in range(2)] for i in range(3)]
    gf_two = [cot_two[t] * f[0][t] for t in range(2)]
    gv_two = [f[1][t] * f[2][t] for t in range(2)]
    ys_two = [[f[2][t] * x[1][t - j] for j in range(3)] + [f[1][t] * x[2][t - j] for j in range(3)] for t in range(2)]

    state_1 = gf_two[1] + moved
    slope_0 = a_t * (slope_1 + state_1)
    state_0 = gf_two[0] + a_t * state_1
    parts = [decays[t] * gv_two[t] for t in range(2)]
    keep(ROW_L, state_0)
    keep(ROW_LP, slope_0)
    keep(ROW_V, each_mode(ROW_V) + parts[0] + parts[1])
    keep(ROW_VP, each_mode(ROW_VP) + float(rows) * parts[0] + float(rows - 1) * parts[1])
    for k in range(6):
        keep(ROW_W + k, each_mode(ROW_W + k) + decays[0] * ys_two[0][k] + decays[1] * ys_two[1][k])
    r_all = each_mode(ROW_R) + gv_two[1] * state_1 + gv_two[0] * state_0
    d_all = each_mode(ROW_D) + gv_two[1] * slope_1 + gv_two[0] * slope_0
    keep(ROW_R, r_all)
    keep(ROW_R + REST, rest(r_all))
    keep(ROW_D, d_all)
    keep(ROW_D + REST, rest(d_all))
    gated_two = [total(coef_t * state_0) + skip * gf_two[0], total(coef_t * state_1) + skip * gf_two[1]]
    for t in range(2):
        for j in range(3):
            plain[j] = plain[j] + gq[RUNS * t : RUNS * t + 1, :] * x[0][t - j]
        for k in range(6):
            plain[3 + k] = plain[3 + k] + gated_two[t] * ys_two[t][k]
        plain[9] = plain[9] + gf_two[t] * gv_two[t]
    plain = jnp.concatenate(plain + [jnp.zeros((MODES - len(plain), width), F32)], axis=0)
    keep(ROW_X, plain)
    keep(ROW_X + REST, rest(plain))
    for m in range(MODES):
        for h in range(2):
            sbuf[2 * m + h] = sums[pl.ds(h * ROWS * MODES + m, ROWS, stride=MODES), :].astype(BF16)

    own_a = pltpu.make_async_copy(sbuf.at[pos], rbuf.at[pos], a_recv)
    own_a.start()
    for p, index in peers:
        pltpu.make_async_remote_copy(
            sbuf.at[p], rbuf.at[pos], a_send, a_recv, device_id={"ctx": index}, device_id_type=MESH
        ).start()

    direct = [direct_sum * gf_two[0] + moved_sum * gf_two[1], direct_sum * gf_two[1]]
    for t in range(2):
        at = slice(RUNS * t, RUNS * t + 1)
        gf[at, :] = gf_two[t]
        longs[at, :] += direct[t]
        for i in (1, 2):
            feat[i - 1, at, :] = f[i][t]

    pltpu.make_async_copy(rbuf, rbuf, a_recv).wait()

    lam_o = owner_lam[pos]
    coef_o = owner_coef[pos]
    flat[...] = rbuf[...].astype(F32).reshape(group * ROWS, half)
    rank8 = lax.broadcasted_iota(jnp.int32, (per_block, half), 0).astype(F32)
    weight = jnp.exp(lam_o * (float(rows) * (rank8 - float(per_block - 1))))
    inside = []
    acc_r = acc_d = acc_x = jnp.zeros((per_block, half), F32)
    acc_w = [acc_r] * 6
    for b in range(4):
        base = b * per_block * ROWS

        def item(k):
            return flat[pl.ds(base + k, per_block, stride=ROWS), :]

        state, slope, v, vp = item(ROW_L), item(ROW_LP), item(ROW_V), item(ROW_VP)
        inner, inner_slope, s_int, sp_int = suffix(state, slope, lam_o, rows, per_block)
        inside.append(s_int)
        parts = [
            inner[0:1, :],
            inner_slope[0:1, :],
            total(weight * v),
            total(weight * (vp + float(rows) * (float(per_block - 1) - rank8) * v)),
        ]
        acc_r = acc_r + (item(ROW_R) + item(ROW_R + REST)) + v * s_int
        acc_d = acc_d + (item(ROW_D) + item(ROW_D + REST)) + vp * s_int + v * sp_int
        acc_x = acc_x + (item(ROW_X) + item(ROW_X + REST))
        for k in range(6):
            w_k = item(ROW_W + k)
            parts.append(total(weight * w_k))
            acc_w[k] = acc_w[k] + w_k * s_int
        for k, part in enumerate(parts):
            flat2[b * ROWS + k : b * ROWS + k + 1, :] = part
        flat2[b * ROWS + 10 : b * ROWS + ROWS, :] = jnp.zeros((ROWS - 10, half), F32)
    for k in range(6):
        value = total(acc_w[k])
        flat2[10 + k : 11 + k, :] = value
        flat2[2 * ROWS + 10 + k : 2 * ROWS + 11 + k, :] = rest(value)
    for k, acc in enumerate((acc_r, acc_d, acc_x)):
        value = total(acc)
        flat2[ROWS + 10 + k : ROWS + 11 + k, :] = value
        flat2[ROWS + 10 + REST + k : ROWS + 11 + REST + k, :] = rest(value)
    bbuf[...] = flat2[: 4 * ROWS, :].astype(BF16).reshape(4, ROWS, half)

    own_b = pltpu.make_async_copy(bbuf, bb.at[:, zh], b_recv)
    own_b.start()
    for index in cousins:
        pltpu.make_async_remote_copy(
            bbuf, bb.at[:, zh], b_send, b_recv, device_id={"ctx": index}, device_id_type=MESH
        ).start()
    pltpu.make_async_copy(bb, bb, b_recv).wait()

    n_int = 4 * n_blocks
    flat2[...] = bb[...].astype(F32).reshape(n_int * ROWS, half)

    def item2(k):
        return flat2[pl.ds(k, n_int, stride=ROWS), :]

    lam2 = jnp.concatenate([lam_o, lam_o], axis=0)
    v, vp = item2(ROW_V), item2(ROW_VP)
    _, _, s_all, sp_all = suffix(item2(ROW_L), item2(ROW_LP), lam2, rows * per_block, n_int)
    si_ref[...] = s_all
    parts = [total(v * s_all), total(vp * s_all + v * sp_all)]
    interval = lax.broadcasted_iota(jnp.int32, (n_int, half), 0) // n_blocks
    in_1, in_0_2 = interval == 1, (interval == 0) | (interval == 2)

    def sum_1(k):
        return total(jnp.where(in_1, item2(10 + k) + item2(10 + REST + k), 0.0))

    for k in range(2):
        parts[k] = parts[k] + sum_1(k)
    for k in range(6):
        parts.append(coef_o[0:1, :] * total(item2(ROW_W + k) * s_all + jnp.where(in_0_2, item2(10 + k), 0.0)))
    parts.append(sum_1(2))
    parts += [rest(parts[0]), rest(parts[1]), rest(parts[8])]
    row16 = lax.broadcasted_iota(jnp.int32, (ROWS, half), 0)
    common = jnp.zeros((ROWS, half), F32)
    for k, part in enumerate(parts):
        common = jnp.where(row16 == 1 + k, part, common)
    for b in range(4):
        s_dev = inside[b] + weight * si_ref[pl.ds(b * n_blocks + zh, 1), :]
        s_rest = rest(s_dev)
        for i in range(per_block):
            own = jnp.where(row16 == 0, s_dev[i : i + 1, :], common)
            cbuf[b * per_block + i] = jnp.where(row16 == 13, s_rest[i : i + 1, :], own).astype(BF16)

    own_c = pltpu.make_async_copy(cbuf.at[pos], cr.at[pos], c_recv)
    own_c.start()
    for p, index in peers:
        pltpu.make_async_remote_copy(
            cbuf.at[p], cr.at[pos], c_send, c_recv, device_id={"ctx": index}, device_id_type=MESH
        ).start()

    for rim in rims[1:]:
        rim.wait_recv()
    has_after = jnp.where(me < n_ctx - 1, 1.0, 0.0)
    ahead = [halo_next[i].astype(F32) * has_after for i in range(5)]

    def ahead_feat(i, k):
        mine = [ext[i, 16 + RUNS * (run - 1 - b) + RUNS - 1 : 16 + RUNS * (run - b), :] for b in range(2)]
        if k == 0:
            return tap(i, 0) * ahead[i][0:1] + tap(i, 1) * mine[0] + tap(i, 2) * mine[1]
        return tap(i, 0) * ahead[i][1:2] + tap(i, 1) * ahead[i][0:1] + tap(i, 2) * mine[0]

    ahead_f = [[ahead_feat(i, k) for k in range(2)] for i in range(3)]
    ahead_gf = [ahead[3][k : k + 1] * ahead_f[0][k] for k in range(2)]
    ahead_gq = [ahead[3][k : k + 1] * ahead[4][k : k + 1] for k in range(2)]

    gather = jnp.where(col == RUNS * lax.rem(row, run) + lax.div(row, run), 1.0, 0.0).astype(BF16)
    last = lax.broadcasted_iota(jnp.int32, (RUNS, width), 0) == RUNS - 1

    def finish(i, beyond):
        for k in range(2):
            head = pltpu.roll(gs[i, RUNS * k : RUNS * (k + 1), :], RUNS - 1, axis=0)
            gs[i, rows + RUNS * k : rows + RUNS * (k + 1), :] = jnp.where(last, beyond[k], head)
        made = (
            tap(i, 0) * gs[i, :rows, :]
            + tap(i, 1) * gs[i, RUNS : rows + RUNS, :]
            + tap(i, 2) * gs[i, 2 * RUNS : rows + 2 * RUNS, :]
        )
        gp_ref[i] = jnp.dot(gather, made.astype(BF16), preferred_element_type=F32).astype(BF16)

    gs[0, :rows, :] = gq[...]
    finish(0, ahead_gq)
    for m in range(MODES):
        sloc[m] = coefs[m] * sloc[m]
        coefs[m] = coefs[m] * jnp.exp(lams[m] * (float(run) * (rank - float(RUNS - 1))))
        lams[m] = jnp.exp(-lams[m])

    pltpu.make_async_copy(cr, cr, c_recv).wait()
    flat[...] = cr[...].astype(F32).reshape(group * ROWS, half)

    def item3(k):
        return jnp.concatenate(
            [flat[pl.ds(h * ROWS + k, MODES, stride=2 * ROWS), :] for h in range(2)], axis=1
        )

    scale = 1.0 / math.sqrt(tokens)
    s_dev = item3(0) + item3(13)
    r_tot, d_tot, x_tot = item3(1) + item3(10), item3(2) + item3(11), item3(9) + item3(12)
    root = jnp.sqrt(lam_t)
    gres_ref[...] = scale * root * r_tot
    grate_ref[...] = scale * res_ref[...] * root * (0.5 / rate_ref[...] * r_tot - d_tot * (1.0 / tokens))
    for j in range(3):
        gshort_ref[0, j : j + 1, :] = scale * x_tot[j : j + 1, :]
        for i in (1, 2):
            k = 3 * (i - 1) + j
            gshort_ref[i, j : j + 1, :] = scale * (x_tot[3 + k : 4 + k, :] + total(item3(3 + k)))
    gskip_ref[...] = scale * x_tot[9:10, :]

    for h in range(2):
        lanes = slice(h * half, (h + 1) * half)
        a = [lams[m, :, lanes] for m in range(MODES)]
        p = [sloc[m, :, lanes] + coefs[m, :, lanes] * s_dev[m : m + 1, lanes] for m in range(MODES)]
        for r in range(run - 1, -1, -1):
            at = slice(RUNS * r, RUNS * (r + 1))
            p = [x * d for x, d in zip(p, a)]
            terms = p
            while len(terms) > 1:
                terms = [u + w for u, w in zip(terms[::2], terms[1::2])]
            longs[at, lanes] += terms[0]

    gated = longs[...] + skip * gf[...]
    gs[1, :rows, :] = gated * feat[1]
    gs[2, :rows, :] = gated * feat[0]
    ahead_long = [
        total(coef_t * s_dev),
        total(coef_t * (s_dev - ahead_gf[0]) * jnp.exp(lam_t)),
    ]
    ahead_gated = [(ahead_long[k] + skip * ahead_gf[k]) * has_after for k in range(2)]
    finish(1, [ahead_gated[k] * ahead_f[2][k] for k in range(2)])
    finish(2, [ahead_gated[k] * ahead_f[1][k] for k in range(2)])

    for rim in rims:
        rim.wait_send()
    others = pl.ds(0, group - 1)
    pltpu.make_async_copy(sbuf.at[others], sbuf.at[others], a_send).wait()
    pltpu.make_async_copy(bb.at[pl.ds(0, n_blocks - 1)], bb.at[pl.ds(0, n_blocks - 1)], b_send).wait()
    pltpu.make_async_copy(cbuf.at[others], cbuf.at[others], c_send).wait()


def hand_over(*refs):
    count = (len(refs) - 1) // 2
    sems = refs[-1]
    copies = [
        pltpu.make_async_copy(src, dst, sems.at[i])
        for i, (src, dst) in enumerate(zip(refs[:count], refs[count : 2 * count]))
    ]
    for copy in copies:
        copy.start()
    for copy in copies:
        copy.wait()


def solution(mesh):
    n_ctx = mesh.shape["ctx"]
    n_blocks = n_ctx // 32

    def body(projections, filtered, cotangent, short_taps, residues, pole_rates, skip_gain):
        rows, width = filtered.shape
        half = width // 2
        vmem = pl.BlockSpec(memory_space=pltpu.VMEM)
        full = (rows, width)
        made = (
            jax.ShapeDtypeStruct((3,) + full, BF16),
            jax.ShapeDtypeStruct((3, 3, width), F32),
            jax.ShapeDtypeStruct((MODES, width), F32),
            jax.ShapeDtypeStruct((MODES, width), F32),
            jax.ShapeDtypeStruct((1, width), F32),
        )
        args = (projections, filtered, cotangent, short_taps, residues.T, pole_rates.T, skip_gain.reshape(1, width))
        out = pl.pallas_call(
            functools.partial(kernel, (n_ctx, n_blocks)),
            out_shape=[pltpu.VMEM(x.shape, x.dtype) for x in made],
            in_specs=[pl.BlockSpec(memory_space=pltpu.HBM)] * 7,
            out_specs=[vmem] * 5,
            scratch_shapes=[pltpu.VMEM(x.shape, x.dtype) for x in args]
            + [
                pltpu.VMEM((3, rows + 16, width), F32),
                pltpu.VMEM((2,) + full, F32),
                pltpu.VMEM(full, F32),
                pltpu.VMEM(full, F32),
                pltpu.VMEM(full, F32),
                pltpu.VMEM(full, F32),
                pltpu.VMEM((6,) + full, F32),
                pltpu.VMEM(full, F32),
                pltpu.VMEM((MODES, RUNS, width), F32),
                pltpu.VMEM((MODES, RUNS, width), F32),
                pltpu.VMEM((2 * MODES, RUNS, half), F32),
                pltpu.VMEM((2 * MODES, RUNS, half), F32),
                pltpu.VMEM((MODES, RUNS, width), F32),
                pltpu.VMEM((6, RUNS, width), F32),
                pltpu.VMEM((2 * MODES * ROWS, half), F32),
                pltpu.VMEM((32, ROWS, half), BF16),
                pltpu.VMEM((32, ROWS, half), BF16),
                pltpu.VMEM((32 * ROWS, half), F32),
                pltpu.VMEM((4, ROWS, half), BF16),
                pltpu.VMEM((4, n_blocks, ROWS, half), BF16),
                pltpu.VMEM((4 * n_blocks * ROWS, half), F32),
                pltpu.VMEM((4 * n_blocks, half), F32),
                pltpu.VMEM((32, ROWS, half), BF16),
                pltpu.VMEM((32, ROWS, half), BF16),
                pltpu.VMEM((3, rows + 16, width), F32),
                pltpu.VMEM((8, width), F32),
                pltpu.VMEM((8, width), F32),
                pltpu.VMEM((5, 16, width), BF16),
                pltpu.SemaphoreType.DMA((7,)),
                pltpu.SemaphoreType.DMA((4,)),
                pltpu.SemaphoreType.DMA((4,)),
                pltpu.SemaphoreType.DMA,
                pltpu.SemaphoreType.DMA,
                pltpu.SemaphoreType.DMA,
                pltpu.SemaphoreType.DMA,
                pltpu.SemaphoreType.DMA,
                pltpu.SemaphoreType.DMA,
            ],
            compiler_params=pltpu.CompilerParams(
                collective_id=0, has_side_effects=True, vmem_limit_bytes=40 * 1024 * 1024
            ),
        )(*(pltpu.with_memory_space_constraint(x, pltpu.HBM) for x in args))
        out = pl.pallas_call(
            hand_over,
            out_shape=[pltpu.HBM(x.shape, x.dtype) for x in made],
            in_specs=[vmem] * 5,
            out_specs=[pl.BlockSpec(memory_space=pltpu.HBM)] * 5,
            scratch_shapes=[pltpu.SemaphoreType.DMA((5,))],
        )(*(pltpu.with_memory_space_constraint(x, pltpu.VMEM) for x in out))
        return out[0], out[1], out[2].T, out[3].T, out[4].reshape(width)

    return jax.shard_map(
        body,
        mesh=mesh,
        in_specs=(
            P(None, "ctx", "ch"),
            P("ctx", "ch"),
            P("ctx", "ch"),
            P(None, None, "ch"),
            P("ch", None),
            P("ch", None),
            P("ch"),
        ),
        out_specs=(
            P(None, "ctx", "ch"),
            P(None, None, "ch"),
            P("ch", None),
            P("ch", None),
            P("ch"),
        ),
        check_vma=False,
    )
```

```python
import functools
import math

import jax
import jax.numpy as jnp
from jax import lax
from jax.experimental import pallas as pl
from jax.experimental.pallas import tpu as pltpu
from jax.sharding import PartitionSpec as P

MESH = pl.DeviceIdType.MESH
F32 = jnp.float32
BF16 = jnp.bfloat16

RUNS = 8
MODES = 16
ROWS = 16
EARLY = 12
TOGETHER = 2
ROW_L, ROW_LP, ROW_V, ROW_VP, ROW_W, ROW_R, ROW_D, ROW_X = 0, 1, 2, 3, 4, 10, 11, 12
REST = 3


def up(x, by, size):
    return pltpu.roll(x, size - by, axis=0)


def suffix(state, slope, lam, length, count):
    row = lax.broadcasted_iota(jnp.int32, state.shape, 0)
    by = 1
    while by < count:
        decay = jnp.where(row < count - by, jnp.exp(lam * float(-length * by)), 0.0)
        later, later_slope = up(state, by, count), up(slope, by, count)
        slope = slope + decay * (later_slope + float(length * by) * later)
        state = state + decay * later
        by *= 2
    inside = row < count - 1
    return (
        state,
        slope,
        jnp.where(inside, up(state, 1, count), 0.0),
        jnp.where(inside, up(slope, 1, count), 0.0),
    )


def total(x):
    return jnp.sum(x, axis=0, keepdims=True)


def rest(x):
    return x - x.astype(BF16).astype(F32)


def kernel(
    geometry,
    proj_hbm,
    filt_hbm,
    cot_hbm,
    taps_hbm,
    res_hbm,
    rate_hbm,
    skip_hbm,
    gp_ref,
    gshort_ref,
    gres_ref,
    grate_ref,
    gskip_ref,
    proj_ref,
    filt_ref,
    cot_ref,
    taps_ref,
    res_ref,
    rate_ref,
    skip_ref,
    ext,
    feat,
    gf,
    gv,
    gz,
    gq,
    ys,
    longs,
    lams,
    coefs,
    owner_lam,
    owner_coef,
    sloc,
    crosses,
    sums,
    sbuf,
    rbuf,
    flat,
    bbuf,
    bb,
    flat2,
    si_ref,
    cbuf,
    cr,
    gs,
    rim_rows,
    halo_prev,
    halo_next,
    passed_on,
    in_sem,
    halo_send,
    halo_recv,
    a_send,
    a_recv,
    b_send,
    b_recv,
    c_send,
    c_recv,
):
    n_ctx, n_blocks = geometry
    rows = proj_ref.shape[1]
    width = proj_ref.shape[2]
    half = width // 2
    run = rows // RUNS
    tokens = rows * n_ctx
    per_block = 8
    group = 32
    me = lax.axis_index("ctx")
    y = lax.div(me, per_block * n_blocks)
    zh = lax.rem(lax.div(me, per_block), n_blocks)
    lo = lax.rem(me, per_block)
    pos = y * per_block + lo
    held = (
        (taps_hbm, taps_ref),
        (res_hbm, res_ref),
        (rate_hbm, rate_ref),
        (skip_hbm, skip_ref),
        (proj_hbm, proj_ref),
        (cot_hbm, cot_ref),
        (filt_hbm, filt_ref),
    )
    loads = [pltpu.make_async_copy(src, dst, in_sem.at[i]) for i, (src, dst) in enumerate(held)]
    for load in loads:
        load.start()

    ys_of = [lax.rem(y + d, 4) for d in range(4)]
    los_of = [lo] + [lax.rem(lo + d, per_block) for d in range(1, per_block)]
    bases = [v * (per_block * n_blocks) + zh * per_block for v in ys_of]
    peers = [
        (ys_of[d] * per_block + los_of[k], bases[d] + los_of[k])
        for d in (2, 1, 3, 0)
        for k in (2, 6, 3, 5, 4, 7, 1, 0)
        if (d, k) != (0, 0)
    ]
    cousins = [y * (per_block * n_blocks) + lax.rem(zh + j, n_blocks) * per_block + lo for j in (2, 1, 3)]
    before, after = lax.rem(me + n_ctx - 1, n_ctx), lax.rem(me + 1, n_ctx)
    barrier = pltpu.get_barrier_semaphore()
    for d in [index for _, index in peers] + cousins[1:] + [before, after]:
        pl.semaphore_signal(barrier, inc=1, device_id={"ctx": d}, device_id_type=MESH)

    row = lax.broadcasted_iota(jnp.int32, (rows, rows), 0)
    col = lax.broadcasted_iota(jnp.int32, (rows, rows), 1)
    spread = jnp.where(col == run * (row % RUNS) + row // RUNS, 1.0, 0.0).astype(BF16)
    for load in loads[:4]:
        load.wait()

    lam_t = rate_ref[...] * (1.0 / tokens)
    coef_t = res_ref[...] * jnp.sqrt(lam_t)
    for m in range(MODES):
        lam_m = jnp.broadcast_to(lam_t[m : m + 1, :], (RUNS, width))
        coef_m = jnp.broadcast_to(coef_t[m : m + 1, :], (RUNS, width))
        lams[m] = lam_m
        coefs[m] = coef_m
        for h in range(2):
            owner_lam[2 * m + h] = lam_m[:, h * half : (h + 1) * half]
            owner_coef[2 * m + h] = coef_m[:, h * half : (h + 1) * half]

    def placed(x):
        return jnp.dot(spread, x, preferred_element_type=F32)

    first = lax.broadcasted_iota(jnp.int32, (RUNS, width), 0) == 0
    first_two = lax.broadcasted_iota(jnp.int32, (2 * RUNS, width), 0) % RUNS == 0
    for load in loads[4:]:
        load.wait()
    for i in range(3):
        ext[i, 16:, :] = placed(proj_ref[i])
        for back in (2, 1):
            tail = pltpu.roll(ext[i, 16 + RUNS * (run - back) : 16 + RUNS * (run - back + 1), :], 1, axis=0)
            ext[i, 16 - 8 * back : 24 - 8 * back, :] = jnp.where(first, 0.0, tail)

    def tap(i, j):
        return taps_ref[i, j : j + 1, :]

    def shifted(i, j):
        return ext[i, 16 - 8 * j : 16 - 8 * j + rows, :]

    def masked(x):
        return jnp.concatenate([jnp.where(first_two, 0.0, x[: 2 * RUNS]), x[2 * RUNS :]], axis=0)

    cot = placed(cot_ref[...])
    gq[...] = cot * placed(filt_ref[...])
    for i in range(3):
        made = tap(i, 0) * shifted(i, 0) + tap(i, 1) * shifted(i, 1) + tap(i, 2) * shifted(i, 2)
        if i == 0:
            gf[...] = masked(cot * made)
        else:
            feat[i - 1] = made
    gv[...] = masked(feat[0] * feat[1])
    step_of = lax.broadcasted_iota(jnp.int32, (rows, width), 0) // RUNS
    to_end = (run - step_of).astype(F32)
    gz[...] = to_end * gv[...]
    for j in range(3):
        ys[j] = masked(feat[1] * shifted(1, j))
        ys[3 + j] = masked(feat[0] * shifted(2, j))

    longs[...] = jnp.zeros_like(longs)
    crosses[...] = jnp.zeros_like(crosses)

    rank = lax.broadcasted_iota(jnp.int32, (RUNS, width), 0).astype(F32)

    def some_modes(at, _):
        for h in range(2):
            some_modes_of_half(at, h)
        return 0

    def some_modes_of_half(at, h):
        lanes = slice(h * half, (h + 1) * half)
        modes = [at * TOGETHER + i for i in range(TOGETHER)]
        lam = [lams[m, :, lanes] for m in modes]
        coef = [coefs[m, :, lanes] for m in modes]
        a = [jnp.exp(-x) for x in lam]
        zero = jnp.zeros((RUNS, half), F32)
        state, slope, r_sum, d_sum, vp = ([zero] * TOGETHER for _ in range(5))
        w = [[zero] * 6 for _ in modes]
        for step in range(run):
            low = slice(RUNS * (run - 1 - step), RUNS * (run - step))
            high = slice(RUNS * step, RUNS * (step + 1))
            gf_low, gv_low, gz_high = gf[low, lanes], gv[low, lanes], gz[high, lanes]
            ys_high = [ys[k, high, lanes] for k in range(6)]
            part = None
            for i in range(TOGETHER):
                slope[i] = a[i] * (slope[i] + state[i])
                state[i] = a[i] * state[i] + gf_low
                given = coef[i] * state[i]
                part = given if part is None else part + given
                r_sum[i] = r_sum[i] + gv_low * state[i]
                d_sum[i] = d_sum[i] + gv_low * slope[i]
                vp[i] = a[i] * (vp[i] + gz_high)
                for k in range(6):
                    w[i][k] = a[i] * (w[i][k] + ys_high[k])
            longs[low, lanes] += part
        rank_h = rank[:, lanes]
        for i, m in enumerate(modes):
            v = sum(taps_ref[1, j : j + 1, lanes] * w[i][j] for j in range(3))
            inner, inner_slope, s_loc, sp_loc = suffix(state[i], slope[i], lam[i], run, RUNS)
            sloc[m, :, lanes] = s_loc
            weight = jnp.exp(lam[i] * (float(run) * (rank_h - float(RUNS - 1))))

            def put(k, value):
                sums[pl.ds((h * ROWS + k) * MODES + m, 1), :] = value

            put(ROW_L, inner[0:1, :])
            put(ROW_LP, inner_slope[0:1, :])
            put(ROW_V, total(weight * v))
            put(ROW_VP, total(weight * (vp[i] + float(run) * (float(RUNS - 1) - rank_h) * v)))
            state_in = coef[i] * s_loc
            for k in range(6):
                put(ROW_W + k, total(weight * w[i][k]))
                crosses[k, :, lanes] += state_in * w[i][k]
            put(ROW_R, total(r_sum[i] + v * s_loc))
            put(ROW_D, total(d_sum[i] + vp[i] * s_loc + v * sp_loc))

    for i in range(3):
        for b in range(2):
            at = 16 + RUNS * (run - 1 - b) + RUNS - 1
            rim_rows[2 * i + 1 - b : 2 * i + 2 - b, :] = ext[i, at : at + 1, :]
    rim_rows[6:8, :] = jnp.zeros((2, width), F32)

    lax.fori_loop(0, EARLY // TOGETHER, some_modes, 0)

    pl.semaphore_wait(barrier, group - 1 + 2 + 2)
    for d in cousins[1:]:
        pl.semaphore_signal(passed_on, inc=1, device_id={"ctx": d}, device_id_type=MESH)
    first_rows = pl.ds(0, 16)
    rims = (
        (rim_rows, halo_prev, after),
        (proj_ref.at[:, first_rows], halo_next.at[pl.ds(0, 3)], before),
        (cot_ref.at[first_rows], halo_next.at[3], before),
        (filt_ref.at[first_rows], halo_next.at[4], before),
    )
    rims = [
        pltpu.make_async_remote_copy(
            src, dst, halo_send.at[i], halo_recv.at[i], device_id={"ctx": to}, device_id_type=MESH
        )
        for i, (src, dst, to) in enumerate(rims)
    ]
    for rim in rims:
        rim.start()
    lax.fori_loop(EARLY // TOGETHER, MODES // TOGETHER, some_modes, 0)

    skip = skip_ref[...]
    inner_gated = longs[...] + skip * gf[...]
    own_query = masked(gq[...])
    plain = [total(own_query * shifted(0, j)) for j in range(3)]
    plain += [total(inner_gated * ys[k]) + total(crosses[k]) for k in range(6)]
    plain.append(total(gf[...] * gv[...]))

    def each_mode(k):
        return jnp.concatenate(
            [sums[(h * ROWS + k) * MODES : (h * ROWS + k + 1) * MODES, :] for h in range(2)], axis=1
        )

    def keep(k, value):
        for h in range(2):
            sums[(h * ROWS + k) * MODES : (h * ROWS + k + 1) * MODES, :] = value[:, h * half : (h + 1) * half]

    a_t = jnp.exp(-lam_t)
    back_two = jnp.exp(2.0 * lam_t)
    two, two_slope = each_mode(ROW_L), each_mode(ROW_LP)
    two, two_slope = back_two * two, back_two * (two_slope - 2.0 * two)
    slope_1 = a_t * (two_slope + two)
    moved = a_t * two
    decays = [jnp.exp(lam_t * -float(rows)), jnp.exp(lam_t * -float(rows - 1))]
    direct_sum, moved_sum = total(coef_t), total(coef_t * a_t)
    cot_two = [cot[0:1], cot[RUNS : RUNS + 1]]

    rims[0].wait_recv()
    has_before = jnp.where(me > 0, 1.0, 0.0)
    before_rows = [halo_prev[2 * i : 2 * i + 2, :] * has_before for i in range(3)]
    x = [
        {-2: before_rows[i][0:1], -1: before_rows[i][1:2], 0: ext[i, 16:17, :], 1: ext[i, 24:25, :]}
        for i in range(3)
    ]
    f = [[tap(i, 0) * x[i][t] + tap(i, 1) * x[i][t - 1] + tap(i, 2) * x[i][t - 2] for t in range(2)] for i in range(3)]
    gf_two = [cot_two[t] * f[0][t] for t in range(2)]
    gv_two = [f[1][t] * f[2][t] for t in range(2)]
    ys_two = [[f[2][t] * x[1][t - j] for j in range(3)] + [f[1][t] * x[2][t - j] for j in range(3)] for t in range(2)]

    state_1 = gf_two[1] + moved
    slope_0 = a_t * (slope_1 + state_1)
    state_0 = gf_two[0] + a_t * state_1
    parts = [decays[t] * gv_two[t] for t in range(2)]
    keep(ROW_L, state_0)
    keep(ROW_LP, slope_0)
    keep(ROW_V, each_mode(ROW_V) + parts[0] + parts[1])
    keep(ROW_VP, each_mode(ROW_VP) + float(rows) * parts[0] + float(rows - 1) * parts[1])
    for k in range(6):
        keep(ROW_W + k, each_mode(ROW_W + k) + decays[0] * ys_two[0][k] + decays[1] * ys_two[1][k])
    r_all = each_mode(ROW_R) + gv_two[1] * state_1 + gv_two[0] * state_0
    d_all = each_mode(ROW_D) + gv_two[1] * slope_1 + gv_two[0] * slope_0
    keep(ROW_R, r_all)
    keep(ROW_R + REST, rest(r_all))
    keep(ROW_D, d_all)
    keep(ROW_D + REST, rest(d_all))
    gated_two = [total(coef_t * state_0) + skip * gf_two[0], total(coef_t * state_1) + skip * gf_two[1]]
    for t in range(2):
        for j in range(3):
            plain[j] = plain[j] + gq[RUNS * t : RUNS * t + 1, :] * x[0][t - j]
        for k in range(6):
            plain[3 + k] = plain[3 + k] + gated_two[t] * ys_two[t][k]
        plain[9] = plain[9] + gf_two[t] * gv_two[t]
    plain = jnp.concatenate(plain + [jnp.zeros((MODES - len(plain), width), F32)], axis=0)
    keep(ROW_X, plain)
    keep(ROW_X + REST, rest(plain))
    for m in range(MODES):
        for h in range(2):
            sbuf[2 * m + h] = sums[pl.ds(h * ROWS * MODES + m, ROWS, stride=MODES), :].astype(BF16)

    own_a = pltpu.make_async_copy(sbuf.at[pos], rbuf.at[pos], a_recv)
    own_a.start()
    for p, index in peers:
        pltpu.make_async_remote_copy(
            sbuf.at[p], rbuf.at[pos], a_send, a_recv, device_id={"ctx": index}, device_id_type=MESH
        ).start()

    direct = [direct_sum * gf_two[0] + moved_sum * gf_two[1], direct_sum * gf_two[1]]
    for t in range(2):
        at = slice(RUNS * t, RUNS * t + 1)
        gf[at, :] = gf_two[t]
        longs[at, :] += direct[t]
        for i in (1, 2):
            feat[i - 1, at, :] = f[i][t]

    pltpu.make_async_copy(rbuf, rbuf, a_recv).wait()

    lam_o = owner_lam[pos]
    coef_o = owner_coef[pos]
    flat[...] = rbuf[...].astype(F32).reshape(group * ROWS, half)
    rank8 = lax.broadcasted_iota(jnp.int32, (per_block, half), 0).astype(F32)
    weight = jnp.exp(lam_o * (float(rows) * (rank8 - float(per_block - 1))))
    inside = []
    acc_r = acc_d = acc_x = jnp.zeros((per_block, half), F32)
    acc_w = [acc_r] * 6
    for b in range(4):
        base = b * per_block * ROWS

        def item(k):
            return flat[pl.ds(base + k, per_block, stride=ROWS), :]

        state, slope, v, vp = item(ROW_L), item(ROW_LP), item(ROW_V), item(ROW_VP)
        inner, inner_slope, s_int, sp_int = suffix(state, slope, lam_o, rows, per_block)
        inside.append(s_int)
        parts = [
            inner[0:1, :],
            inner_slope[0:1, :],
            total(weight * v),
            total(weight * (vp + float(rows) * (float(per_block - 1) - rank8) * v)),
        ]
        acc_r = acc_r + (item(ROW_R) + item(ROW_R + REST)) + v * s_int
        acc_d = acc_d + (item(ROW_D) + item(ROW_D + REST)) + vp * s_int + v * sp_int
        acc_x = acc_x + (item(ROW_X) + item(ROW_X + REST))
        for k in range(6):
            w_k = item(ROW_W + k)
            parts.append(total(weight * w_k))
            acc_w[k] = acc_w[k] + w_k * s_int
        for k, part in enumerate(parts):
            flat2[b * ROWS + k : b * ROWS + k + 1, :] = part
        flat2[b * ROWS + 10 : b * ROWS + ROWS, :] = jnp.zeros((ROWS - 10, half), F32)
    for k in range(6):
        value = total(acc_w[k])
        flat2[10 + k : 11 + k, :] = value
        flat2[2 * ROWS + 10 + k : 2 * ROWS + 11 + k, :] = rest(value)
    for k, acc in enumerate((acc_r, acc_d, acc_x)):
        value = total(acc)
        flat2[ROWS + 10 + k : ROWS + 11 + k, :] = value
        flat2[ROWS + 10 + REST + k : ROWS + 11 + REST + k, :] = rest(value)
    bbuf[...] = flat2[: 4 * ROWS, :].astype(BF16).reshape(4, ROWS, half)

    own_b = pltpu.make_async_copy(bbuf, bb.at[:, zh], b_recv)
    own_b.start()
    pl.semaphore_wait(passed_on, 2)
    for index in cousins:
        pltpu.make_async_remote_copy(
            bbuf, bb.at[:, zh], b_send, b_recv, device_id={"ctx": index}, device_id_type=MESH
        ).start()
    pltpu.make_async_copy(bb, bb, b_recv).wait()

    n_int = 4 * n_blocks
    flat2[...] = bb[...].astype(F32).reshape(n_int * ROWS, half)

    def item2(k):
        return flat2[pl.ds(k, n_int, stride=ROWS), :]

    lam2 = jnp.concatenate([lam_o, lam_o], axis=0)
    v, vp = item2(ROW_V), item2(ROW_VP)
    _, _, s_all, sp_all = suffix(item2(ROW_L), item2(ROW_LP), lam2, rows * per_block, n_int)
    si_ref[...] = s_all
    parts = [total(v * s_all), total(vp * s_all + v * sp_all)]
    interval = lax.broadcasted_iota(jnp.int32, (n_int, half), 0) // n_blocks
    in_1, in_0_2 = interval == 1, (interval == 0) | (interval == 2)

    def sum_1(k):
        return total(jnp.where(in_1, item2(10 + k) + item2(10 + REST + k), 0.0))

    for k in range(2):
        parts[k] = parts[k] + sum_1(k)
    for k in range(6):
        parts.append(coef_o[0:1, :] * total(item2(ROW_W + k) * s_all + jnp.where(in_0_2, item2(10 + k), 0.0)))
    parts.append(sum_1(2))
    parts += [rest(parts[0]), rest(parts[1]), rest(parts[8])]
    row16 = lax.broadcasted_iota(jnp.int32, (ROWS, half), 0)
    common = jnp.zeros((ROWS, half), F32)
    for k, part in enumerate(parts):
        common = jnp.where(row16 == 1 + k, part, common)
    for b in range(4):
        s_dev = inside[b] + weight * si_ref[pl.ds(b * n_blocks + zh, 1), :]
        s_rest = rest(s_dev)
        for i in range(per_block):
            own = jnp.where(row16 == 0, s_dev[i : i + 1, :], common)
            cbuf[b * per_block + i] = jnp.where(row16 == 13, s_rest[i : i + 1, :], own).astype(BF16)

    own_c = pltpu.make_async_copy(cbuf.at[pos], cr.at[pos], c_recv)
    own_c.start()
    for p, index in peers:
        pltpu.make_async_remote_copy(
            cbuf.at[p], cr.at[pos], c_send, c_recv, device_id={"ctx": index}, device_id_type=MESH
        ).start()

    for rim in rims[1:]:
        rim.wait_recv()
    has_after = jnp.where(me < n_ctx - 1, 1.0, 0.0)
    ahead = [halo_next[i].astype(F32) * has_after for i in range(5)]

    def ahead_feat(i, k):
        mine = [ext[i, 16 + RUNS * (run - 1 - b) + RUNS - 1 : 16 + RUNS * (run - b), :] for b in range(2)]
        if k == 0:
            return tap(i, 0) * ahead[i][0:1] + tap(i, 1) * mine[0] + tap(i, 2) * mine[1]
        return tap(i, 0) * ahead[i][1:2] + tap(i, 1) * ahead[i][0:1] + tap(i, 2) * mine[0]

    ahead_f = [[ahead_feat(i, k) for k in range(2)] for i in range(3)]
    ahead_gf = [ahead[3][k : k + 1] * ahead_f[0][k] for k in range(2)]
    ahead_gq = [ahead[3][k : k + 1] * ahead[4][k : k + 1] for k in range(2)]

    gather = jnp.where(col == RUNS * lax.rem(row, run) + lax.div(row, run), 1.0, 0.0).astype(BF16)
    last = lax.broadcasted_iota(jnp.int32, (RUNS, width), 0) == RUNS - 1

    def finish(i, beyond):
        for k in range(2):
            head = pltpu.roll(gs[i, RUNS * k : RUNS * (k + 1), :], RUNS - 1, axis=0)
            gs[i, rows + RUNS * k : rows + RUNS * (k + 1), :] = jnp.where(last, beyond[k], head)
        made = (
            tap(i, 0) * gs[i, :rows, :]
            + tap(i, 1) * gs[i, RUNS : rows + RUNS, :]
            + tap(i, 2) * gs[i, 2 * RUNS : rows + 2 * RUNS, :]
        )
        gp_ref[i] = jnp.dot(gather, made.astype(BF16), preferred_element_type=F32).astype(BF16)

    gs[0, :rows, :] = gq[...]
    finish(0, ahead_gq)
    for m in range(MODES):
        sloc[m] = coefs[m] * sloc[m]
        coefs[m] = coefs[m] * jnp.exp(lams[m] * (float(run) * (rank - float(RUNS - 1))))
        lams[m] = jnp.exp(-lams[m])

    pltpu.make_async_copy(cr, cr, c_recv).wait()
    flat[...] = cr[...].astype(F32).reshape(group * ROWS, half)

    def item3(k):
        return jnp.concatenate(
            [flat[pl.ds(h * ROWS + k, MODES, stride=2 * ROWS), :] for h in range(2)], axis=1
        )

    scale = 1.0 / math.sqrt(tokens)
    s_dev = item3(0) + item3(13)
    r_tot, d_tot, x_tot = item3(1) + item3(10), item3(2) + item3(11), item3(9) + item3(12)
    root = jnp.sqrt(lam_t)
    gres_ref[...] = scale * root * r_tot
    grate_ref[...] = scale * res_ref[...] * root * (0.5 / rate_ref[...] * r_tot - d_tot * (1.0 / tokens))
    for j in range(3):
        gshort_ref[0, j : j + 1, :] = scale * x_tot[j : j + 1, :]
        for i in (1, 2):
            k = 3 * (i - 1) + j
            gshort_ref[i, j : j + 1, :] = scale * (x_tot[3 + k : 4 + k, :] + total(item3(3 + k)))
    gskip_ref[...] = scale * x_tot[9:10, :]

    for h in range(2):
        lanes = slice(h * half, (h + 1) * half)
        a = [lams[m, :, lanes] for m in range(MODES)]
        p = [sloc[m, :, lanes] + coefs[m, :, lanes] * s_dev[m : m + 1, lanes] for m in range(MODES)]
        for r in range(run - 1, -1, -1):
            at = slice(RUNS * r, RUNS * (r + 1))
            p = [x * d for x, d in zip(p, a)]
            terms = p
            while len(terms) > 1:
                terms = [u + w for u, w in zip(terms[::2], terms[1::2])]
            longs[at, lanes] += terms[0]

    gated = longs[...] + skip * gf[...]
    gs[1, :rows, :] = gated * feat[1]
    gs[2, :rows, :] = gated * feat[0]
    ahead_long = [
        total(coef_t * s_dev),
        total(coef_t * (s_dev - ahead_gf[0]) * jnp.exp(lam_t)),
    ]
    ahead_gated = [(ahead_long[k] + skip * ahead_gf[k]) * has_after for k in range(2)]
    finish(1, [ahead_gated[k] * ahead_f[2][k] for k in range(2)])
    finish(2, [ahead_gated[k] * ahead_f[1][k] for k in range(2)])

    for rim in rims:
        rim.wait_send()
    others = pl.ds(0, group - 1)
    pltpu.make_async_copy(sbuf.at[others], sbuf.at[others], a_send).wait()
    pltpu.make_async_copy(bb.at[pl.ds(0, n_blocks - 1)], bb.at[pl.ds(0, n_blocks - 1)], b_send).wait()
    pltpu.make_async_copy(cbuf.at[others], cbuf.at[others], c_send).wait()


def hand_over(*refs):
    count = (len(refs) - 1) // 2
    sems = refs[-1]
    copies = [
        pltpu.make_async_copy(src, dst, sems.at[i])
        for i, (src, dst) in enumerate(zip(refs[:count], refs[count : 2 * count]))
    ]
    for copy in copies:
        copy.start()
    for copy in copies:
        copy.wait()


def solution(mesh):
    n_ctx = mesh.shape["ctx"]
    n_blocks = n_ctx // 32

    def body(projections, filtered, cotangent, short_taps, residues, pole_rates, skip_gain):
        rows, width = filtered.shape
        half = width // 2
        vmem = pl.BlockSpec(memory_space=pltpu.VMEM)
        full = (rows, width)
        made = (
            jax.ShapeDtypeStruct((3,) + full, BF16),
            jax.ShapeDtypeStruct((3, 3, width), F32),
            jax.ShapeDtypeStruct((MODES, width), F32),
            jax.ShapeDtypeStruct((MODES, width), F32),
            jax.ShapeDtypeStruct((1, width), F32),
        )
        args = (projections, filtered, cotangent, short_taps, residues.T, pole_rates.T, skip_gain.reshape(1, width))
        out = pl.pallas_call(
            functools.partial(kernel, (n_ctx, n_blocks)),
            out_shape=[pltpu.VMEM(x.shape, x.dtype) for x in made],
            in_specs=[pl.BlockSpec(memory_space=pltpu.HBM)] * 7,
            out_specs=[vmem] * 5,
            scratch_shapes=[pltpu.VMEM(x.shape, x.dtype) for x in args]
            + [
                pltpu.VMEM((3, rows + 16, width), F32),
                pltpu.VMEM((2,) + full, F32),
                pltpu.VMEM(full, F32),
                pltpu.VMEM(full, F32),
                pltpu.VMEM(full, F32),
                pltpu.VMEM(full, F32),
                pltpu.VMEM((6,) + full, F32),
                pltpu.VMEM(full, F32),
                pltpu.VMEM((MODES, RUNS, width), F32),
                pltpu.VMEM((MODES, RUNS, width), F32),
                pltpu.VMEM((2 * MODES, RUNS, half), F32),
                pltpu.VMEM((2 * MODES, RUNS, half), F32),
                pltpu.VMEM((MODES, RUNS, width), F32),
                pltpu.VMEM((6, RUNS, width), F32),
                pltpu.VMEM((2 * MODES * ROWS, half), F32),
                pltpu.VMEM((32, ROWS, half), BF16),
                pltpu.VMEM((32, ROWS, half), BF16),
                pltpu.VMEM((32 * ROWS, half), F32),
                pltpu.VMEM((4, ROWS, half), BF16),
                pltpu.VMEM((4, n_blocks, ROWS, half), BF16),
                pltpu.VMEM((4 * n_blocks * ROWS, half), F32),
                pltpu.VMEM((4 * n_blocks, half), F32),
                pltpu.VMEM((32, ROWS, half), BF16),
                pltpu.VMEM((32, ROWS, half), BF16),
                pltpu.VMEM((3, rows + 16, width), F32),
                pltpu.VMEM((8, width), F32),
                pltpu.VMEM((8, width), F32),
                pltpu.VMEM((5, 16, width), BF16),
                pltpu.SemaphoreType.REGULAR,
                pltpu.SemaphoreType.DMA((7,)),
                pltpu.SemaphoreType.DMA((4,)),
                pltpu.SemaphoreType.DMA((4,)),
                pltpu.SemaphoreType.DMA,
                pltpu.SemaphoreType.DMA,
                pltpu.SemaphoreType.DMA,
                pltpu.SemaphoreType.DMA,
                pltpu.SemaphoreType.DMA,
                pltpu.SemaphoreType.DMA,
            ],
            compiler_params=pltpu.CompilerParams(
                collective_id=0, has_side_effects=True, vmem_limit_bytes=40 * 1024 * 1024
            ),
        )(*(pltpu.with_memory_space_constraint(x, pltpu.HBM) for x in args))
        out = pl.pallas_call(
            hand_over,
            out_shape=[pltpu.HBM(x.shape, x.dtype) for x in made],
            in_specs=[vmem] * 5,
            out_specs=[pl.BlockSpec(memory_space=pltpu.HBM)] * 5,
            scratch_shapes=[pltpu.SemaphoreType.DMA((5,))],
        )(*(pltpu.with_memory_space_constraint(x, pltpu.VMEM) for x in out))
        return out[0], out[1], out[2].T, out[3].T, out[4].reshape(width)

    return jax.shard_map(
        body,
        mesh=mesh,
        in_specs=(
            P(None, "ctx", "ch"),
            P("ctx", "ch"),
            P("ctx", "ch"),
            P(None, None, "ch"),
            P("ch", None),
            P("ch", None),
            P("ch"),
        ),
        out_specs=(
            P(None, "ctx", "ch"),
            P(None, None, "ch"),
            P("ch", None),
            P("ch", None),
            P("ch"),
        ),
        check_vma=False,
    )
```

```python
import functools
import math

import jax
import jax.numpy as jnp
from jax import lax
from jax.experimental import pallas as pl
from jax.experimental.pallas import tpu as pltpu
from jax.sharding import PartitionSpec as P

MESH = pl.DeviceIdType.MESH
F32 = jnp.float32
BF16 = jnp.bfloat16

RUNS = 8
MODES = 16
ROWS = 16
EARLY = 12
TOGETHER = 2
ROW_L, ROW_LP, ROW_V, ROW_VP, ROW_W, ROW_R, ROW_D, ROW_X = 0, 1, 2, 3, 4, 10, 11, 12
REST = 3


def up(x, by, size):
    return pltpu.roll(x, size - by, axis=0)


def suffix(state, slope, lam, length, count):
    row = lax.broadcasted_iota(jnp.int32, state.shape, 0)
    by = 1
    while by < count:
        decay = jnp.where(row < count - by, jnp.exp(lam * float(-length * by)), 0.0)
        later, later_slope = up(state, by, count), up(slope, by, count)
        slope = slope + decay * (later_slope + float(length * by) * later)
        state = state + decay * later
        by *= 2
    inside = row < count - 1
    return (
        state,
        slope,
        jnp.where(inside, up(state, 1, count), 0.0),
        jnp.where(inside, up(slope, 1, count), 0.0),
    )


def total(x):
    return jnp.sum(x, axis=0, keepdims=True)


def rest(x):
    return x - x.astype(BF16).astype(F32)


def kernel(
    geometry,
    proj_hbm,
    filt_hbm,
    cot_hbm,
    taps_hbm,
    res_hbm,
    rate_hbm,
    skip_hbm,
    gp_ref,
    gshort_ref,
    gres_ref,
    grate_ref,
    gskip_ref,
    proj_ref,
    filt_ref,
    cot_ref,
    taps_ref,
    res_ref,
    rate_ref,
    skip_ref,
    ext,
    feat,
    gf,
    gv,
    gz,
    gq,
    ys,
    longs,
    lams,
    coefs,
    owner_lam,
    owner_coef,
    sloc,
    crosses,
    sums,
    sbuf,
    rbuf,
    flat,
    bbuf,
    bb,
    flat2,
    si_ref,
    cbuf,
    cr,
    gs,
    rim_rows,
    halo_prev,
    halo_next,
    passed_on,
    in_sem,
    halo_send,
    halo_recv,
    a_send,
    a_recv,
    b_send,
    b_recv,
    c_send,
    c_recv,
):
    n_ctx, n_blocks = geometry
    rows = proj_ref.shape[1]
    width = proj_ref.shape[2]
    half = width // 2
    run = rows // RUNS
    tokens = rows * n_ctx
    per_block = 8
    group = 32
    me = lax.axis_index("ctx")
    y = lax.div(me, per_block * n_blocks)
    zh = lax.rem(lax.div(me, per_block), n_blocks)
    lo = lax.rem(me, per_block)
    pos = y * per_block + lo
    held = (
        (taps_hbm, taps_ref),
        (res_hbm, res_ref),
        (rate_hbm, rate_ref),
        (skip_hbm, skip_ref),
        (proj_hbm, proj_ref),
        (cot_hbm, cot_ref),
        (filt_hbm, filt_ref),
    )
    loads = [pltpu.make_async_copy(src, dst, in_sem.at[i]) for i, (src, dst) in enumerate(held)]
    for load in loads:
        load.start()

    ys_of = [lax.rem(y + d, 4) for d in range(4)]
    bases = [v * (per_block * n_blocks) + zh * per_block for v in ys_of]
    zl, core = lax.div(lo, 2), lax.rem(lo, 2)
    zls_of = (zl, zl + 1 - 2 * lax.rem(zl, 2), lax.rem(zl + 2, 4), 3 - zl)
    los_of = [[2 * v + core, 2 * v + 1 - core] for v in zls_of]
    steps = ((2, 3), (2, 2), (1, 3), (3, 3), (1, 2), (3, 2), (2, 1), (0, 3), (2, 0), (0, 2), (1, 1), (3, 1), (1, 0), (3, 0), (0, 1), (0, 0))
    peers = [
        (ys_of[d] * per_block + los_of[k][c], bases[d] + los_of[k][c])
        for d, k in steps
        for c in (1, 0)
        if (d, k, c) != (0, 0, 0)
    ]
    cousins = [y * (per_block * n_blocks) + lax.rem(zh + j, n_blocks) * per_block + lo for j in (2, 1, 3)]
    before, after = lax.rem(me + n_ctx - 1, n_ctx), lax.rem(me + 1, n_ctx)
    barrier = pltpu.get_barrier_semaphore()
    for d in [index for _, index in peers] + cousins[1:] + [before, after]:
        pl.semaphore_signal(barrier, inc=1, device_id={"ctx": d}, device_id_type=MESH)

    row = lax.broadcasted_iota(jnp.int32, (rows, rows), 0)
    col = lax.broadcasted_iota(jnp.int32, (rows, rows), 1)
    spread = jnp.where(col == run * (row % RUNS) + row // RUNS, 1.0, 0.0).astype(BF16)
    for load in loads[:4]:
        load.wait()

    lam_t = rate_ref[...] * (1.0 / tokens)
    coef_t = res_ref[...] * jnp.sqrt(lam_t)
    for m in range(MODES):
        lam_m = jnp.broadcast_to(lam_t[m : m + 1, :], (RUNS, width))
        coef_m = jnp.broadcast_to(coef_t[m : m + 1, :], (RUNS, width))
        lams[m] = lam_m
        coefs[m] = coef_m
        for h in range(2):
            owner_lam[2 * m + h] = lam_m[:, h * half : (h + 1) * half]
            owner_coef[2 * m + h] = coef_m[:, h * half : (h + 1) * half]

    def placed(x):
        return jnp.dot(spread, x, preferred_element_type=F32)

    first = lax.broadcasted_iota(jnp.int32, (RUNS, width), 0) == 0
    first_two = lax.broadcasted_iota(jnp.int32, (2 * RUNS, width), 0) % RUNS == 0
    for load in loads[4:]:
        load.wait()
    for i in range(3):
        ext[i, 16:, :] = placed(proj_ref[i])
        for back in (2, 1):
            tail = pltpu.roll(ext[i, 16 + RUNS * (run - back) : 16 + RUNS * (run - back + 1), :], 1, axis=0)
            ext[i, 16 - 8 * back : 24 - 8 * back, :] = jnp.where(first, 0.0, tail)

    def tap(i, j):
        return taps_ref[i, j : j + 1, :]

    def shifted(i, j):
        return ext[i, 16 - 8 * j : 16 - 8 * j + rows, :]

    def masked(x):
        return jnp.concatenate([jnp.where(first_two, 0.0, x[: 2 * RUNS]), x[2 * RUNS :]], axis=0)

    cot = placed(cot_ref[...])
    gq[...] = cot * placed(filt_ref[...])
    for i in range(3):
        made = tap(i, 0) * shifted(i, 0) + tap(i, 1) * shifted(i, 1) + tap(i, 2) * shifted(i, 2)
        if i == 0:
            gf[...] = masked(cot * made)
        else:
            feat[i - 1] = made
    gv[...] = masked(feat[0] * feat[1])
    step_of = lax.broadcasted_iota(jnp.int32, (rows, width), 0) // RUNS
    to_end = (run - step_of).astype(F32)
    gz[...] = to_end * gv[...]
    for j in range(3):
        ys[j] = masked(feat[1] * shifted(1, j))
        ys[3 + j] = masked(feat[0] * shifted(2, j))

    longs[...] = jnp.zeros_like(longs)
    crosses[...] = jnp.zeros_like(crosses)

    rank = lax.broadcasted_iota(jnp.int32, (RUNS, width), 0).astype(F32)

    def some_modes(at, _):
        for h in range(2):
            some_modes_of_half(at, h)
        return 0

    def some_modes_of_half(at, h):
        lanes = slice(h * half, (h + 1) * half)
        modes = [at * TOGETHER + i for i in range(TOGETHER)]
        lam = [lams[m, :, lanes] for m in modes]
        coef = [coefs[m, :, lanes] for m in modes]
        a = [jnp.exp(-x) for x in lam]
        zero = jnp.zeros((RUNS, half), F32)
        state, slope, r_sum, d_sum, vp = ([zero] * TOGETHER for _ in range(5))
        w = [[zero] * 6 for _ in modes]
        for step in range(run):
            low = slice(RUNS * (run - 1 - step), RUNS * (run - step))
            high = slice(RUNS * step, RUNS * (step + 1))
            gf_low, gv_low, gz_high = gf[low, lanes], gv[low, lanes], gz[high, lanes]
            ys_high = [ys[k, high, lanes] for k in range(6)]
            part = None
            for i in range(TOGETHER):
                slope[i] = a[i] * (slope[i] + state[i])
                state[i] = a[i] * state[i] + gf_low
                given = coef[i] * state[i]
                part = given if part is None else part + given
                r_sum[i] = r_sum[i] + gv_low * state[i]
                d_sum[i] = d_sum[i] + gv_low * slope[i]
                vp[i] = a[i] * (vp[i] + gz_high)
                for k in range(6):
                    w[i][k] = a[i] * (w[i][k] + ys_high[k])
            longs[low, lanes] += part
        rank_h = rank[:, lanes]
        for i, m in enumerate(modes):
            v = sum(taps_ref[1, j : j + 1, lanes] * w[i][j] for j in range(3))
            inner, inner_slope, s_loc, sp_loc = suffix(state[i], slope[i], lam[i], run, RUNS)
            sloc[m, :, lanes] = s_loc
            weight = jnp.exp(lam[i] * (float(run) * (rank_h - float(RUNS - 1))))

            def put(k, value):
                sums[pl.ds((h * ROWS + k) * MODES + m, 1), :] = value

            put(ROW_L, inner[0:1, :])
            put(ROW_LP, inner_slope[0:1, :])
            put(ROW_V, total(weight * v))
            put(ROW_VP, total(weight * (vp[i] + float(run) * (float(RUNS - 1) - rank_h) * v)))
            state_in = coef[i] * s_loc
            for k in range(6):
                put(ROW_W + k, total(weight * w[i][k]))
                crosses[k, :, lanes] += state_in * w[i][k]
            put(ROW_R, total(r_sum[i] + v * s_loc))
            put(ROW_D, total(d_sum[i] + vp[i] * s_loc + v * sp_loc))

    for i in range(3):
        for b in range(2):
            at = 16 + RUNS * (run - 1 - b) + RUNS - 1
            rim_rows[2 * i + 1 - b : 2 * i + 2 - b, :] = ext[i, at : at + 1, :]
    rim_rows[6:8, :] = jnp.zeros((2, width), F32)

    lax.fori_loop(0, EARLY // TOGETHER, some_modes, 0)

    pl.semaphore_wait(barrier, group - 1 + 2 + 2)
    for d in cousins[1:]:
        pl.semaphore_signal(passed_on, inc=1, device_id={"ctx": d}, device_id_type=MESH)
    first_rows = pl.ds(0, 16)
    rims = (
        (rim_rows, halo_prev, after),
        (proj_ref.at[:, first_rows], halo_next.at[pl.ds(0, 3)], before),
        (cot_ref.at[first_rows], halo_next.at[3], before),
        (filt_ref.at[first_rows], halo_next.at[4], before),
    )
    rims = [
        pltpu.make_async_remote_copy(
            src, dst, halo_send.at[i], halo_recv.at[i], device_id={"ctx": to}, device_id_type=MESH
        )
        for i, (src, dst, to) in enumerate(rims)
    ]
    for rim in rims:
        rim.start()
    lax.fori_loop(EARLY // TOGETHER, MODES // TOGETHER, some_modes, 0)

    skip = skip_ref[...]
    inner_gated = longs[...] + skip * gf[...]
    own_query = masked(gq[...])
    plain = [total(own_query * shifted(0, j)) for j in range(3)]
    plain += [total(inner_gated * ys[k]) + total(crosses[k]) for k in range(6)]
    plain.append(total(gf[...] * gv[...]))

    def each_mode(k):
        return jnp.concatenate(
            [sums[(h * ROWS + k) * MODES : (h * ROWS + k + 1) * MODES, :] for h in range(2)], axis=1
        )

    def keep(k, value):
        for h in range(2):
            sums[(h * ROWS + k) * MODES : (h * ROWS + k + 1) * MODES, :] = value[:, h * half : (h + 1) * half]

    a_t = jnp.exp(-lam_t)
    back_two = jnp.exp(2.0 * lam_t)
    two, two_slope = each_mode(ROW_L), each_mode(ROW_LP)
    two, two_slope = back_two * two, back_two * (two_slope - 2.0 * two)
    slope_1 = a_t * (two_slope + two)
    moved = a_t * two
    decays = [jnp.exp(lam_t * -float(rows)), jnp.exp(lam_t * -float(rows - 1))]
    direct_sum, moved_sum = total(coef_t), total(coef_t * a_t)
    cot_two = [cot[0:1], cot[RUNS : RUNS + 1]]

    rims[0].wait_recv()
    has_before = jnp.where(me > 0, 1.0, 0.0)
    before_rows = [halo_prev[2 * i : 2 * i + 2, :] * has_before for i in range(3)]
    x = [
        {-2: before_rows[i][0:1], -1: before_rows[i][1:2], 0: ext[i, 16:17, :], 1: ext[i, 24:25, :]}
        for i in range(3)
    ]
    f = [[tap(i, 0) * x[i][t] + tap(i, 1) * x[i][t - 1] + tap(i, 2) * x[i][t - 2] for t in range(2)] for i in range(3)]
    gf_two = [cot_two[t] * f[0][t] for t in range(2)]
    gv_two = [f[1][t] * f[2][t] for t in range(2)]
    ys_two = [[f[2][t] * x[1][t - j] for j in range(3)] + [f[1][t] * x[2][t - j] for j in range(3)] for t in range(2)]

    state_1 = gf_two[1] + moved
    slope_0 = a_t * (slope_1 + state_1)
    state_0 = gf_two[0] + a_t * state_1
    parts = [decays[t] * gv_two[t] for t in range(2)]
    keep(ROW_L, state_0)
    keep(ROW_LP, slope_0)
    keep(ROW_V, each_mode(ROW_V) + parts[0] + parts[1])
    keep(ROW_VP, each_mode(ROW_VP) + float(rows) * parts[0] + float(rows - 1) * parts[1])
    for k in range(6):
        keep(ROW_W + k, each_mode(ROW_W + k) + decays[0] * ys_two[0][k] + decays[1] * ys_two[1][k])
    r_all = each_mode(ROW_R) + gv_two[1] * state_1 + gv_two[0] * state_0
    d_all = each_mode(ROW_D) + gv_two[1] * slope_1 + gv_two[0] * slope_0
    keep(ROW_R, r_all)
    keep(ROW_R + REST, rest(r_all))
    keep(ROW_D, d_all)
    keep(ROW_D + REST, rest(d_all))
    gated_two = [total(coef_t * state_0) + skip * gf_two[0], total(coef_t * state_1) + skip * gf_two[1]]
    for t in range(2):
        for j in range(3):
            plain[j] = plain[j] + gq[RUNS * t : RUNS * t + 1, :] * x[0][t - j]
        for k in range(6):
            plain[3 + k] = plain[3 + k] + gated_two[t] * ys_two[t][k]
        plain[9] = plain[9] + gf_two[t] * gv_two[t]
    plain = jnp.concatenate(plain + [jnp.zeros((MODES - len(plain), width), F32)], axis=0)
    keep(ROW_X, plain)
    keep(ROW_X + REST, rest(plain))
    for m in range(MODES):
        for h in range(2):
            sbuf[2 * m + h] = sums[pl.ds(h * ROWS * MODES + m, ROWS, stride=MODES), :].astype(BF16)

    own_a = pltpu.make_async_copy(sbuf.at[pos], rbuf.at[pos], a_recv)
    own_a.start()
    for p, index in peers:
        pltpu.make_async_remote_copy(
            sbuf.at[p], rbuf.at[pos], a_send, a_recv, device_id={"ctx": index}, device_id_type=MESH
        ).start()

    direct = [direct_sum * gf_two[0] + moved_sum * gf_two[1], direct_sum * gf_two[1]]
    for t in range(2):
        at = slice(RUNS * t, RUNS * t + 1)
        gf[at, :] = gf_two[t]
        longs[at, :] += direct[t]
        for i in (1, 2):
            feat[i - 1, at, :] = f[i][t]

    pltpu.make_async_copy(rbuf, rbuf, a_recv).wait()

    lam_o = owner_lam[pos]
    coef_o = owner_coef[pos]
    flat[...] = rbuf[...].astype(F32).reshape(group * ROWS, half)
    rank8 = lax.broadcasted_iota(jnp.int32, (per_block, half), 0).astype(F32)
    weight = jnp.exp(lam_o * (float(rows) * (rank8 - float(per_block - 1))))
    inside = []
    acc_r = acc_d = acc_x = jnp.zeros((per_block, half), F32)
    acc_w = [acc_r] * 6
    for b in range(4):
        base = b * per_block * ROWS

        def item(k):
            return flat[pl.ds(base + k, per_block, stride=ROWS), :]

        state, slope, v, vp = item(ROW_L), item(ROW_LP), item(ROW_V), item(ROW_VP)
        inner, inner_slope, s_int, sp_int = suffix(state, slope, lam_o, rows, per_block)
        inside.append(s_int)
        parts = [
            inner[0:1, :],
            inner_slope[0:1, :],
            total(weight * v),
            total(weight * (vp + float(rows) * (float(per_block - 1) - rank8) * v)),
        ]
        acc_r = acc_r + (item(ROW_R) + item(ROW_R + REST)) + v * s_int
        acc_d = acc_d + (item(ROW_D) + item(ROW_D + REST)) + vp * s_int + v * sp_int
        acc_x = acc_x + (item(ROW_X) + item(ROW_X + REST))
        for k in range(6):
            w_k = item(ROW_W + k)
            parts.append(total(weight * w_k))
            acc_w[k] = acc_w[k] + w_k * s_int
        for k, part in enumerate(parts):
            flat2[b * ROWS + k : b * ROWS + k + 1, :] = part
        flat2[b * ROWS + 10 : b * ROWS + ROWS, :] = jnp.zeros((ROWS - 10, half), F32)
    for k in range(6):
        value = total(acc_w[k])
        flat2[10 + k : 11 + k, :] = value
        flat2[2 * ROWS + 10 + k : 2 * ROWS + 11 + k, :] = rest(value)
    for k, acc in enumerate((acc_r, acc_d, acc_x)):
        value = total(acc)
        flat2[ROWS + 10 + k : ROWS + 11 + k, :] = value
        flat2[ROWS + 10 + REST + k : ROWS + 11 + REST + k, :] = rest(value)
    bbuf[...] = flat2[: 4 * ROWS, :].astype(BF16).reshape(4, ROWS, half)

    own_b = pltpu.make_async_copy(bbuf, bb.at[:, zh], b_recv)
    own_b.start()
    pl.semaphore_wait(passed_on, 2)
    for index in cousins:
        pltpu.make_async_remote_copy(
            bbuf, bb.at[:, zh], b_send, b_recv, device_id={"ctx": index}, device_id_type=MESH
        ).start()
    pltpu.make_async_copy(bb, bb, b_recv).wait()

    n_int = 4 * n_blocks
    flat2[...] = bb[...].astype(F32).reshape(n_int * ROWS, half)

    def item2(k):
        return flat2[pl.ds(k, n_int, stride=ROWS), :]

    lam2 = jnp.concatenate([lam_o, lam_o], axis=0)
    v, vp = item2(ROW_V), item2(ROW_VP)
    _, _, s_all, sp_all = suffix(item2(ROW_L), item2(ROW_LP), lam2, rows * per_block, n_int)
    si_ref[...] = s_all
    parts = [total(v * s_all), total(vp * s_all + v * sp_all)]
    interval = lax.broadcasted_iota(jnp.int32, (n_int, half), 0) // n_blocks
    in_1, in_0_2 = interval == 1, (interval == 0) | (interval == 2)

    def sum_1(k):
        return total(jnp.where(in_1, item2(10 + k) + item2(10 + REST + k), 0.0))

    for k in range(2):
        parts[k] = parts[k] + sum_1(k)
    for k in range(6):
        parts.append(coef_o[0:1, :] * total(item2(ROW_W + k) * s_all + jnp.where(in_0_2, item2(10 + k), 0.0)))
    parts.append(sum_1(2))
    parts += [rest(parts[0]), rest(parts[1]), rest(parts[8])]
    row16 = lax.broadcasted_iota(jnp.int32, (ROWS, half), 0)
    common = jnp.zeros((ROWS, half), F32)
    for k, part in enumerate(parts):
        common = jnp.where(row16 == 1 + k, part, common)
    for b in range(4):
        s_dev = inside[b] + weight * si_ref[pl.ds(b * n_blocks + zh, 1), :]
        s_rest = rest(s_dev)
        for i in range(per_block):
            own = jnp.where(row16 == 0, s_dev[i : i + 1, :], common)
            cbuf[b * per_block + i] = jnp.where(row16 == 13, s_rest[i : i + 1, :], own).astype(BF16)

    own_c = pltpu.make_async_copy(cbuf.at[pos], cr.at[pos], c_recv)
    own_c.start()
    for p, index in peers:
        pltpu.make_async_remote_copy(
            cbuf.at[p], cr.at[pos], c_send, c_recv, device_id={"ctx": index}, device_id_type=MESH
        ).start()

    for rim in rims[1:]:
        rim.wait_recv()
    has_after = jnp.where(me < n_ctx - 1, 1.0, 0.0)
    ahead = [halo_next[i].astype(F32) * has_after for i in range(5)]

    def ahead_feat(i, k):
        mine = [ext[i, 16 + RUNS * (run - 1 - b) + RUNS - 1 : 16 + RUNS * (run - b), :] for b in range(2)]
        if k == 0:
            return tap(i, 0) * ahead[i][0:1] + tap(i, 1) * mine[0] + tap(i, 2) * mine[1]
        return tap(i, 0) * ahead[i][1:2] + tap(i, 1) * ahead[i][0:1] + tap(i, 2) * mine[0]

    ahead_f = [[ahead_feat(i, k) for k in range(2)] for i in range(3)]
    ahead_gf = [ahead[3][k : k + 1] * ahead_f[0][k] for k in range(2)]
    ahead_gq = [ahead[3][k : k + 1] * ahead[4][k : k + 1] for k in range(2)]

    gather = jnp.where(col == RUNS * lax.rem(row, run) + lax.div(row, run), 1.0, 0.0).astype(BF16)
    last = lax.broadcasted_iota(jnp.int32, (RUNS, width), 0) == RUNS - 1

    def finish(i, beyond):
        for k in range(2):
            head = pltpu.roll(gs[i, RUNS * k : RUNS * (k + 1), :], RUNS - 1, axis=0)
            gs[i, rows + RUNS * k : rows + RUNS * (k + 1), :] = jnp.where(last, beyond[k], head)
        made = (
            tap(i, 0) * gs[i, :rows, :]
            + tap(i, 1) * gs[i, RUNS : rows + RUNS, :]
            + tap(i, 2) * gs[i, 2 * RUNS : rows + 2 * RUNS, :]
        )
        gp_ref[i] = jnp.dot(gather, made.astype(BF16), preferred_element_type=F32).astype(BF16)

    gs[0, :rows, :] = gq[...]
    finish(0, ahead_gq)
    for m in range(MODES):
        sloc[m] = coefs[m] * sloc[m]
        coefs[m] = coefs[m] * jnp.exp(lams[m] * (float(run) * (rank - float(RUNS - 1))))
        lams[m] = jnp.exp(-lams[m])

    pltpu.make_async_copy(cr, cr, c_recv).wait()
    flat[...] = cr[...].astype(F32).reshape(group * ROWS, half)

    def item3(k):
        return jnp.concatenate(
            [flat[pl.ds(h * ROWS + k, MODES, stride=2 * ROWS), :] for h in range(2)], axis=1
        )

    scale = 1.0 / math.sqrt(tokens)
    s_dev = item3(0) + item3(13)
    r_tot, d_tot, x_tot = item3(1) + item3(10), item3(2) + item3(11), item3(9) + item3(12)
    root = jnp.sqrt(lam_t)
    gres_ref[...] = scale * root * r_tot
    grate_ref[...] = scale * res_ref[...] * root * (0.5 / rate_ref[...] * r_tot - d_tot * (1.0 / tokens))
    for j in range(3):
        gshort_ref[0, j : j + 1, :] = scale * x_tot[j : j + 1, :]
        for i in (1, 2):
            k = 3 * (i - 1) + j
            gshort_ref[i, j : j + 1, :] = scale * (x_tot[3 + k : 4 + k, :] + total(item3(3 + k)))
    gskip_ref[...] = scale * x_tot[9:10, :]

    for h in range(2):
        lanes = slice(h * half, (h + 1) * half)
        a = [lams[m, :, lanes] for m in range(MODES)]
        p = [sloc[m, :, lanes] + coefs[m, :, lanes] * s_dev[m : m + 1, lanes] for m in range(MODES)]
        for r in range(run - 1, -1, -1):
            at = slice(RUNS * r, RUNS * (r + 1))
            p = [x * d for x, d in zip(p, a)]
            terms = p
            while len(terms) > 1:
                terms = [u + w for u, w in zip(terms[::2], terms[1::2])]
            longs[at, lanes] += terms[0]

    gated = longs[...] + skip * gf[...]
    gs[1, :rows, :] = gated * feat[1]
    gs[2, :rows, :] = gated * feat[0]
    ahead_long = [
        total(coef_t * s_dev),
        total(coef_t * (s_dev - ahead_gf[0]) * jnp.exp(lam_t)),
    ]
    ahead_gated = [(ahead_long[k] + skip * ahead_gf[k]) * has_after for k in range(2)]
    finish(1, [ahead_gated[k] * ahead_f[2][k] for k in range(2)])
    finish(2, [ahead_gated[k] * ahead_f[1][k] for k in range(2)])

    for rim in rims:
        rim.wait_send()
    others = pl.ds(0, group - 1)
    pltpu.make_async_copy(sbuf.at[others], sbuf.at[others], a_send).wait()
    pltpu.make_async_copy(bb.at[pl.ds(0, n_blocks - 1)], bb.at[pl.ds(0, n_blocks - 1)], b_send).wait()
    pltpu.make_async_copy(cbuf.at[others], cbuf.at[others], c_send).wait()


def hand_over(*refs):
    count = (len(refs) - 1) // 2
    sems = refs[-1]
    copies = [
        pltpu.make_async_copy(src, dst, sems.at[i])
        for i, (src, dst) in enumerate(zip(refs[:count], refs[count : 2 * count]))
    ]
    for copy in copies:
        copy.start()
    for copy in copies:
        copy.wait()


def solution(mesh):
    n_ctx = mesh.shape["ctx"]
    n_blocks = n_ctx // 32

    def body(projections, filtered, cotangent, short_taps, residues, pole_rates, skip_gain):
        rows, width = filtered.shape
        half = width // 2
        vmem = pl.BlockSpec(memory_space=pltpu.VMEM)
        full = (rows, width)
        made = (
            jax.ShapeDtypeStruct((3,) + full, BF16),
            jax.ShapeDtypeStruct((3, 3, width), F32),
            jax.ShapeDtypeStruct((MODES, width), F32),
            jax.ShapeDtypeStruct((MODES, width), F32),
            jax.ShapeDtypeStruct((1, width), F32),
        )
        args = (projections, filtered, cotangent, short_taps, residues.T, pole_rates.T, skip_gain.reshape(1, width))
        out = pl.pallas_call(
            functools.partial(kernel, (n_ctx, n_blocks)),
            out_shape=[pltpu.VMEM(x.shape, x.dtype) for x in made],
            in_specs=[pl.BlockSpec(memory_space=pltpu.HBM)] * 7,
            out_specs=[vmem] * 5,
            scratch_shapes=[pltpu.VMEM(x.shape, x.dtype) for x in args]
            + [
                pltpu.VMEM((3, rows + 16, width), F32),
                pltpu.VMEM((2,) + full, F32),
                pltpu.VMEM(full, F32),
                pltpu.VMEM(full, F32),
                pltpu.VMEM(full, F32),
                pltpu.VMEM(full, F32),
                pltpu.VMEM((6,) + full, F32),
                pltpu.VMEM(full, F32),
                pltpu.VMEM((MODES, RUNS, width), F32),
                pltpu.VMEM((MODES, RUNS, width), F32),
                pltpu.VMEM((2 * MODES, RUNS, half), F32),
                pltpu.VMEM((2 * MODES, RUNS, half), F32),
                pltpu.VMEM((MODES, RUNS, width), F32),
                pltpu.VMEM((6, RUNS, width), F32),
                pltpu.VMEM((2 * MODES * ROWS, half), F32),
                pltpu.VMEM((32, ROWS, half), BF16),
                pltpu.VMEM((32, ROWS, half), BF16),
                pltpu.VMEM((32 * ROWS, half), F32),
                pltpu.VMEM((4, ROWS, half), BF16),
                pltpu.VMEM((4, n_blocks, ROWS, half), BF16),
                pltpu.VMEM((4 * n_blocks * ROWS, half), F32),
                pltpu.VMEM((4 * n_blocks, half), F32),
                pltpu.VMEM((32, ROWS, half), BF16),
                pltpu.VMEM((32, ROWS, half), BF16),
                pltpu.VMEM((3, rows + 16, width), F32),
                pltpu.VMEM((8, width), F32),
                pltpu.VMEM((8, width), F32),
                pltpu.VMEM((5, 16, width), BF16),
                pltpu.SemaphoreType.REGULAR,
                pltpu.SemaphoreType.DMA((7,)),
                pltpu.SemaphoreType.DMA((4,)),
                pltpu.SemaphoreType.DMA((4,)),
                pltpu.SemaphoreType.DMA,
                pltpu.SemaphoreType.DMA,
                pltpu.SemaphoreType.DMA,
                pltpu.SemaphoreType.DMA,
                pltpu.SemaphoreType.DMA,
                pltpu.SemaphoreType.DMA,
            ],
            compiler_params=pltpu.CompilerParams(
                collective_id=0, has_side_effects=True, vmem_limit_bytes=40 * 1024 * 1024
            ),
        )(*(pltpu.with_memory_space_constraint(x, pltpu.HBM) for x in args))
        out = pl.pallas_call(
            hand_over,
            out_shape=[pltpu.HBM(x.shape, x.dtype) for x in made],
            in_specs=[vmem] * 5,
            out_specs=[pl.BlockSpec(memory_space=pltpu.HBM)] * 5,
            scratch_shapes=[pltpu.SemaphoreType.DMA((5,))],
        )(*(pltpu.with_memory_space_constraint(x, pltpu.VMEM) for x in out))
        return out[0], out[1], out[2].T, out[3].T, out[4].reshape(width)

    return jax.shard_map(
        body,
        mesh=mesh,
        in_specs=(
            P(None, "ctx", "ch"),
            P("ctx", "ch"),
            P("ctx", "ch"),
            P(None, None, "ch"),
            P("ch", None),
            P("ch", None),
            P("ch"),
        ),
        out_specs=(
            P(None, "ctx", "ch"),
            P(None, None, "ch"),
            P("ch", None),
            P("ch", None),
            P("ch"),
        ),
        check_vma=False,
    )
```

```python
import functools
import math

import jax
import jax.numpy as jnp
from jax import lax
from jax.experimental import pallas as pl
from jax.experimental.pallas import tpu as pltpu
from jax.sharding import PartitionSpec as P

MESH = pl.DeviceIdType.MESH
F32 = jnp.float32
BF16 = jnp.bfloat16

RUNS = 8
MODES = 16
ROWS = 16
EARLY = 12
TOGETHER = 2
ROW_L, ROW_LP, ROW_V, ROW_VP, ROW_W, ROW_R, ROW_D, ROW_X = 0, 1, 2, 3, 4, 10, 11, 12
REST = 3


def up(x, by, size):
    return pltpu.roll(x, size - by, axis=0)


def suffix(state, slope, lam, length, count):
    row = lax.broadcasted_iota(jnp.int32, state.shape, 0)
    by = 1
    while by < count:
        decay = jnp.where(row < count - by, jnp.exp(lam * float(-length * by)), 0.0)
        later, later_slope = up(state, by, count), up(slope, by, count)
        slope = slope + decay * (later_slope + float(length * by) * later)
        state = state + decay * later
        by *= 2
    inside = row < count - 1
    return (
        state,
        slope,
        jnp.where(inside, up(state, 1, count), 0.0),
        jnp.where(inside, up(slope, 1, count), 0.0),
    )


def total(x):
    return jnp.sum(x, axis=0, keepdims=True)


def rest(x):
    return x - x.astype(BF16).astype(F32)


def kernel(
    geometry,
    proj_hbm,
    filt_hbm,
    cot_hbm,
    taps_hbm,
    res_hbm,
    rate_hbm,
    skip_hbm,
    gp_ref,
    gshort_ref,
    gres_ref,
    grate_ref,
    gskip_ref,
    proj_ref,
    filt_ref,
    cot_ref,
    taps_ref,
    res_ref,
    rate_ref,
    skip_ref,
    ext,
    feat,
    gf,
    gv,
    gz,
    gq,
    ys,
    longs,
    lams,
    coefs,
    owner_lam,
    owner_coef,
    sloc,
    crosses,
    sums,
    sbuf,
    rbuf,
    flat,
    bbuf,
    bb,
    flat2,
    si_ref,
    cbuf,
    cr,
    gs,
    rim_rows,
    halo_prev,
    halo_next,
    passed_on,
    in_sem,
    halo_send,
    halo_recv,
    a_send,
    a_recv,
    b_send,
    b_recv,
    c_send,
    c_recv,
):
    n_ctx, n_blocks = geometry
    rows = proj_ref.shape[1]
    width = proj_ref.shape[2]
    half = width // 2
    run = rows // RUNS
    tokens = rows * n_ctx
    per_block = 8
    group = 32
    me = lax.axis_index("ctx")
    y = lax.div(me, per_block * n_blocks)
    zh = lax.rem(lax.div(me, per_block), n_blocks)
    lo = lax.rem(me, per_block)
    pos = y * per_block + lo
    held = (
        (taps_hbm, taps_ref),
        (res_hbm, res_ref),
        (rate_hbm, rate_ref),
        (skip_hbm, skip_ref),
        (proj_hbm, proj_ref),
        (cot_hbm, cot_ref),
        (filt_hbm, filt_ref),
    )
    loads = [pltpu.make_async_copy(src, dst, in_sem.at[i]) for i, (src, dst) in enumerate(held)]
    for load in loads:
        load.start()

    ys_of = [lax.rem(y + d, 4) for d in range(4)]
    bases = [v * (per_block * n_blocks) + zh * per_block for v in ys_of]
    zl, core = lax.div(lo, 2), lax.rem(lo, 2)
    zls_of = (zl, zl + 1 - 2 * lax.rem(zl, 2), lax.rem(zl + 2, 4), 3 - zl)
    los_of = [[2 * v + core, 2 * v + 1 - core] for v in zls_of]
    steps = ((2, 3), (2, 2), (1, 3), (3, 3), (1, 2), (3, 2), (2, 1), (0, 3), (2, 0), (0, 2), (1, 1), (3, 1), (1, 0), (3, 0), (0, 1), (0, 0))
    peers = [
        (ys_of[d] * per_block + los_of[k][c], bases[d] + los_of[k][c])
        for d, k in steps
        for c in (1, 0)
        if (d, k, c) != (0, 0, 0)
    ]
    cousins = [y * (per_block * n_blocks) + lax.rem(zh + j, n_blocks) * per_block + lo for j in (2, 1, 3)]
    before, after = lax.rem(me + n_ctx - 1, n_ctx), lax.rem(me + 1, n_ctx)
    barrier = pltpu.get_barrier_semaphore()
    for d in [index for _, index in peers] + cousins[1:] + [before, after]:
        pl.semaphore_signal(barrier, inc=1, device_id={"ctx": d}, device_id_type=MESH)

    row = lax.broadcasted_iota(jnp.int32, (rows, rows), 0)
    col = lax.broadcasted_iota(jnp.int32, (rows, rows), 1)
    spread = jnp.where(col == run * (row % RUNS) + row // RUNS, 1.0, 0.0).astype(BF16)
    for load in loads[:4]:
        load.wait()

    lam_t = rate_ref[...] * (1.0 / tokens)
    coef_t = res_ref[...] * jnp.sqrt(lam_t)
    for m in range(MODES):
        lam_m = jnp.broadcast_to(lam_t[m : m + 1, :], (RUNS, width))
        coef_m = jnp.broadcast_to(coef_t[m : m + 1, :], (RUNS, width))
        lams[m] = lam_m
        coefs[m] = coef_m
        for h in range(2):
            owner_lam[2 * m + h] = lam_m[:, h * half : (h + 1) * half]
            owner_coef[2 * m + h] = coef_m[:, h * half : (h + 1) * half]

    def placed(x):
        return jnp.dot(spread, x, preferred_element_type=F32)

    first = lax.broadcasted_iota(jnp.int32, (RUNS, width), 0) == 0
    first_two = lax.broadcasted_iota(jnp.int32, (2 * RUNS, width), 0) % RUNS == 0
    for load in loads[4:]:
        load.wait()
    for i in range(3):
        ext[i, 16:, :] = placed(proj_ref[i])
        for back in (2, 1):
            tail = pltpu.roll(ext[i, 16 + RUNS * (run - back) : 16 + RUNS * (run - back + 1), :], 1, axis=0)
            ext[i, 16 - 8 * back : 24 - 8 * back, :] = jnp.where(first, 0.0, tail)

    def tap(i, j):
        return taps_ref[i, j : j + 1, :]

    def shifted(i, j):
        return ext[i, 16 - 8 * j : 16 - 8 * j + rows, :]

    def masked(x):
        return jnp.concatenate([jnp.where(first_two, 0.0, x[: 2 * RUNS]), x[2 * RUNS :]], axis=0)

    cot = placed(cot_ref[...])
    gq[...] = cot * placed(filt_ref[...])
    for i in range(3):
        made = tap(i, 0) * shifted(i, 0) + tap(i, 1) * shifted(i, 1) + tap(i, 2) * shifted(i, 2)
        if i == 0:
            gf[...] = masked(cot * made)
        else:
            feat[i - 1] = made
    gv[...] = masked(feat[0] * feat[1])
    step_of = lax.broadcasted_iota(jnp.int32, (rows, width), 0) // RUNS
    to_end = (run - step_of).astype(F32)
    gz[...] = to_end * gv[...]
    for j in range(3):
        ys[j] = masked(feat[1] * shifted(1, j))
        ys[3 + j] = masked(feat[0] * shifted(2, j))

    longs[...] = jnp.zeros_like(longs)
    crosses[...] = jnp.zeros_like(crosses)

    rank = lax.broadcasted_iota(jnp.int32, (RUNS, width), 0).astype(F32)

    def some_modes(at, _):
        for h in range(2):
            some_modes_of_half(at, h)
        return 0

    def some_modes_of_half(at, h):
        lanes = slice(h * half, (h + 1) * half)
        modes = [at * TOGETHER + i for i in range(TOGETHER)]
        lam = [lams[m, :, lanes] for m in modes]
        coef = [coefs[m, :, lanes] for m in modes]
        a = [jnp.exp(-x) for x in lam]
        zero = jnp.zeros((RUNS, half), F32)
        state, slope, r_sum, d_sum, vp = ([zero] * TOGETHER for _ in range(5))
        w = [[zero] * 6 for _ in modes]
        for step in range(run):
            low = slice(RUNS * (run - 1 - step), RUNS * (run - step))
            high = slice(RUNS * step, RUNS * (step + 1))
            gf_low, gv_low, gz_high = gf[low, lanes], gv[low, lanes], gz[high, lanes]
            ys_high = [ys[k, high, lanes] for k in range(6)]
            part = None
            for i in range(TOGETHER):
                slope[i] = a[i] * (slope[i] + state[i])
                state[i] = a[i] * state[i] + gf_low
                given = coef[i] * state[i]
                part = given if part is None else part + given
                r_sum[i] = r_sum[i] + gv_low * state[i]
                d_sum[i] = d_sum[i] + gv_low * slope[i]
                vp[i] = a[i] * (vp[i] + gz_high)
                for k in range(6):
                    w[i][k] = a[i] * (w[i][k] + ys_high[k])
            longs[low, lanes] += part
        rank_h = rank[:, lanes]
        for i, m in enumerate(modes):
            v = sum(taps_ref[1, j : j + 1, lanes] * w[i][j] for j in range(3))
            inner, inner_slope, s_loc, sp_loc = suffix(state[i], slope[i], lam[i], run, RUNS)
            sloc[m, :, lanes] = s_loc
            weight = jnp.exp(lam[i] * (float(run) * (rank_h - float(RUNS - 1))))

            def put(k, value):
                sums[pl.ds((h * ROWS + k) * MODES + m, 1), :] = value

            put(ROW_L, inner[0:1, :])
            put(ROW_LP, inner_slope[0:1, :])
            put(ROW_V, total(weight * v))
            put(ROW_VP, total(weight * (vp[i] + float(run) * (float(RUNS - 1) - rank_h) * v)))
            state_in = coef[i] * s_loc
            for k in range(6):
                put(ROW_W + k, total(weight * w[i][k]))
                crosses[k, :, lanes] += state_in * w[i][k]
            put(ROW_R, total(r_sum[i] + v * s_loc))
            put(ROW_D, total(d_sum[i] + vp[i] * s_loc + v * sp_loc))

    for i in range(3):
        for b in range(2):
            at = 16 + RUNS * (run - 1 - b) + RUNS - 1
            rim_rows[2 * i + 1 - b : 2 * i + 2 - b, :] = ext[i, at : at + 1, :]
    rim_rows[6:8, :] = jnp.zeros((2, width), F32)

    lax.fori_loop(0, EARLY // TOGETHER, some_modes, 0)

    pl.semaphore_wait(barrier, group - 1 + 2 + 2)
    for d in cousins[1:]:
        pl.semaphore_signal(passed_on, inc=1, device_id={"ctx": d}, device_id_type=MESH)
    first_rows = pl.ds(0, 16)
    rims = (
        (rim_rows, halo_prev, after),
        (proj_ref.at[:, first_rows], halo_next.at[pl.ds(0, 3)], before),
        (cot_ref.at[first_rows], halo_next.at[3], before),
        (filt_ref.at[first_rows], halo_next.at[4], before),
    )
    rims = [
        pltpu.make_async_remote_copy(
            src, dst, halo_send.at[i], halo_recv.at[i], device_id={"ctx": to}, device_id_type=MESH
        )
        for i, (src, dst, to) in enumerate(rims)
    ]
    for rim in rims:
        rim.start()
    lax.fori_loop(EARLY // TOGETHER, MODES // TOGETHER, some_modes, 0)

    skip = skip_ref[...]
    inner_gated = longs[...] + skip * gf[...]
    own_query = masked(gq[...])
    plain = [total(own_query * shifted(0, j)) for j in range(3)]
    plain += [total(inner_gated * ys[k]) + total(crosses[k]) for k in range(6)]
    plain.append(total(gf[...] * gv[...]))

    def each_mode(k):
        return jnp.concatenate(
            [sums[(h * ROWS + k) * MODES : (h * ROWS + k + 1) * MODES, :] for h in range(2)], axis=1
        )

    def keep(k, value):
        for h in range(2):
            sums[(h * ROWS + k) * MODES : (h * ROWS + k + 1) * MODES, :] = value[:, h * half : (h + 1) * half]

    a_t = jnp.exp(-lam_t)
    back_two = jnp.exp(2.0 * lam_t)
    two, two_slope = each_mode(ROW_L), each_mode(ROW_LP)
    two, two_slope = back_two * two, back_two * (two_slope - 2.0 * two)
    slope_1 = a_t * (two_slope + two)
    moved = a_t * two
    decays = [jnp.exp(lam_t * -float(rows)), jnp.exp(lam_t * -float(rows - 1))]
    direct_sum, moved_sum = total(coef_t), total(coef_t * a_t)
    cot_two = [cot[0:1], cot[RUNS : RUNS + 1]]

    rims[0].wait_recv()
    has_before = jnp.where(me > 0, 1.0, 0.0)
    before_rows = [halo_prev[2 * i : 2 * i + 2, :] * has_before for i in range(3)]
    x = [
        {-2: before_rows[i][0:1], -1: before_rows[i][1:2], 0: ext[i, 16:17, :], 1: ext[i, 24:25, :]}
        for i in range(3)
    ]
    f = [[tap(i, 0) * x[i][t] + tap(i, 1) * x[i][t - 1] + tap(i, 2) * x[i][t - 2] for t in range(2)] for i in range(3)]
    gf_two = [cot_two[t] * f[0][t] for t in range(2)]
    gv_two = [f[1][t] * f[2][t] for t in range(2)]
    ys_two = [[f[2][t] * x[1][t - j] for j in range(3)] + [f[1][t] * x[2][t - j] for j in range(3)] for t in range(2)]

    state_1 = gf_two[1] + moved
    slope_0 = a_t * (slope_1 + state_1)
    state_0 = gf_two[0] + a_t * state_1
    parts = [decays[t] * gv_two[t] for t in range(2)]
    keep(ROW_L, state_0)
    keep(ROW_LP, slope_0)
    keep(ROW_V, each_mode(ROW_V) + parts[0] + parts[1])
    keep(ROW_VP, each_mode(ROW_VP) + float(rows) * parts[0] + float(rows - 1) * parts[1])
    for k in range(6):
        keep(ROW_W + k, each_mode(ROW_W + k) + decays[0] * ys_two[0][k] + decays[1] * ys_two[1][k])
    r_all = each_mode(ROW_R) + gv_two[1] * state_1 + gv_two[0] * state_0
    d_all = each_mode(ROW_D) + gv_two[1] * slope_1 + gv_two[0] * slope_0
    keep(ROW_R, r_all)
    keep(ROW_R + REST, rest(r_all))
    keep(ROW_D, d_all)
    keep(ROW_D + REST, rest(d_all))
    gated_two = [total(coef_t * state_0) + skip * gf_two[0], total(coef_t * state_1) + skip * gf_two[1]]
    for t in range(2):
        for j in range(3):
            plain[j] = plain[j] + gq[RUNS * t : RUNS * t + 1, :] * x[0][t - j]
        for k in range(6):
            plain[3 + k] = plain[3 + k] + gated_two[t] * ys_two[t][k]
        plain[9] = plain[9] + gf_two[t] * gv_two[t]
    plain = jnp.concatenate(plain + [jnp.zeros((MODES - len(plain), width), F32)], axis=0)
    keep(ROW_X, plain)
    keep(ROW_X + REST, rest(plain))
    for m in range(MODES):
        for h in range(2):
            sbuf[2 * m + h] = sums[pl.ds(h * ROWS * MODES + m, ROWS, stride=MODES), :].astype(BF16)

    own_a = pltpu.make_async_copy(sbuf.at[pos], rbuf.at[pos], a_recv)
    own_a.start()
    for p, index in peers:
        pltpu.make_async_remote_copy(
            sbuf.at[p], rbuf.at[pos], a_send, a_recv, device_id={"ctx": index}, device_id_type=MESH
        ).start()

    direct = [direct_sum * gf_two[0] + moved_sum * gf_two[1], direct_sum * gf_two[1]]
    for t in range(2):
        at = slice(RUNS * t, RUNS * t + 1)
        gf[at, :] = gf_two[t]
        longs[at, :] += direct[t]
        for i in (1, 2):
            feat[i - 1, at, :] = f[i][t]

    pltpu.make_async_copy(rbuf, rbuf, a_recv).wait()

    lam_o = owner_lam[pos]
    coef_o = owner_coef[pos]
    flat[...] = rbuf[...].astype(F32).reshape(group * ROWS, half)
    rank8 = lax.broadcasted_iota(jnp.int32, (per_block, half), 0).astype(F32)
    weight = jnp.exp(lam_o * (float(rows) * (rank8 - float(per_block - 1))))
    inside = []
    acc_r = acc_d = acc_x = jnp.zeros((per_block, half), F32)
    acc_w = [acc_r] * 6
    for b in range(4):
        base = b * per_block * ROWS

        def item(k):
            return flat[pl.ds(base + k, per_block, stride=ROWS), :]

        state, slope, v, vp = item(ROW_L), item(ROW_LP), item(ROW_V), item(ROW_VP)
        inner, inner_slope, s_int, sp_int = suffix(state, slope, lam_o, rows, per_block)
        inside.append(s_int)
        parts = [
            inner[0:1, :],
            inner_slope[0:1, :],
            total(weight * v),
            total(weight * (vp + float(rows) * (float(per_block - 1) - rank8) * v)),
        ]
        acc_r = acc_r + (item(ROW_R) + item(ROW_R + REST)) + v * s_int
        acc_d = acc_d + (item(ROW_D) + item(ROW_D + REST)) + vp * s_int + v * sp_int
        acc_x = acc_x + (item(ROW_X) + item(ROW_X + REST))
        for k in range(6):
            w_k = item(ROW_W + k)
            parts.append(total(weight * w_k))
            acc_w[k] = acc_w[k] + w_k * s_int
        for k, part in enumerate(parts):
            flat2[b * ROWS + k : b * ROWS + k + 1, :] = part
        flat2[b * ROWS + 10 : b * ROWS + ROWS, :] = jnp.zeros((ROWS - 10, half), F32)
    for k in range(6):
        value = total(acc_w[k])
        flat2[10 + k : 11 + k, :] = value
        flat2[2 * ROWS + 10 + k : 2 * ROWS + 11 + k, :] = rest(value)
    for k, acc in enumerate((acc_r, acc_d, acc_x)):
        value = total(acc)
        flat2[ROWS + 10 + k : ROWS + 11 + k, :] = value
        flat2[ROWS + 10 + REST + k : ROWS + 11 + REST + k, :] = rest(value)
    bbuf[...] = flat2[: 4 * ROWS, :].astype(BF16).reshape(4, ROWS, half)

    own_b = pltpu.make_async_copy(bbuf, bb.at[:, zh], b_recv)
    own_b.start()
    pl.semaphore_wait(passed_on, 2)
    for index in cousins:
        pltpu.make_async_remote_copy(
            bbuf, bb.at[:, zh], b_send, b_recv, device_id={"ctx": index}, device_id_type=MESH
        ).start()
    pltpu.make_async_copy(bb, bb, b_recv).wait()

    n_int = 4 * n_blocks
    flat2[...] = bb[...].astype(F32).reshape(n_int * ROWS, half)

    def item2(k):
        return flat2[pl.ds(k, n_int, stride=ROWS), :]

    lam2 = jnp.concatenate([lam_o, lam_o], axis=0)
    v, vp = item2(ROW_V), item2(ROW_VP)
    _, _, s_all, sp_all = suffix(item2(ROW_L), item2(ROW_LP), lam2, rows * per_block, n_int)
    si_ref[...] = s_all
    parts = [total(v * s_all), total(vp * s_all + v * sp_all)]
    interval = lax.broadcasted_iota(jnp.int32, (n_int, half), 0) // n_blocks
    in_1, in_0_2 = interval == 1, (interval == 0) | (interval == 2)

    def sum_1(k):
        return total(jnp.where(in_1, item2(10 + k) + item2(10 + REST + k), 0.0))

    for k in range(2):
        parts[k] = parts[k] + sum_1(k)
    for k in range(6):
        parts.append(coef_o[0:1, :] * total(item2(ROW_W + k) * s_all + jnp.where(in_0_2, item2(10 + k), 0.0)))
    parts.append(sum_1(2))
    parts += [rest(parts[0]), rest(parts[1]), rest(parts[8])]
    row16 = lax.broadcasted_iota(jnp.int32, (ROWS, half), 0)
    common = jnp.zeros((ROWS, half), F32)
    for k, part in enumerate(parts):
        common = jnp.where(row16 == 1 + k, part, common)
    for b in range(4):
        s_dev = inside[b] + weight * si_ref[pl.ds(b * n_blocks + zh, 1), :]
        s_rest = rest(s_dev)
        for i in range(per_block):
            own = jnp.where(row16 == 0, s_dev[i : i + 1, :], common)
            cbuf[b * per_block + i] = jnp.where(row16 == 13, s_rest[i : i + 1, :], own).astype(BF16)

    own_c = pltpu.make_async_copy(cbuf.at[pos], cr.at[pos], c_recv)
    own_c.start()
    for p, index in peers:
        pltpu.make_async_remote_copy(
            cbuf.at[p], cr.at[pos], c_send, c_recv, device_id={"ctx": index}, device_id_type=MESH
        ).start()

    for rim in rims[1:]:
        rim.wait_recv()
    has_after = jnp.where(me < n_ctx - 1, 1.0, 0.0)
    ahead = [halo_next[i].astype(F32) * has_after for i in range(5)]

    def ahead_feat(i, k):
        mine = [ext[i, 16 + RUNS * (run - 1 - b) + RUNS - 1 : 16 + RUNS * (run - b), :] for b in range(2)]
        if k == 0:
            return tap(i, 0) * ahead[i][0:1] + tap(i, 1) * mine[0] + tap(i, 2) * mine[1]
        return tap(i, 0) * ahead[i][1:2] + tap(i, 1) * ahead[i][0:1] + tap(i, 2) * mine[0]

    ahead_f = [[ahead_feat(i, k) for k in range(2)] for i in range(3)]
    ahead_gf = [ahead[3][k : k + 1] * ahead_f[0][k] for k in range(2)]
    ahead_gq = [ahead[3][k : k + 1] * ahead[4][k : k + 1] for k in range(2)]

    gather = jnp.where(col == RUNS * lax.rem(row, run) + lax.div(row, run), 1.0, 0.0).astype(BF16)
    last = lax.broadcasted_iota(jnp.int32, (RUNS, width), 0) == RUNS - 1

    def finish(i, beyond):
        for k in range(2):
            head = pltpu.roll(gs[i, RUNS * k : RUNS * (k + 1), :], RUNS - 1, axis=0)
            gs[i, rows + RUNS * k : rows + RUNS * (k + 1), :] = jnp.where(last, beyond[k], head)
        made = (
            tap(i, 0) * gs[i, :rows, :]
            + tap(i, 1) * gs[i, RUNS : rows + RUNS, :]
            + tap(i, 2) * gs[i, 2 * RUNS : rows + 2 * RUNS, :]
        )
        gp_ref[i] = jnp.dot(gather, made.astype(BF16), preferred_element_type=F32).astype(BF16)

    gs[0, :rows, :] = gq[...]
    finish(0, ahead_gq)
    for m in range(MODES):
        sloc[m] = coefs[m] * sloc[m]
        coefs[m] = coefs[m] * jnp.exp(lams[m] * (float(run) * (rank - float(RUNS - 1))))
        lams[m] = jnp.exp(-lams[m])

    pltpu.make_async_copy(cr, cr, c_recv).wait()
    flat[...] = cr[...].astype(F32).reshape(group * ROWS, half)

    def item3(k):
        return jnp.concatenate(
            [flat[pl.ds(h * ROWS + k, MODES, stride=2 * ROWS), :] for h in range(2)], axis=1
        )

    scale = 1.0 / math.sqrt(tokens)
    s_dev = item3(0) + item3(13)
    r_tot, d_tot, x_tot = item3(1) + item3(10), item3(2) + item3(11), item3(9) + item3(12)
    root = jnp.sqrt(lam_t)
    gres_ref[...] = scale * root * r_tot
    grate_ref[...] = scale * res_ref[...] * root * (0.5 / rate_ref[...] * r_tot - d_tot * (1.0 / tokens))
    for j in range(3):
        gshort_ref[0, j : j + 1, :] = scale * x_tot[j : j + 1, :]
        for i in (1, 2):
            k = 3 * (i - 1) + j
            gshort_ref[i, j : j + 1, :] = scale * (x_tot[3 + k : 4 + k, :] + total(item3(3 + k)))
    gskip_ref[...] = scale * x_tot[9:10, :]

    for h in range(2):
        lanes = slice(h * half, (h + 1) * half)
        a = [lams[m, :, lanes] for m in range(MODES)]
        p = [sloc[m, :, lanes] + coefs[m, :, lanes] * s_dev[m : m + 1, lanes] for m in range(MODES)]
        for r in range(run - 1, -1, -1):
            at = slice(RUNS * r, RUNS * (r + 1))
            p = [x * d for x, d in zip(p, a)]
            terms = p
            while len(terms) > 1:
                terms = [u + w for u, w in zip(terms[::2], terms[1::2])]
            longs[at, lanes] += terms[0]

    gated = longs[...] + skip * gf[...]
    gs[1, :rows, :] = gated * feat[1]
    gs[2, :rows, :] = gated * feat[0]
    ahead_long = [
        total(coef_t * s_dev),
        total(coef_t * (s_dev - ahead_gf[0]) * jnp.exp(lam_t)),
    ]
    ahead_gated = [(ahead_long[k] + skip * ahead_gf[k]) * has_after for k in range(2)]
    finish(1, [ahead_gated[k] * ahead_f[2][k] for k in range(2)])
    finish(2, [ahead_gated[k] * ahead_f[1][k] for k in range(2)])

    for rim in rims:
        rim.wait_send()
    others = pl.ds(0, group - 1)
    pltpu.make_async_copy(sbuf.at[others], sbuf.at[others], a_send).wait()
    pltpu.make_async_copy(bb.at[pl.ds(0, n_blocks - 1)], bb.at[pl.ds(0, n_blocks - 1)], b_send).wait()
    pltpu.make_async_copy(cbuf.at[others], cbuf.at[others], c_send).wait()


def hand_over(*refs):
    count = (len(refs) - 1) // 2
    sems = refs[-1]
    pairs = [(refs[0].at[i], refs[count].at[i]) for i in range(3)]
    pairs += list(zip(refs[1:count], refs[count + 1 : 2 * count]))
    copies = [pltpu.make_async_copy(src, dst, sems.at[i]) for i, (src, dst) in enumerate(pairs)]
    for copy in copies:
        copy.start()
    for copy in copies:
        copy.wait()


def solution(mesh):
    n_ctx = mesh.shape["ctx"]
    n_blocks = n_ctx // 32

    def body(projections, filtered, cotangent, short_taps, residues, pole_rates, skip_gain):
        rows, width = filtered.shape
        half = width // 2
        vmem = pl.BlockSpec(memory_space=pltpu.VMEM)
        full = (rows, width)
        made = (
            jax.ShapeDtypeStruct((3,) + full, BF16),
            jax.ShapeDtypeStruct((3, 3, width), F32),
            jax.ShapeDtypeStruct((MODES, width), F32),
            jax.ShapeDtypeStruct((MODES, width), F32),
            jax.ShapeDtypeStruct((1, width), F32),
        )
        args = (projections, filtered, cotangent, short_taps, residues.T, pole_rates.T, skip_gain.reshape(1, width))
        out = pl.pallas_call(
            functools.partial(kernel, (n_ctx, n_blocks)),
            out_shape=[pltpu.VMEM(x.shape, x.dtype) for x in made],
            in_specs=[pl.BlockSpec(memory_space=pltpu.HBM)] * 7,
            out_specs=[vmem] * 5,
            scratch_shapes=[pltpu.VMEM(x.shape, x.dtype) for x in args]
            + [
                pltpu.VMEM((3, rows + 16, width), F32),
                pltpu.VMEM((2,) + full, F32),
                pltpu.VMEM(full, F32),
                pltpu.VMEM(full, F32),
                pltpu.VMEM(full, F32),
                pltpu.VMEM(full, F32),
                pltpu.VMEM((6,) + full, F32),
                pltpu.VMEM(full, F32),
                pltpu.VMEM((MODES, RUNS, width), F32),
                pltpu.VMEM((MODES, RUNS, width), F32),
                pltpu.VMEM((2 * MODES, RUNS, half), F32),
                pltpu.VMEM((2 * MODES, RUNS, half), F32),
                pltpu.VMEM((MODES, RUNS, width), F32),
                pltpu.VMEM((6, RUNS, width), F32),
                pltpu.VMEM((2 * MODES * ROWS, half), F32),
                pltpu.VMEM((32, ROWS, half), BF16),
                pltpu.VMEM((32, ROWS, half), BF16),
                pltpu.VMEM((32 * ROWS, half), F32),
                pltpu.VMEM((4, ROWS, half), BF16),
                pltpu.VMEM((4, n_blocks, ROWS, half), BF16),
                pltpu.VMEM((4 * n_blocks * ROWS, half), F32),
                pltpu.VMEM((4 * n_blocks, half), F32),
                pltpu.VMEM((32, ROWS, half), BF16),
                pltpu.VMEM((32, ROWS, half), BF16),
                pltpu.VMEM((3, rows + 16, width), F32),
                pltpu.VMEM((8, width), F32),
                pltpu.VMEM((8, width), F32),
                pltpu.VMEM((5, 16, width), BF16),
                pltpu.SemaphoreType.REGULAR,
                pltpu.SemaphoreType.DMA((7,)),
                pltpu.SemaphoreType.DMA((4,)),
                pltpu.SemaphoreType.DMA((4,)),
                pltpu.SemaphoreType.DMA,
                pltpu.SemaphoreType.DMA,
                pltpu.SemaphoreType.DMA,
                pltpu.SemaphoreType.DMA,
                pltpu.SemaphoreType.DMA,
                pltpu.SemaphoreType.DMA,
            ],
            compiler_params=pltpu.CompilerParams(
                collective_id=0, has_side_effects=True, vmem_limit_bytes=40 * 1024 * 1024
            ),
        )(*(pltpu.with_memory_space_constraint(x, pltpu.HBM) for x in args))
        out = pl.pallas_call(
            hand_over,
            out_shape=[pltpu.HBM(x.shape, x.dtype) for x in made],
            in_specs=[vmem] * 5,
            out_specs=[pl.BlockSpec(memory_space=pltpu.HBM)] * 5,
            scratch_shapes=[pltpu.SemaphoreType.DMA((7,))],
        )(*(pltpu.with_memory_space_constraint(x, pltpu.VMEM) for x in out))
        return out[0], out[1], out[2].T, out[3].T, out[4].reshape(width)

    return jax.shard_map(
        body,
        mesh=mesh,
        in_specs=(
            P(None, "ctx", "ch"),
            P("ctx", "ch"),
            P("ctx", "ch"),
            P(None, None, "ch"),
            P("ch", None),
            P("ch", None),
            P("ch"),
        ),
        out_specs=(
            P(None, "ctx", "ch"),
            P(None, None, "ch"),
            P("ch", None),
            P("ch", None),
            P("ch"),
        ),
        check_vma=False,
    )
```
